32 devices in a mesh: ctx: 8 (over y, x, core), fsdp: 4 (over z).
Axes of the slice: x: 2, y: 2, z: 4, core: 2. Of those that a mesh axis runs over, the one named last changes fastest.
Arguments:
- tokens: bfloat16 [16384, 1024], P(('fsdp', 'ctx')), may hold values from -6 to 6
- encoder_out: bfloat16 [8192, 1024], P(('fsdp', 'ctx')), may hold values from -6 to 6
- prompt_offsets: int32 [4, 1], P('fsdp'), may hold values from 512 to 2048, as said below
- gains: bfloat16 [3, 1024], P(None, 'fsdp'), may hold values from 0.5 to 1.5
- shifts: bfloat16 [9, 1024], P(None, 'fsdp'), may hold values from -0.59765625 to 0.59765625
- self_in: bfloat16 [1024, 3072], P('fsdp'), may hold values from -0.1875 to 0.1875
- self_out: bfloat16 [1024, 1024], P('fsdp'), may hold values from -3 to 3
- cross_q: bfloat16 [1024, 1024], P('fsdp'), may hold values from -0.1875 to 0.1875
- cross_kv: bfloat16 [1024, 2048], P('fsdp'), may hold values from -0.1875 to 0.1875
- cross_out: bfloat16 [1024, 1024], P('fsdp'), may hold values from -3 to 3
- ffn_in: bfloat16 [1024, 4096], P('fsdp'), may hold values from -0.1875 to 0.1875
- ffn_bias: bfloat16 [4096], P('fsdp'), may hold values from -0.59765625 to 0.59765625
- ffn_out: bfloat16 [4096, 1024], P('fsdp'), may hold values from -0.09375 to 0.09375
- out_bias: bfloat16 [1024], P('fsdp'), may hold values from -1 to 1
- cotangent: bfloat16 [16384, 1024], P(('fsdp', 'ctx')), may hold values from -6 to 6
Outputs:
- layer_out: bfloat16 [16384, 1024], P(('fsdp', 'ctx'))
- input_grad: float32 [16384, 1024], P(('fsdp', 'ctx'))
- enc_grad: float32 [8192, 1024], P(('fsdp', 'ctx'))
- grad_gains: float32 [3, 1024], P(None, 'fsdp')
- grad_shifts: float32 [9, 1024], P(None, 'fsdp')
- grad_self_in: float32 [1024, 3072], P('fsdp')
- grad_self_out: float32 [1024, 1024], P('fsdp')
- grad_cross_q: float32 [1024, 1024], P('fsdp')
- grad_cross_kv: float32 [1024, 2048], P('fsdp')
- grad_cross_out: float32 [1024, 1024], P('fsdp')
- grad_ffn_in: float32 [1024, 4096], P('fsdp')
- grad_ffn_bias: float32 [4096], P('fsdp')
- grad_ffn_out: float32 [4096, 1024], P('fsdp')
- grad_out_bias: float32 [1024], P('fsdp')
The draws below stay inside these ranges and needn't reach their ends.
Inputs may be any that keep to these rules, and one draw needn't show every extreme that they name: prompt_offsets[g, c] is the number of leading prompt rows that continuation c of group g sees; each row of it has an entry equal to 2048.
All inputs are finite; a program needn't handle non-finite values.
Results may differ from the reference program's by a relative error of at most 0.024.
Values may be sent and summed in bfloat16 or wider, within the bound.
A program may use at most 640 MiB of HBM per device.

```python
import math
import jax
import jax.numpy as jnp
from jax import lax

D = 1024
HEADS = 16
FF = 4096
HEAD_DIM = 64
TOK_DEV = 512
CONT = 2048
ENC = 2048
GROUPS = 4
PROMPT = 2048
NCONT = 1
TOKENS = 16384
ENC_ALL = 8192
N_CTX = 8


def draw_prompt_offsets(key, part):
    draw_key = jax.random.fold_in(key, 11)
    pick_key = jax.random.fold_in(key, 23)
    values = jax.random.randint(draw_key, (GROUPS, NCONT), PROMPT // 4, PROMPT + 1, dtype=jnp.int32)
    chosen = jax.random.randint(pick_key, (GROUPS, 1), 0, NCONT, dtype=jnp.int32)
    columns = jnp.arange(NCONT, dtype=jnp.int32)[None, :]
    return jnp.where(columns == chosen, PROMPT, values).astype(jnp.int32)


def level_of(rng, shape, pieces, least, top_value):
    def one(axis_at, shards_of):
        draws = jax.random.uniform(jax.random.fold_in(jax.random.fold_in(rng, 6), axis_at), (shards_of,), jnp.float32, least / len(pieces), top_value / len(pieces))
        return jnp.repeat(jnp.exp(draws), shape[axis_at] // shards_of).reshape((-1,) + (1,) * (len(shape) - axis_at - 1))

    level = one(*pieces[0])
    for cut in pieces[1:]:
        level = level * one(*cut)
    return level


def normal_values(stream_key, shape, deviation, most, pieces=(), held_as=jnp.bfloat16):
    values = deviation * jax.random.normal(stream_key, shape, jnp.float32)
    if pieces:
        values = values * level_of(stream_key, shape, pieces, -0.22, 0.18)
    return jnp.clip(values, -most, most).astype(held_as)


def setup_inputs(seed: int = 0) -> dict:
    key_list = jax.random.split(jax.random.key(seed), 16)
    return {
        "tokens": normal_values(key_list[0], (TOKENS, D), 1.0, 6.0, ((0, 32),)),
        "encoder_out": normal_values(key_list[1], (ENC_ALL, D), 1.0, 6.0, ((0, 32),)),
        "prompt_offsets": draw_prompt_offsets(jax.random.fold_in(key_list[15], 71), 0),
        "gains": jnp.clip(1.0 + 0.1 * jax.random.normal(key_list[3], (3, D), jnp.float32), 0.5, 1.5).astype(jnp.bfloat16),
        "shifts": normal_values(key_list[4], (9, D), 0.1, 0.59765625, ((1, 4),)),
        "self_in": normal_values(key_list[5], (D, 3 * D), D ** -0.5, 0.1875, ((0, 4),)),
        "self_out": normal_values(key_list[6], (D, D), 4 ** -0.5, 3.0, ((0, 4),)),
        "cross_q": normal_values(key_list[7], (D, D), D ** -0.5, 0.1875, ((0, 4),)),
        "cross_kv": normal_values(key_list[8], (D, 2 * D), D ** -0.5, 0.1875, ((0, 4),)),
        "cross_out": normal_values(key_list[9], (D, D), 4 ** -0.5, 3.0, ((0, 4),)),
        "ffn_in": normal_values(key_list[10], (D, FF), D ** -0.5, 0.1875, ((0, 4),)),
        "ffn_bias": normal_values(key_list[11], (FF,), 0.1, 0.59765625, ((0, 4),)),
        "ffn_out": normal_values(key_list[12], (FF, D), FF ** -0.5, 0.09375, ((0, 4),)),
        "out_bias": normal_values(key_list[13], (D,), 0.2, 1.0, ((0, 4),)),
        "cotangent": normal_values(key_list[14], (TOKENS, D), 1.0, 6.0, ((0, 32),)),
    }


epsilon = 1e-05
negative = -1e+30
precise = lax.Precision.HIGHEST

@jax.custom_vjp
def low(v):
    return lax.optimization_barrier(v.astype(jnp.bfloat16)).astype(jnp.float32)

@jax.custom_vjp
def low_back(v):
    return v

def low_keep(v):
    return (low(v), None)

def low_pass(kept, grad):
    return (grad,)

def back_keep(v):
    return (v, None)

def back_low(kept, grad):
    return (low(grad),)
low.defvjp(low_keep, low_pass)
low_back.defvjp(back_keep, back_low)

def layer_norm(values, gain, shift):
    center = values - lax.optimization_barrier(jnp.mean(values, axis=-1, keepdims=True))
    spread = lax.optimization_barrier(jnp.mean(center * center, axis=-1, keepdims=True))
    return center * lax.rsqrt(spread + epsilon) * gain + shift

def matmul(left, right):
    return jnp.dot(left, right, precision=precise)

def softmax(scores):
    peaks = lax.optimization_barrier(jnp.max(scores, axis=-1, keepdims=True))
    raised = jnp.exp(scores - peaks)
    return raised / lax.optimization_barrier(jnp.sum(raised, axis=-1, keepdims=True))

def allowed_mask(query_pos, key_pos, offsets):
    cont_index = jnp.maximum(query_pos - PROMPT, 0) // CONT
    cont_table = jnp.arange(NCONT, dtype=jnp.int32)
    prompt_limit = lax.optimization_barrier(jnp.sum(jnp.where(cont_index[..., None] == cont_table, offsets, 0), axis=-1))
    own_start = PROMPT + cont_index * CONT
    return (key_pos <= query_pos) & ((query_pos < PROMPT) | (key_pos >= own_start) | (key_pos < prompt_limit))

def self_attention(queries, keys, values, offsets):
    total_rows = queries.shape[0]
    block_rows = math.gcd(512, total_rows)
    key_heads = keys.reshape(total_rows, HEADS, HEAD_DIM)
    value_heads = values.reshape(total_rows, HEADS, HEAD_DIM)
    query_blocks = queries.reshape(total_rows // block_rows, block_rows, HEADS, HEAD_DIM)
    block_starts = jnp.arange(total_rows // block_rows, dtype=jnp.int32) * block_rows
    key_pos = jnp.arange(total_rows, dtype=jnp.int32)[None, :]

    def one_block(inputs):
        query_block, block_start = inputs
        query_pos = block_start + jnp.arange(block_rows, dtype=jnp.int32)[:, None]
        permitted = allowed_mask(query_pos, key_pos, offsets)
        scores = low_back(jnp.einsum('qhd,khd->hqk', query_block, key_heads, precision=precise))
        scores = jnp.where(permitted[None], scores, negative)
        weights = low(softmax(scores))
        return jnp.einsum('hqk,khd->qhd', weights, value_heads, precision=precise)
    result = lax.map(jax.checkpoint(one_block), (query_blocks, block_starts))
    return result.reshape(total_rows, D)

def cross_attention(queries, enc_keys, enc_values):
    total_rows = queries.shape[0]
    block_rows = math.gcd(512, total_rows)
    key_heads = enc_keys.reshape(ENC, HEADS, HEAD_DIM)
    value_heads = enc_values.reshape(ENC, HEADS, HEAD_DIM)
    query_blocks = queries.reshape(total_rows // block_rows, block_rows, HEADS, HEAD_DIM)

    def one_block(query_block):
        scores = low_back(jnp.einsum('qhd,khd->hqk', query_block, key_heads, precision=precise))
        weights = low(softmax(scores))
        return jnp.einsum('hqk,khd->qhd', weights, value_heads, precision=precise)
    result = lax.map(jax.checkpoint(one_block), query_blocks)
    return result.reshape(total_rows, D)

def layer_forward(params, token_values, encoder_values, offsets):
    gains, shifts, self_in, self_out, cross_q, cross_kv, cross_out, ffn_in, ffn_bias, ffn_out, out_bias = params
    scale = 1.0 / math.sqrt(HEAD_DIM)
    normed_one = low(layer_norm(token_values, gains[0], shifts[0]))
    projected = matmul(normed_one, self_in)
    queries = low(low_back(scale * (projected[:, :D] + shifts[3])))
    keys = low(low_back(projected[:, D:2 * D]))
    values = low(low_back(projected[:, 2 * D:] + shifts[4]))
    mixed = low(low_back(self_attention(queries, keys, values, offsets)))
    first_sum = token_values + low_back(matmul(mixed, self_out) + shifts[5])
    normed_two = low(layer_norm(first_sum, gains[1], shifts[1]))
    cross_queries = low(low_back(scale * (matmul(normed_two, cross_q) + shifts[6])))
    enc_projected = matmul(encoder_values, cross_kv)
    enc_keys = low(low_back(enc_projected[:, :D]))
    enc_values = low(low_back(enc_projected[:, D:] + shifts[7]))
    cross_mixed = low(low_back(cross_attention(cross_queries, enc_keys, enc_values)))
    second_sum = first_sum + low_back(matmul(cross_mixed, cross_out) + shifts[8])
    normed_three = low(layer_norm(second_sum, gains[2], shifts[2]))
    hidden = low(jax.nn.gelu(low_back(matmul(normed_three, ffn_in) + ffn_bias), approximate=False))
    return second_sum + matmul(hidden, ffn_out) + out_bias

def reference(tokens, encoder_out, prompt_offsets, gains, shifts, self_in, self_out, cross_q, cross_kv, cross_out, ffn_in, ffn_bias, ffn_out, out_bias, cotangent):
    weights = tuple((array.astype(jnp.float32) for array in (gains, shifts, self_in, self_out, cross_q, cross_kv, cross_out, ffn_in, ffn_bias, ffn_out, out_bias)))
    group_rows = TOK_DEV * N_CTX
    outputs = []
    input_grads = []
    encoder_grads = []
    weight_grads = tuple((jnp.zeros_like(array) for array in weights))
    for group in range(GROUPS):
        token_part = tokens[group * group_rows:(group + 1) * group_rows].astype(jnp.float32)
        encoder_part = encoder_out[group * ENC:(group + 1) * ENC].astype(jnp.float32)
        offsets = prompt_offsets[group]

        def forward(token_values, encoder_values, *params):
            return layer_forward(params, token_values, encoder_values, offsets)
        result, backward = jax.vjp(forward, token_part, encoder_part, *weights)
        grads = backward(cotangent[group * group_rows:(group + 1) * group_rows].astype(jnp.float32))
        outputs.append(result.astype(jnp.bfloat16))
        input_grads.append(grads[0])
        encoder_grads.append(grads[1])
        weight_grads = tuple((total + piece for total, piece in zip(weight_grads, grads[2:])))
    return (jnp.concatenate(outputs, axis=0), jnp.concatenate(input_grads, axis=0), jnp.concatenate(encoder_grads, axis=0), weight_grads[0], weight_grads[1], weight_grads[2], weight_grads[3], weight_grads[4], weight_grads[5], weight_grads[6], weight_grads[7], weight_grads[8], weight_grads[9], weight_grads[10])
```

```python
import functools
import math

import jax
import jax.numpy as jnp
from jax import lax
from jax.experimental import pallas as pl
from jax.experimental.pallas import tpu as pltpu
from jax.sharding import PartitionSpec as P

HEADS = 16
CONT = 2048
EPS = 1e-05
NEG = -1e30
TILE = 512
BF = jnp.bfloat16
F32 = jnp.float32
VMEM_BYTES = 56 * 2**20


def nn(left, right):
    return lax.dot_general(left, right, (((1,), (0,)), ((), ())), preferred_element_type=F32)


def nt(left, right):
    return lax.dot_general(left, right, (((1,), (1,)), ((), ())), preferred_element_type=F32)


def tn(left, right):
    return lax.dot_general(left, right, (((0,), (0,)), ((), ())), preferred_element_type=F32)


def normalize(values):
    center = values - jnp.mean(values, axis=-1, keepdims=True)
    scale = lax.rsqrt(jnp.mean(center * center, axis=-1, keepdims=True) + EPS)
    return center * scale, scale


def normalize_back(unit, scale, gain, grad):
    q = gain * grad
    back = scale * (
        q - jnp.mean(q, axis=-1, keepdims=True) - unit * jnp.mean(q * unit, axis=-1, keepdims=True)
    )
    return back, jnp.sum(grad * unit, axis=0), jnp.sum(grad, axis=0)


def head_lanes(head, array):
    lane = lax.broadcasted_iota(jnp.int32, array.shape, 1)
    keep = (lane < 64) if head == 0 else (lane >= 64)
    return jnp.where(keep, array, jnp.zeros_like(array))


def transposed(array):
    return array.astype(F32).T.astype(BF)


def visible(key_start, query_start, key_count, query_count, own_start, limit):
    key = key_start + lax.broadcasted_iota(jnp.int32, (key_count, query_count), 0)
    query = query_start + lax.broadcasted_iota(jnp.int32, (key_count, query_count), 1)
    shown = key <= query
    if limit is not None:
        shown = shown & ((key >= own_start) | (key < limit))
    return shown


def soften(scores, total, peak, value_t):
    old = peak[:1]
    new = jnp.maximum(old, jnp.max(scores, axis=0, keepdims=True))
    raised = jnp.exp(scores - new).astype(BF)
    total[...] = total[...] * jnp.exp(old - new) + nn(value_t, raised)
    peak[...] = jnp.broadcast_to(new, peak.shape)


def set_value_rows(value_t, head, columns, value):
    value_t[head, :64, columns] = value[64 * head : 64 * head + 64]
    value_t[head, 64:, columns] = jnp.ones((16, value.shape[1]), BF)


def tile_rows(tile):
    return pl.ds(pl.multiple_of(tile * TILE, TILE), TILE)


def flipped_bits(index, mask):
    out, bit = index, 1
    while bit <= mask:
        if mask & bit:
            out = out + bit - 2 * bit * ((index // bit) % 2)
        bit *= 2
    return out


def greet(peers):
    barrier = pltpu.get_barrier_semaphore()
    for peer in peers:
        pl.semaphore_signal(
            barrier, inc=1, device_id=peer, device_id_type=pl.DeviceIdType.MESH
        )
    pl.semaphore_wait(barrier, len(peers))


def others(axis):
    me, count = lax.axis_index(axis), lax.axis_size(axis)
    return [{axis: (me + step) % count} for step in range(1, count)]


def remote(source, target, send_sem, recv_sem, device):
    return pltpu.make_async_remote_copy(
        source, target, send_sem, recv_sem, device_id=device,
        device_id_type=pl.DeviceIdType.MESH,
    )


def exchange(source, target, send_sems, recv_sems, own_sem):
    me, count = lax.axis_index("ctx"), lax.axis_size("ctx")

    def copy(there, slot):
        return remote(
            source.at[there], target.at[slot], send_sems.at[there], recv_sems.at[slot],
            {"ctx": there},
        )

    def send(there):
        @pl.when(there != me)
        def _():
            copy(there, me).start()

        @pl.when(there == me)
        def _():
            pltpu.make_async_copy(source.at[me], target.at[me], own_sem).start()

    def arrived(there):
        @pl.when(there != me)
        def _():
            copy(there, there).wait_recv()

        @pl.when(there == me)
        def _():
            pltpu.make_async_copy(source.at[me], target.at[me], own_sem).wait()

    def sent():
        for step in range(1, count):
            copy((me + step) % count, me).wait_send()

    return send, arrived, sent


def attend_forward_kernel(cross, heads, conts, offs_ref, q_ref, k_ref, v_ref, *refs):
    if cross:
        mixed_ref, att_ref, lse_ref, q_out, *refs = refs
    else:
        mixed_ref, att_ref, lse_ref, *refs = refs
    total, peak, value_t, score_a, score_b, stage, send_sem, recv_sem, own_sem, *refs = refs
    me, count = lax.axis_index("ctx"), lax.axis_size("ctx")
    rows = att_ref.shape[1]
    tiles = rows // TILE
    key_tiles = k_ref.shape[0] // TILE
    prompt = rows - conts * CONT
    prompt_tiles = prompt // TILE
    greet(others("ctx"))
    send, arrived, sent = exchange(stage, mixed_ref, send_sem, recv_sem, own_sem)
    if cross:
        q_all, q_send, q_recv, q_own = refs
        put, got, put_done = exchange(q_ref, q_all, q_send, q_recv, q_own)
        for step in range(count):
            put((me + step) % count)

    for tile in range(key_tiles):
        at = pl.ds(tile * TILE, TILE)
        turned = transposed(v_ref[at, :])
        for head in range(heads):
            set_value_rows(value_t, head, at, turned)

    def query_tile(step, carry):
        if cross:
            i = (me + step) % count
            got(i)
            q = q_all[i]
            q_out[i] = q
        else:
            i = step
            q = q_ref[tile_rows(i), :]
        masked = [head_lanes(head, q) for head in range(heads)]
        total[...] = jnp.zeros_like(total)
        peak[...] = jnp.full_like(peak, NEG)

        def score(j, target):
            k = k_ref[tile_rows(j), :]
            for head in range(heads):
                target[head] = nt(k, masked[head])

        def soft(j, source, shown=None):
            for head in range(heads):
                scores = source[head]
                if shown is not None:
                    scores = jnp.where(shown, scores, NEG)
                soften(
                    scores, total.at[head], peak.at[head], value_t[head, :, tile_rows(j)]
                )

        if cross:
            both = (score_a, score_b)
            score(0, score_a)
            for j in range(key_tiles):
                if j + 1 < key_tiles:
                    score(j + 1, both[(j + 1) % 2])
                soft(j, both[j % 2])
        elif conts == 1:
            score(i, score_a)
            diagonal = visible(0, 0, TILE, TILE, 0, None)

            @pl.when(i > 0)
            def _():
                score(i - 1, score_b)
                soft(i, score_a, diagonal)

            @pl.when(i == 0)
            def _():
                soft(i, score_a, diagonal)

            def two(t, carry):
                j = i - 1 - 2 * t
                score(jnp.maximum(j - 1, 0), score_a)
                soft(j, score_b)
                score(jnp.maximum(j - 2, 0), score_b)
                soft(j - 1, score_a)
                return carry

            lax.fori_loop(0, i // 2, two, 0)

            @pl.when(i % 2 == 1)
            def _():
                soft(0, score_b)
        else:
            cont = jnp.maximum(i * TILE - prompt, 0) // CONT
            inside = i * TILE < prompt
            own = jnp.where(inside, 0, prompt + cont * CONT)
            limit = offs_ref[0, cont]

            def one(j, carry):
                score(j, score_a)
                soft(j, score_a, visible(j * TILE, i * TILE, TILE, TILE, own, limit))
                return carry

            lax.fori_loop(jnp.where(inside, 0, own // TILE), i + 1, one, 0)
            lax.fori_loop(0, jnp.where(inside, 0, prompt_tiles), one, 0)

        for head in range(heads):
            part = total[head]
            att_ref[64 * head : 64 * head + 64, tile_rows(i)] = part[:64] / part[64:65]
            lse_ref[head : head + 1, tile_rows(i)] = peak[head][:1] + jnp.log(part[64:65])
        stage[i] = att_ref[:, tile_rows(i)].T.astype(BF)
        send(i)
        return carry

    if heads < 2:
        att_ref[...] = jnp.zeros_like(att_ref)
    lax.fori_loop(0, tiles, query_tile, 0)
    for step in range(count):
        arrived((me + step) % count)
    sent()
    if cross:
        put_done()


def attend_forward(cross, heads, offsets, q, k, v):
    count = lax.axis_size("ctx")
    rows = count * TILE
    vmem = pl.BlockSpec(memory_space=pltpu.VMEM)
    hbm = pl.BlockSpec(memory_space=pl.ANY)
    dma = pltpu.SemaphoreType.DMA
    tiles = jax.ShapeDtypeStruct((count, TILE, 128), BF)
    outs = [
        tiles,
        jax.ShapeDtypeStruct((128, rows), F32),
        jax.ShapeDtypeStruct((8, rows), F32),
    ]
    scratch = [
        pltpu.VMEM((heads, 80, TILE), F32),
        pltpu.VMEM((heads, 8, TILE), F32),
        pltpu.VMEM((heads, 80, k.shape[0]), BF),
        pltpu.VMEM((heads, TILE, TILE), F32),
        pltpu.VMEM((heads, TILE, TILE), F32),
        pltpu.VMEM((count, TILE, 128), BF),
        dma((count,)), dma((count,)), dma,
    ]
    if cross:
        outs.append(tiles)
        scratch += [pltpu.VMEM((count, TILE, 128), BF), dma((count,)), dma((count,)), dma]
    return pl.pallas_call(
        functools.partial(attend_forward_kernel, cross, heads, offsets.shape[1]),
        out_shape=outs,
        in_specs=[pl.BlockSpec(memory_space=pltpu.SMEM), vmem, vmem, vmem],
        out_specs=[hbm] + [vmem] * (len(outs) - 1),
        scratch_shapes=scratch,
        compiler_params=pltpu.CompilerParams(
            vmem_limit_bytes=VMEM_BYTES, collective_id=2 if cross else 1,
            has_side_effects=True,
        ),
        cost_estimate=pl.CostEstimate(
            flops=40 * 10**9, bytes_accessed=2**23, transcendentals=2**24
        ),
    )(offsets, q, k, v)


def rest_copies(sources, targets, send_sem, recv_sem):
    me = lax.axis_index("ctx")
    half = lax.axis_size("ctx") // 4
    out = []
    for other in range(1, half):
        for part in range(2):
            mine = me // 4 if part == 0 else (me // 2) % half
            sem = len(out)
            out.append(
                remote(
                    sources[part].at[:, :, flipped_bits(mine, other)],
                    targets[part].at[other - 1],
                    send_sem.at[sem], recv_sem.at[sem],
                    {"ctx": flipped_bits(me, (4 if part == 0 else 2) * other)},
                )
            )
    return out


def last_copies(sources, targets, send_sem, recv_sem):
    me, zone = lax.axis_index("ctx"), lax.axis_index("fsdp")
    chips, groups = lax.axis_size("ctx") // 2, lax.axis_size("fsdp")
    out = []
    for other in range(1, chips):
        sem = len(out)
        out.append(
            remote(
                sources[0].at[flipped_bits(me // 2, other)], targets[0].at[other - 1],
                send_sem.at[sem], recv_sem.at[sem], {"ctx": flipped_bits(me, 2 * other)},
            )
        )
    for shift in range(1, groups):
        sem = len(out)
        there = (zone + shift) % groups
        out.append(
            remote(
                sources[1].at[there], targets[1].at[shift - 1],
                send_sem.at[sem], recv_sem.at[sem], {"fsdp": there},
            )
        )
    return out


def attend_backward_kernel(
    cross, heads, conts, scale, carried, offs_ref, q_ref, k_ref, v_ref, do_ref, att_ref,
    lse_ref, *refs,
):
    sources, refs = refs[:2], refs[2:]
    if cross:
        moved_ref, dk_ref, dv_ref, *refs = refs
    else:
        moved_ref, stage, *refs = refs
    targets, refs = refs[:2], refs[2:]
    if cross:
        stage, *refs = refs
    (
        do_all, key_t, delta, dq_sum, dk_sum, dv_sum,
        send_sem, recv_sem, own_sem, do_send, do_recv, do_own, carry_send, carry_recv,
    ) = refs
    me, count = lax.axis_index("ctx"), lax.axis_size("ctx")
    tiles = count
    key_tiles = k_ref.shape[0] // TILE
    prompt = tiles * TILE - conts * CONT
    prompt_tiles = prompt // TILE
    greet(others("ctx") + ([] if cross else others("fsdp")))
    put, got, put_done = exchange(do_ref, do_all, do_send, do_recv, do_own)
    for step in range(count):
        put((me + step) % count)
    carry_copies = carried(sources, targets, carry_send, carry_recv)
    for copy in carry_copies:
        copy.start()
    send, arrived, sent = exchange(stage, moved_ref, send_sem, recv_sem, own_sem)
    dk_sum[...] = jnp.zeros_like(dk_sum)
    dv_sum[...] = jnp.zeros_like(dv_sum)
    for tile in range(key_tiles):
        at = pl.ds(tile * TILE, TILE)
        key_t[:, at] = transposed(k_ref[at, :])

    def query_tile(step, carry):
        i = (me + step) % count if cross else tiles - 1 - step
        q = q_ref[tile_rows(i), :]
        got(i)
        do = do_all[i]
        q_masked = [head_lanes(head, q) for head in range(heads)]
        do_masked = [head_lanes(head, do) for head in range(heads)]
        both = do.astype(F32).T * att_ref[:, tile_rows(i)]
        for head in range(heads):
            delta[head : head + 1, :] = jnp.sum(
                both[64 * head : 64 * head + 64], axis=0, keepdims=True
            )
        dq_sum[...] = jnp.zeros_like(dq_sum)

        def key_step(j, shown):
            at = tile_rows(j)
            k, v = k_ref[at, :], v_ref[at, :]
            for head in range(heads):
                scores = nt(k, q_masked[head])
                weights = jnp.exp(scores - lse_ref[head : head + 1, tile_rows(i)])
                if shown is not None:
                    weights = jnp.where(shown, weights, 0.0)
                weight_grad = nt(v, do_masked[head])
                score_grad = (weights * (weight_grad - delta[head : head + 1, :])).astype(BF)
                dv_sum[at, :] += nn(weights.astype(BF), do_masked[head])
                dk_sum[at, :] += nn(score_grad, q_masked[head])
                own = slice(64 * head, 64 * head + 64)
                dq_sum[own, :] += nn(key_t[own, at], score_grad)

        def plain(j, carry):
            key_step(j, None)
            return carry

        if cross:
            lax.fori_loop(0, key_tiles, plain, 0)
        elif conts == 1:
            key_step(i, visible(0, 0, TILE, TILE, 0, None))
            lax.fori_loop(0, i, plain, 0)
        else:
            cont = jnp.maximum(i * TILE - prompt, 0) // CONT
            inside = i * TILE < prompt
            own = jnp.where(inside, 0, prompt + cont * CONT)
            limit = offs_ref[0, cont]

            def one(j, carry):
                key_step(j, visible(j * TILE, i * TILE, TILE, TILE, own, limit))
                return carry

            lax.fori_loop(jnp.where(inside, 0, own // TILE), i + 1, one, 0)
            lax.fori_loop(0, jnp.where(inside, 0, prompt_tiles), one, 0)

        dq = dq_sum[...].T.astype(BF).astype(F32)
        stage[i, :, :128] = (dq * scale).astype(BF)
        if not cross:
            stage[i, :, 128:256] = dk_sum[tile_rows(i), :].astype(BF)
            stage[i, :, 256:] = dv_sum[tile_rows(i), :].astype(BF)
        send(i)
        return carry

    lax.fori_loop(0, tiles, query_tile, 0)
    if cross:
        dk_ref[...] = dk_sum[...].astype(BF)
        dv_ref[...] = dv_sum[...].astype(BF)
    for step in range(count):
        arrived((me + step) % count)
    sent()
    put_done()
    for copy in carry_copies:
        copy.wait_send()
        copy.wait_recv()


def attend_backward(cross, heads, scale, offsets, q, k, v, do, att, lse, sources, target_shapes):
    count = lax.axis_size("ctx")
    vmem = pl.BlockSpec(memory_space=pltpu.VMEM)
    hbm = pl.BlockSpec(memory_space=pl.ANY)
    dma = pltpu.SemaphoreType.DMA
    keys = k.shape[0]
    wide = 128 if cross else 384
    moved = jax.ShapeDtypeStruct((count, TILE, wide), BF)
    if cross:
        local = [jax.ShapeDtypeStruct((keys, 128), BF)] * 2
        carries = 2 * max(count // 4 - 1, 1)
    else:
        local = [jax.ShapeDtypeStruct((count, TILE, wide), BF)]
        carries = count // 2 - 1 + lax.axis_size("fsdp") - 1
    targets = [jax.ShapeDtypeStruct(shape, BF) for shape in target_shapes]
    return pl.pallas_call(
        functools.partial(
            attend_backward_kernel, cross, heads, offsets.shape[1], scale,
            rest_copies if cross else last_copies,
        ),
        out_shape=[moved] + local + targets,
        in_specs=[pl.BlockSpec(memory_space=pltpu.SMEM)] + [vmem] * 6 + [hbm] * 2,
        out_specs=[hbm] + [vmem] * len(local) + [hbm] * 2,
        scratch_shapes=([pltpu.VMEM((count, TILE, wide), BF)] if cross else [])
        + [
            pltpu.VMEM((count, TILE, 128), BF),
            pltpu.VMEM((128, keys), BF),
            pltpu.VMEM((8, TILE), F32),
            pltpu.VMEM((128, TILE), F32),
            pltpu.VMEM((keys, 128), F32),
            pltpu.VMEM((keys, 128), F32),
            dma((count,)), dma((count,)), dma,
            dma((count,)), dma((count,)), dma,
            dma((carries,)), dma((carries,)),
        ],
        compiler_params=pltpu.CompilerParams(
            vmem_limit_bytes=VMEM_BYTES, collective_id=3 if cross else 4,
            has_side_effects=True,
        ),
        cost_estimate=pl.CostEstimate(
            flops=60 * 10**9, bytes_accessed=2**23, transcendentals=2**24
        ),
    )(offsets, q, k, v, do, att, lse, *sources)


def ffn_kernel(
    steps, groups, n_ref, dy_ref, base_ref, bias_ref, win_ref, wout_ref,
    out_ref, gn_ref, gb_ref, in_ref, sum_ref,
    n_t, own_in, own_out, post_in, post_out, got_in, got_out,
    keep_in, keep_out, flow_in, flow_out, near_in, near_out,
    send_sem, recv_sem, flow_send, flow_recv, save_sem,
):
    f = pl.program_id(0)
    me = lax.axis_index("ctx")
    count = lax.axis_size("ctx")
    chips = count // 2
    core = me % 2
    low_bit = (me // 2) % 2
    high_bit = me // chips
    cols = keep_in.shape[2]
    slot = f % 2
    sibling = {"ctx": flipped_bits(me, 1)}
    low = {"ctx": flipped_bits(me, 2)}
    high = {"ctx": flipped_bits(me, chips)}

    def copies(step, place):
        return (
            remote(post_in.at[place], got_in.at[step], send_sem.at[0, place],
                   recv_sem.at[0, step], sibling),
            remote(post_out.at[place], got_out.at[step], send_sem.at[1, place],
                   recv_sem.at[1, step], sibling),
        )

    def flows(step, place):
        return (
            remote(flow_in.at[place], near_in.at[step], flow_send.at[0, place],
                   flow_recv.at[0, step], low),
            remote(flow_out.at[place], near_out.at[step], flow_send.at[1, place],
                   flow_recv.at[1, step], high),
        )

    @pl.when(f == 0)
    def _():
        greet([sibling, low, high])
        n_t[...] = transposed(n_ref[...])
        gn_ref[...] = jnp.zeros_like(gn_ref)
        out_ref[...] = base_ref[...]

    @pl.when(f < steps)
    def _():
        @pl.when(f >= 2)
        def _():
            for copy in copies(jnp.maximum(f - 2, 0), slot):
                copy.wait_send()

        pre = nn(n_ref[...], win_ref[...]) + bias_ref[0, :1]
        below = 0.5 * (1.0 + lax.erf(pre * (1.0 / math.sqrt(2.0))))
        hidden = (pre * below).astype(BF)
        out_ref[...] += nn(hidden, wout_ref[...])
        slope = below + pre * (jnp.exp(-0.5 * pre * pre) * (1.0 / math.sqrt(2.0 * math.pi)))
        dy = dy_ref[...]
        grad_pre = (nt(dy, wout_ref[...]) * slope).astype(BF)
        gb_ref[0] = jnp.broadcast_to(
            jnp.sum(grad_pre.astype(F32), axis=0, keepdims=True), gb_ref.shape[1:]
        )
        gn_ref[...] += nt(grad_pre, win_ref[...])

        def split(part, keep, post, half):
            left, right = part[:, :half], part[:, half:]
            keep[slot] = jnp.where(core == 0, left, right)
            post[slot] = jnp.where(core == 0, right, left).astype(BF)

        first, second = copies(jnp.minimum(f, steps - 1), slot)
        split(nn(n_t[...], grad_pre), own_in, post_in, cols)
        first.start()
        split(tn(hidden, dy), own_out, post_out, 2 * cols)
        second.start()

    @pl.when(f > 0)
    def _():
        past = jnp.maximum(f - 1, 0)
        place = (f + 1) % 2
        for copy in copies(past, place):
            copy.wait_recv()

        @pl.when(f >= 3)
        def _():
            for copy in flows(jnp.maximum(f - 3, 0), place):
                copy.wait_send()

        unit = keep_in.shape[1] // (groups * (chips // 2))
        for slab in range(groups * (chips // 2)):
            for kept in (True, False):
                take = low_bit if kept else 1 - low_bit
                rows = pl.ds(pl.multiple_of((2 * slab + take) * unit, unit), unit)
                both = own_in[place, rows, :] + got_in[past, rows, :].astype(F32)
                at = slice(unit * slab, unit * slab + unit)
                if kept:
                    keep_in[past, at, :] = both.astype(BF)
                else:
                    flow_in[place, at, :] = both.astype(BF)
        unit = n_t.shape[0] // groups // 2
        for slab in range(own_out.shape[1] // (2 * unit)):
            for kept in (True, False):
                take = high_bit if kept else 1 - high_bit
                rows = pl.ds(pl.multiple_of((2 * slab + take) * unit, unit), unit)
                both = own_out[place, rows, :] + got_out[past, rows, :].astype(F32)
                at = slice(unit * slab, unit * slab + unit)
                for half in range(2):
                    value = both[:, half * cols : half * cols + cols].astype(BF)
                    if kept:
                        keep_out[past, half, at, :] = value
                    else:
                        flow_out[place, half, at, :] = value
        for copy in flows(past, place):
            copy.start()

    @pl.when(f == steps)
    def _():
        for back in (2, 1):
            for copy in copies(steps - back, (steps - back) % 2):
                copy.wait_send()
            for copy in flows(steps - back, (steps - back) % 2):
                copy.wait_send()
        per = steps // sum_ref.shape[0]
        height = keep_out.shape[2]

        def saves(step):
            rows = pl.ds(pl.multiple_of((step % per) * height, height), height)
            return (
                pltpu.make_async_copy(
                    keep_in.at[step], in_ref.at[step], save_sem.at[0, step]
                ),
                pltpu.make_async_copy(
                    keep_out.at[step], sum_ref.at[step // per, :, rows], save_sem.at[1, step]
                ),
            )

        def join(step, carry):
            for copy in flows(step, step % 2):
                copy.wait_recv()
            keep_in[step] = (
                keep_in[step].astype(F32) + near_in[step].astype(F32)
            ).astype(BF)
            keep_out[step] = (
                keep_out[step].astype(F32) + near_out[step].astype(F32)
            ).astype(BF)
            for copy in saves(step):
                copy.start()
            return carry

        def saved(step, carry):
            for copy in saves(step):
                copy.wait()
            return carry

        lax.fori_loop(0, steps, join, 0)
        lax.fori_loop(0, steps, saved, 0)


def ffn(normed, dy, base, bias, weights):
    rows, width = normed.shape
    hidden = weights.shape[1] // 2
    groups = lax.axis_size("fsdp")
    step = 512
    cols = step // 2
    steps = hidden // step
    per = width // step
    last = steps - 1

    def now(f):
        return jnp.minimum(f, last)

    whole = lambda f: (0, 0)
    hbm = pl.BlockSpec(memory_space=pl.ANY)
    dma = pltpu.SemaphoreType.DMA
    once = pl.BlockSpec((rows, width), whole, pipeline_mode=pl.Buffered(1))
    return pl.pallas_call(
        functools.partial(ffn_kernel, steps, groups),
        grid=(steps + 1,),
        out_shape=(
            jax.ShapeDtypeStruct((rows, width), F32),
            jax.ShapeDtypeStruct((rows, width), F32),
            jax.ShapeDtypeStruct((steps, 8, step), F32),
            jax.ShapeDtypeStruct((steps, width // 2, cols), BF),
            jax.ShapeDtypeStruct((hidden // width, 2, width // 2, cols), BF),
        ),
        in_specs=[
            once, once, once,
            pl.BlockSpec((1, 8, step), lambda f: (now(f), 0, 0)),
            pl.BlockSpec((width, step), lambda f: (0, now(f))),
            pl.BlockSpec(
                (step, width), lambda f: (now(f) % per, hidden // width + now(f) // per)
            ),
        ],
        out_specs=(
            pl.BlockSpec((rows, width), whole),
            pl.BlockSpec((rows, width), whole),
            pl.BlockSpec((1, 8, step), lambda f: (now(f), 0, 0)),
            hbm, hbm,
        ),
        scratch_shapes=[
            pltpu.VMEM((width, rows), BF),
            pltpu.VMEM((2, width, cols), F32),
            pltpu.VMEM((2, step, 2 * cols), F32),
            pltpu.VMEM((2, width, cols), BF),
            pltpu.VMEM((2, step, 2 * cols), BF),
            pltpu.VMEM((steps, width, cols), BF),
            pltpu.VMEM((steps, step, 2 * cols), BF),
            pltpu.VMEM((steps, width // 2, cols), BF),
            pltpu.VMEM((steps, 2, step // 2, cols), BF),
            pltpu.VMEM((2, width // 2, cols), BF),
            pltpu.VMEM((2, 2, step // 2, cols), BF),
            pltpu.VMEM((steps, width // 2, cols), BF),
            pltpu.VMEM((steps, 2, step // 2, cols), BF),
            dma((2, 2)), dma((2, steps)), dma((2, 2)), dma((2, steps)), dma((2, steps)),
        ],
        compiler_params=pltpu.CompilerParams(
            vmem_limit_bytes=60 * 2**20, collective_id=0, has_side_effects=True
        ),
        cost_estimate=pl.CostEstimate(
            flops=30 * 10**9, bytes_accessed=2**26, transcendentals=2**22
        ),
    )(normed, dy, base, bias, weights, weights)


def token_grad_kernel(
    own, moved_ref, wq_ref, wk_ref, wv_ref, tokens_ref, gain_ref, first_ref, out_ref
):
    step = pl.program_id(0)

    @pl.when(step == 0)
    def _():
        out_ref[...] = jnp.zeros_like(out_ref)

    grads = moved_ref[0]
    total = out_ref[...]
    for part, weight in enumerate((wq_ref, wk_ref, wv_ref)):
        total = total + nt(grads[:, part * 128 : part * 128 + own], weight[...])
    out_ref[...] = total

    @pl.when(step == pl.num_programs(0) - 1)
    def _():
        unit, scale = normalize(tokens_ref[...].astype(F32))
        q = gain_ref[...] * out_ref[...]
        mean = jnp.mean(q, axis=-1, keepdims=True)
        slant = jnp.mean(q * unit, axis=-1, keepdims=True)
        out_ref[...] = first_ref[...] + scale * (q - mean - unit * slant)


def token_grad(moved, weights, tokens, gain, first):
    ctx, rows, wide = moved.shape
    width = tokens.shape[1]
    own = width // ctx
    if own < 128:
        cut = moved.reshape(ctx, rows, 3, 128)[:, :, :, :own]
        grads = jnp.transpose(cut, (1, 2, 0, 3)).reshape(rows, 3 * width)
        unit, scale = normalize(tokens.astype(F32))
        return first + normalize_back(unit, scale, gain, nt(grads, weights))[0]
    whole = pl.BlockSpec((rows, width), lambda s: (0, 0))
    return pl.pallas_call(
        functools.partial(token_grad_kernel, own),
        grid=(ctx,),
        out_shape=jax.ShapeDtypeStruct((rows, width), F32),
        in_specs=[
            pl.BlockSpec((1, rows, wide), lambda s: (s, 0, 0)),
            pl.BlockSpec((width, own), lambda s: (0, s)),
            pl.BlockSpec((width, own), lambda s: (0, ctx + s)),
            pl.BlockSpec((width, own), lambda s: (0, 2 * ctx + s)),
            whole,
            pl.BlockSpec((1, width), lambda s: (0, 0)),
            whole,
        ],
        out_specs=whole,
        compiler_params=pltpu.CompilerParams(vmem_limit_bytes=VMEM_BYTES),
        cost_estimate=pl.CostEstimate(flops=10**10, bytes_accessed=2**24, transcendentals=0),
    )(moved, weights, weights, weights, tokens, gain, first)


def swap(value, bit):
    count = lax.axis_size("ctx")
    return lax.ppermute(value, "ctx", [(i, i ^ bit) for i in range(count)])


def across_groups(value):
    count = lax.axis_size("fsdp")
    me = lax.axis_index("fsdp")
    total = lax.dynamic_index_in_dim(value, me, 0, keepdims=False).astype(F32)
    for shift in range(1, count):
        send = lax.dynamic_index_in_dim(value, (me + shift) % count, 0, keepdims=False)
        got = lax.ppermute(send, "fsdp", [(i, (i + shift) % count) for i in range(count)])
        total = total + got.astype(F32)
    return total


def pair_product(left, right):
    core = lax.axis_index("ctx") % 2
    half = right.shape[1] // 2
    send = tn(left, lax.dynamic_slice_in_dim(right, (1 - core) * half, half, 1)).astype(BF)
    got = swap(send, 1).astype(F32)
    kept = tn(left, lax.dynamic_slice_in_dim(right, core * half, half, 1))
    return (kept + got).astype(BF)


def ctx_gather(value):
    count = lax.axis_size("ctx")
    full = lax.all_gather(value, "ctx", axis=0)
    return full.reshape((count // 2, 2) + value.shape)


def gather_all(pieces):
    count = lax.axis_size("ctx")
    me = lax.axis_index("ctx")
    rows = pieces[0].shape[0] // count
    cut = [lax.dynamic_slice_in_dim(p, me * rows, rows, 0) for p in pieces]
    joined = jnp.concatenate(cut, axis=1)
    full = lax.all_gather(joined, ("fsdp", "ctx"), axis=0, tiled=True)
    out, at = [], 0
    for p in pieces:
        out.append(full[:, at : at + p.shape[1]])
        at += p.shape[1]
    return out


def gather_ffn(ffn_in, ffn_out):
    count = lax.axis_size("ctx")
    groups = lax.axis_size("fsdp")
    me = lax.axis_index("ctx")
    depth, hidden = ffn_in.shape
    width = ffn_out.shape[1]
    blocks = hidden // width
    rows = depth // count
    left = lax.dynamic_slice_in_dim(ffn_in, me * rows, rows, 0)
    left = left.reshape(rows, groups, blocks, depth)
    left = jnp.transpose(left, (0, 2, 1, 3)).reshape(rows, hidden)
    right = lax.dynamic_index_in_dim(
        ffn_out.reshape(blocks, count, rows, width), me, 1, keepdims=False
    )
    right = jnp.moveaxis(right, 0, 1).reshape(rows, hidden)
    joined = jnp.concatenate([left, right], axis=1)
    return lax.all_gather(joined, ("fsdp", "ctx"), axis=0, tiled=True)


def body(
    tokens, encoder_out, prompt_offsets, gains, shifts, self_in, self_out, cross_q, cross_kv,
    cross_out, ffn_in, ffn_bias, ffn_out, out_bias, cotangent,
):
    row_count, width = tokens.shape
    head_dim = width // HEADS
    scale = 1.0 / math.sqrt(head_dim)
    ctx = lax.axis_size("ctx")
    groups = lax.axis_size("fsdp")
    me = lax.axis_index("ctx")
    heads = HEADS // ctx
    own = heads * head_dim

    shard = gains.shape[1]
    small = jnp.concatenate(
        [gains, shifts, out_bias[None], ffn_bias.reshape(-1, shard)], axis=0
    )
    small = lax.all_gather(small, "fsdp", axis=0).astype(F32)
    vectors = jnp.moveaxis(small[:, :13], 0, 1).reshape(13, width)
    gain, shift, full_out_bias = vectors[:3], vectors[3:12], vectors[12]
    full_ffn_bias = small[:, 13:].reshape(-1)

    head_in = lax.dynamic_index_in_dim(
        self_in.reshape(self_in.shape[0], 3, ctx, own), me, 2, keepdims=False
    )
    head_in = lax.all_gather(head_in, "fsdp", axis=0, tiled=True)
    my_shift = lax.dynamic_index_in_dim(shift[3:5].reshape(2, ctx, own), me, 1, keepdims=False)
    all_tokens = lax.all_gather(tokens, "ctx", axis=0, tiled=True)
    all_encoder = lax.all_gather(encoder_out, "ctx", axis=0, tiled=True)
    full_self_out, full_cross_q, full_cross_kv, full_cross_out = gather_all(
        [self_out, cross_q, cross_kv, cross_out]
    )
    ffn_weights = gather_ffn(ffn_in, ffn_out)
    (full_self_in,) = gather_all([self_in])

    all_unit, _ = normalize(all_tokens.astype(F32))
    all_normed = (all_unit * gain[0] + shift[0]).astype(BF)
    projected = nn(all_normed, head_in.reshape(width, 3 * own))

    def lanes(value):
        gap = [(0, 0)] * (value.ndim - 1) + [(0, 128 - own)]
        return value if own == 128 else jnp.pad(value, gap)

    queries = lanes((scale * (projected[:, :own] + my_shift[0])).astype(BF))
    keys = lanes(projected[:, own : 2 * own].astype(BF))
    values = lanes((projected[:, 2 * own :] + my_shift[1]).astype(BF))
    mixed_heads, att_self, lse_self = attend_forward(
        False, heads, prompt_offsets, queries, keys, values
    )

    def to_rows(value):
        return jnp.moveaxis(value[:, :, :own], 0, 1).reshape(row_count, width)

    def to_heads(value):
        return lanes(jnp.moveaxis(value.reshape(row_count, ctx, own), 1, 0))

    mixed = to_rows(mixed_heads)
    token_values = tokens.astype(F32)
    first = token_values + nn(mixed, full_self_out) + shift[5]
    unit_two, scale_two = normalize(first)
    normed_two = (unit_two * gain[1] + shift[1]).astype(BF)
    cross_queries = (scale * (nn(normed_two, full_cross_q) + shift[6])).astype(BF)
    head_kv = lax.dynamic_index_in_dim(
        full_cross_kv.reshape(width, 2, ctx, own), me, 2, keepdims=False
    ).reshape(width, 2 * own)
    enc_shift = lax.dynamic_slice_in_dim(shift[7], me * own, own, 0)
    enc_projected = nn(all_encoder, head_kv)
    enc_keys = lanes(enc_projected[:, :own].astype(BF))
    enc_values = lanes((enc_projected[:, own:] + enc_shift).astype(BF))
    cross_heads, att_cross, lse_cross, all_cross_q = attend_forward(
        True, heads, prompt_offsets, to_heads(cross_queries), enc_keys, enc_values
    )
    cross_mixed = to_rows(cross_heads)
    second = first + nn(cross_mixed, full_cross_out) + shift[8]
    unit_three, scale_three = normalize(second)
    normed_three = (unit_three * gain[2] + shift[2]).astype(BF)
    depth = ffn_in.shape[0]
    blocks = ffn_in.shape[1] // width
    order = full_ffn_bias.reshape(groups, blocks, depth)
    order = jnp.moveaxis(order, 0, 1).reshape(-1, 1, 512)
    layer_sum, grad_three, bias_parts, in_sum, out_sum = ffn(
        normed_three, cotangent, second + full_out_bias,
        jnp.broadcast_to(order, (order.shape[0], 8, 512)), ffn_weights,
    )
    layer_out = layer_sum.astype(BF)
    chips = ctx // 2
    part = depth // chips
    in_sum = in_sum.reshape(-1, groups, chips // 2, part, 256)
    out_sum = out_sum.reshape(-1, groups, chips // 2, part, 256)

    dy = cotangent.astype(F32)
    back_three = normalize_back(unit_three, scale_three, gain[2], grad_three)
    grad_second = dy + back_three[0]
    branch_two = grad_second.astype(BF)
    middle = [pair_product(cross_mixed, branch_two)]
    grad_cross_mixed = nt(branch_two, full_cross_out).astype(BF)
    got_shape = (max(chips // 2 - 1, 1),) + in_sum.shape[:2] + in_sum.shape[3:]
    cross_moved, cross_dk, cross_dv, in_got, out_got = attend_backward(
        True, heads, scale, prompt_offsets, all_cross_q.reshape(-1, 128), enc_keys, enc_values,
        to_heads(grad_cross_mixed), att_cross, lse_cross, (in_sum, out_sum),
        (got_shape, got_shape),
    )

    def joined(value, mine, dim, got):
        kept = lax.dynamic_index_in_dim(value, mine, dim, keepdims=False).astype(F32)
        return kept + jnp.sum(got.astype(F32), axis=0)

    cross_dq = to_rows(cross_moved)
    back_two = normalize_back(unit_two, scale_two, gain[1], nt(cross_dq, full_cross_q))
    grad_first = grad_second + back_two[0]
    branch_one = grad_first.astype(BF)
    grad_mixed = nt(branch_one, full_self_out).astype(BF)
    middle.append(pair_product(normed_two, cross_dq))
    middle.append(pair_product(mixed, branch_one))
    middle = jnp.stack([m.reshape(groups, chips, part, -1) for m in middle])
    middle = jnp.moveaxis(middle, 2, 0)
    ffn_sums = jnp.concatenate(
        [
            joined(in_sum, me // 4, 2, in_got),
            joined(out_sum, (me // 2) % (chips // 2), 2, out_got),
        ],
        axis=0,
    )
    ffn_sums = jnp.moveaxis(ffn_sums.astype(BF), 1, 0)
    moved, grad_heads, middle_got, ffn_got = attend_backward(
        False, heads, scale, prompt_offsets, queries, keys, values, to_heads(grad_mixed),
        att_self, lse_self, (middle, ffn_sums),
        ((chips - 1,) + middle.shape[1:], (groups - 1,) + ffn_sums.shape[1:]),
    )
    zone = lax.axis_index("fsdp")
    ffn_sums = joined(ffn_sums, zone, 0, ffn_got).astype(BF)
    middle = joined(middle, me // 2, 0, middle_got).astype(BF)
    input_grad = token_grad(moved, full_self_in, tokens, gain[:1], grad_first)
    grad_heads = grad_heads.reshape(-1, 3, 128)[:, :, :own].reshape(-1, 3 * own)

    in_sum, out_sum = jnp.split(ctx_gather(ffn_sums), 2, axis=2)
    grad_ffn_in = jnp.transpose(in_sum, (0, 3, 2, 1, 4)).reshape(depth, blocks, groups, depth)
    grad_ffn_in = jnp.swapaxes(grad_ffn_in, 1, 2).reshape(depth, -1).astype(F32)
    out_sum = out_sum.reshape(chips, 2, blocks, 2, part, -1)
    grad_ffn_out = jnp.transpose(out_sum, (2, 0, 4, 1, 3, 5)).reshape(-1, width).astype(F32)

    grad_head_in = tn(all_normed, grad_heads)
    enc_heads = jnp.concatenate([cross_dk[:, :own], cross_dv[:, :own]], axis=1)
    grad_head_kv = tn(all_encoder, enc_heads)
    column = jnp.sum(grad_heads.astype(F32), axis=0)
    weight = head_in.reshape(width, 3 * own).astype(F32)
    grad_shift_one = jnp.sum(weight * column, axis=1)
    grad_gain_one = jnp.sum(weight * (grad_head_in - shift[0][:, None] * column), axis=1) / gain[0]

    def spread(value):
        return lax.dynamic_update_slice_in_dim(jnp.zeros((width,), F32), value, me * own, 0)

    totals = jnp.stack(
        [
            grad_gain_one, back_two[1], back_three[1],
            grad_shift_one, back_two[2], back_three[2],
            spread(column[:own]), spread(column[2 * own :]),
            jnp.sum(branch_one.astype(F32), axis=0),
            jnp.sum(cross_dq.astype(F32), axis=0),
            spread(jnp.sum(enc_heads[:, own:].astype(F32), axis=0)),
            jnp.sum(branch_two.astype(F32), axis=0),
            jnp.sum(dy, axis=0),
        ]
    )
    totals = jnp.moveaxis(totals.reshape(13, groups, shard), 1, 0).reshape(groups, -1)
    bias = jnp.moveaxis(bias_parts[:, 0].reshape(blocks, groups, depth), 0, 1)
    totals = jnp.concatenate([totals, bias.reshape(groups, -1)], axis=1)
    count = totals.shape[1]
    totals = jnp.pad(totals, ((0, 0), (0, 80 * own - count))).reshape(groups, 16, 5 * own)
    late = jnp.concatenate([grad_head_in, grad_head_kv], axis=1).reshape(groups, depth, 5 * own)
    late = jnp.concatenate([late, totals], axis=1)
    late = across_groups(late.astype(BF)).astype(BF)
    middle = across_groups(jnp.moveaxis(middle, 1, 0)).astype(BF)
    packed = jnp.concatenate([late.reshape(-1, own), middle.reshape(-1, own)], axis=0)
    packed = ctx_gather(packed)
    rows = 5 * (depth + 16)
    late = packed[:, :, :rows].reshape(ctx, depth + 16, 5, own)
    heads_in = jnp.transpose(late[:, :depth], (1, 2, 0, 3)).reshape(depth, 5 * width)
    heads_in = heads_in.astype(F32)
    grad_self_in, grad_cross_kv = heads_in[:, : 3 * width], heads_in[:, 3 * width :]
    sums = jnp.sum(late[:, depth:].astype(F32), axis=0).reshape(-1)[:count]
    mine, grad_ffn_bias = sums[: 13 * shard].reshape(13, shard), sums[13 * shard :]
    middle = packed[:, :, rows:].reshape(chips, 2, 3, part, width // 2)
    middle = jnp.transpose(middle, (2, 0, 3, 1, 4)).reshape(3, depth, width).astype(F32)

    enc_sum = enc_heads.reshape(ctx, -1, 2 * own)
    enc_sum = lax.all_to_all(enc_sum, "ctx", split_axis=0, concat_axis=0, tiled=True)
    enc_sum = jnp.transpose(enc_sum.reshape(ctx, -1, 2, own), (1, 2, 0, 3))
    grad_encoder = nt(enc_sum.reshape(-1, 2 * width), full_cross_kv)
    return (
        layer_out, input_grad, grad_encoder, mine[:3], mine[3:12], grad_self_in, middle[2],
        middle[1], grad_cross_kv, middle[0], grad_ffn_in, grad_ffn_bias, grad_ffn_out, mine[12],
    )


def solution(mesh):
    rows = P(("fsdp", "ctx"), None)
    shard = P("fsdp", None)
    thin = P(None, "fsdp")
    flat = P("fsdp")
    return jax.shard_map(
        body,
        mesh=mesh,
        in_specs=(
            rows, rows, shard, thin, thin, shard, shard, shard, shard, shard, shard, flat, shard,
            flat, rows,
        ),
        out_specs=(
            rows, rows, rows, thin, thin, shard, shard, shard, shard, shard, shard, flat, shard,
            flat,
        ),
        check_vma=False,
    )
```

```python
import functools
import math

import jax
import jax.numpy as jnp
from jax import lax
from jax.experimental import pallas as pl
from jax.experimental.pallas import tpu as pltpu
from jax.sharding import PartitionSpec as P

HEADS = 16
CONT = 2048
EPS = 1e-05
NEG = -1e30
TILE = 512
BF = jnp.bfloat16
F32 = jnp.float32
VMEM_BYTES = 56 * 2**20


def nn(left, right):
    return lax.dot_general(left, right, (((1,), (0,)), ((), ())), preferred_element_type=F32)


def nt(left, right):
    return lax.dot_general(left, right, (((1,), (1,)), ((), ())), preferred_element_type=F32)


def tn(left, right):
    return lax.dot_general(left, right, (((0,), (0,)), ((), ())), preferred_element_type=F32)


def normalize(values):
    center = values - jnp.mean(values, axis=-1, keepdims=True)
    scale = lax.rsqrt(jnp.mean(center * center, axis=-1, keepdims=True) + EPS)
    return center * scale, scale


def normalize_back(unit, scale, gain, grad):
    q = gain * grad
    back = scale * (
        q - jnp.mean(q, axis=-1, keepdims=True) - unit * jnp.mean(q * unit, axis=-1, keepdims=True)
    )
    return back, jnp.sum(grad * unit, axis=0), jnp.sum(grad, axis=0)


def head_lanes(head, array):
    lane = lax.broadcasted_iota(jnp.int32, array.shape, 1)
    keep = (lane < 64) if head == 0 else (lane >= 64)
    return jnp.where(keep, array, jnp.zeros_like(array))


def transposed(array):
    return array.astype(F32).T.astype(BF)


def visible(key_start, query_start, key_count, query_count, own_start, limit):
    key = key_start + lax.broadcasted_iota(jnp.int32, (key_count, query_count), 0)
    query = query_start + lax.broadcasted_iota(jnp.int32, (key_count, query_count), 1)
    shown = key <= query
    if limit is not None:
        shown = shown & ((key >= own_start) | (key < limit))
    return shown


def soften(scores, total, peak, value_t):
    old = peak[:1]
    new = jnp.maximum(old, jnp.max(scores, axis=0, keepdims=True))
    raised = jnp.exp(scores - new).astype(BF)
    total[...] = total[...] * jnp.exp(old - new) + nn(value_t, raised)
    peak[...] = jnp.broadcast_to(new, peak.shape)


def set_value_rows(value_t, head, columns, value):
    value_t[head, :64, columns] = value[64 * head : 64 * head + 64]
    value_t[head, 64:, columns] = jnp.ones((16, value.shape[1]), BF)


def tile_rows(tile):
    return pl.ds(pl.multiple_of(tile * TILE, TILE), TILE)


def flipped_bits(index, mask):
    out, bit = index, 1
    while bit <= mask:
        if mask & bit:
            out = out + bit - 2 * bit * ((index // bit) % 2)
        bit *= 2
    return out


def greet(peers):
    barrier = pltpu.get_barrier_semaphore()
    for peer in peers:
        pl.semaphore_signal(
            barrier, inc=1, device_id=peer, device_id_type=pl.DeviceIdType.MESH
        )
    pl.semaphore_wait(barrier, len(peers))


def others(axis):
    me, count = lax.axis_index(axis), lax.axis_size(axis)
    return [{axis: (me + step) % count} for step in range(1, count)]


def remote(source, target, send_sem, recv_sem, device):
    return pltpu.make_async_remote_copy(
        source, target, send_sem, recv_sem, device_id=device,
        device_id_type=pl.DeviceIdType.MESH,
    )


def exchange(source, target, send_sems, recv_sems, own_sem):
    me, count = lax.axis_index("ctx"), lax.axis_size("ctx")

    def copy(there, slot):
        return remote(
            source.at[there], target.at[slot], send_sems.at[there], recv_sems.at[slot],
            {"ctx": there},
        )

    def send(there):
        @pl.when(there != me)
        def _():
            copy(there, me).start()

        @pl.when(there == me)
        def _():
            pltpu.make_async_copy(source.at[me], target.at[me], own_sem).start()

    def arrived(there):
        @pl.when(there != me)
        def _():
            copy(there, there).wait_recv()

        @pl.when(there == me)
        def _():
            pltpu.make_async_copy(source.at[me], target.at[me], own_sem).wait()

    def sent():
        for step in range(1, count):
            copy((me + step) % count, me).wait_send()

    return send, arrived, sent


def attend_forward_kernel(cross, heads, conts, offs_ref, q_ref, k_ref, v_ref, *refs):
    if cross:
        mixed_ref, att_ref, lse_ref, q_out, *refs = refs
    else:
        enc_ref, kv_ref, mixed_ref, att_ref, lse_ref, enc_all, kv_all, *refs = refs
    total, peak, value_t, score_a, score_b, stage, send_sem, recv_sem, own_sem, *refs = refs
    me, count = lax.axis_index("ctx"), lax.axis_size("ctx")
    rows = att_ref.shape[1]
    tiles = rows // TILE
    key_tiles = k_ref.shape[0] // TILE
    prompt = rows - conts * CONT
    prompt_tiles = prompt // TILE
    greet(others("ctx") + ([] if cross else others("fsdp")))
    send, arrived, sent = exchange(stage, mixed_ref, send_sem, recv_sem, own_sem)
    if not cross:
        gather_send, gather_recv, gather_own = refs
        first, second, local = gather_copies(
            enc_ref, kv_ref, enc_all, kv_all, gather_send, gather_recv, gather_own
        )
        for copy in first + local:
            copy.start()
    if cross:
        q_all, q_send, q_recv, q_own = refs
        put, got, put_done = exchange(q_ref, q_all, q_send, q_recv, q_own)
        for step in range(count):
            put((me + step) % count)

    for tile in range(key_tiles):
        at = pl.ds(tile * TILE, TILE)
        turned = transposed(v_ref[at, :])
        for head in range(heads):
            set_value_rows(value_t, head, at, turned)

    def query_tile(step, carry):
        if cross:
            i = (me + step) % count
            got(i)
            q = q_all[i]
            q_out[i] = q
        else:
            i = step
            q = q_ref[tile_rows(i), :]
        masked = [head_lanes(head, q) for head in range(heads)]
        total[...] = jnp.zeros_like(total)
        peak[...] = jnp.full_like(peak, NEG)

        def score(j, target):
            k = k_ref[tile_rows(j), :]
            for head in range(heads):
                target[head] = nt(k, masked[head])

        def soft(j, source, shown=None):
            for head in range(heads):
                scores = source[head]
                if shown is not None:
                    scores = jnp.where(shown, scores, NEG)
                soften(
                    scores, total.at[head], peak.at[head], value_t[head, :, tile_rows(j)]
                )

        if cross:
            both = (score_a, score_b)
            score(0, score_a)
            for j in range(key_tiles):
                if j + 1 < key_tiles:
                    score(j + 1, both[(j + 1) % 2])
                soft(j, both[j % 2])
        elif conts == 1:
            score(i, score_a)
            diagonal = visible(0, 0, TILE, TILE, 0, None)

            @pl.when(i > 0)
            def _():
                score(i - 1, score_b)
                soft(i, score_a, diagonal)

            @pl.when(i == 0)
            def _():
                soft(i, score_a, diagonal)

            def two(t, carry):
                j = i - 1 - 2 * t
                score(jnp.maximum(j - 1, 0), score_a)
                soft(j, score_b)
                score(jnp.maximum(j - 2, 0), score_b)
                soft(j - 1, score_a)
                return carry

            lax.fori_loop(0, i // 2, two, 0)

            @pl.when(i % 2 == 1)
            def _():
                soft(0, score_b)
        else:
            cont = jnp.maximum(i * TILE - prompt, 0) // CONT
            inside = i * TILE < prompt
            own = jnp.where(inside, 0, prompt + cont * CONT)
            limit = offs_ref[0, cont]

            def one(j, carry):
                score(j, score_a)
                soft(j, score_a, visible(j * TILE, i * TILE, TILE, TILE, own, limit))
                return carry

            lax.fori_loop(jnp.where(inside, 0, own // TILE), i + 1, one, 0)
            lax.fori_loop(0, jnp.where(inside, 0, prompt_tiles), one, 0)

        for head in range(heads):
            part = total[head]
            att_ref[64 * head : 64 * head + 64, tile_rows(i)] = part[:64] / part[64:65]
            lse_ref[head : head + 1, tile_rows(i)] = peak[head][:1] + jnp.log(part[64:65])
        stage[i] = att_ref[:, tile_rows(i)].T.astype(BF)
        send(i)
        if not cross:

            @pl.when(step == tiles - 2)
            def _():
                for copy in local:
                    copy.wait()
                for copy in first:
                    copy.wait_recv()
                second.start()

        return carry

    if heads < 2:
        att_ref[...] = jnp.zeros_like(att_ref)
    lax.fori_loop(0, tiles, query_tile, 0)
    for step in range(count):
        arrived((me + step) % count)
    sent()
    if cross:
        put_done()
    else:
        for copy in first:
            copy.wait_send()
        second.wait()


def gather_copies(enc_ref, kv_ref, enc_all, kv_all, send_sem, recv_sem, own_sem):
    me, zone = lax.axis_index("ctx"), lax.axis_index("fsdp")
    chip, core = me // 2, me % 2
    chips, groups = lax.axis_size("ctx") // 2, lax.axis_size("fsdp")
    first = []
    for other in range(1, chips):
        sem = len(first)
        first.append(
            remote(enc_ref, enc_all.at[chip, core], send_sem.at[sem], recv_sem.at[sem],
                   {"ctx": flipped_bits(me, 2 * other)})
        )
    for shift in range(1, groups):
        sem = len(first)
        first.append(
            remote(kv_ref, kv_all.at[zone], send_sem.at[sem], recv_sem.at[sem],
                   {"fsdp": (zone + shift) % groups})
        )
    sem = len(first)
    second = remote(
        enc_all.at[:, core], enc_all.at[:, core], send_sem.at[sem], recv_sem.at[sem],
        {"ctx": flipped_bits(me, 1)},
    )
    local = [
        pltpu.make_async_copy(enc_ref, enc_all.at[chip, core], own_sem.at[0]),
        pltpu.make_async_copy(kv_ref, kv_all.at[zone], own_sem.at[1]),
    ]
    return first, second, local


def attend_forward(cross, heads, offsets, q, k, v, extra=()):
    count = lax.axis_size("ctx")
    rows = count * TILE
    vmem = pl.BlockSpec(memory_space=pltpu.VMEM)
    hbm = pl.BlockSpec(memory_space=pl.ANY)
    dma = pltpu.SemaphoreType.DMA
    tiles = jax.ShapeDtypeStruct((count, TILE, 128), BF)
    outs = [
        tiles,
        jax.ShapeDtypeStruct((128, rows), F32),
        jax.ShapeDtypeStruct((8, rows), F32),
    ]
    scratch = [
        pltpu.VMEM((heads, 80, TILE), F32),
        pltpu.VMEM((heads, 8, TILE), F32),
        pltpu.VMEM((heads, 80, k.shape[0]), BF),
        pltpu.VMEM((heads, TILE, TILE), F32),
        pltpu.VMEM((heads, TILE, TILE), F32),
        pltpu.VMEM((count, TILE, 128), BF),
        dma((count,)), dma((count,)), dma,
    ]
    if cross:
        outs.append(tiles)
        scratch += [pltpu.VMEM((count, TILE, 128), BF), dma((count,)), dma((count,)), dma]
        places = [vmem]
    else:
        enc, kv = extra
        groups = lax.axis_size("fsdp")
        outs.append(jax.ShapeDtypeStruct((count // 2, 2) + enc.shape, BF))
        outs.append(jax.ShapeDtypeStruct((groups,) + kv.shape, BF))
        copies = count // 2 + groups - 1
        scratch += [dma((copies,)), dma((copies,)), dma((2,))]
        places = [hbm, hbm]
    return pl.pallas_call(
        functools.partial(attend_forward_kernel, cross, heads, offsets.shape[1]),
        out_shape=outs,
        in_specs=[pl.BlockSpec(memory_space=pltpu.SMEM), vmem, vmem, vmem] + [hbm] * len(extra),
        out_specs=[hbm, vmem, vmem] + places,
        scratch_shapes=scratch,
        compiler_params=pltpu.CompilerParams(
            vmem_limit_bytes=VMEM_BYTES, collective_id=2 if cross else 1,
            has_side_effects=True,
        ),
        cost_estimate=pl.CostEstimate(
            flops=40 * 10**9, bytes_accessed=2**23, transcendentals=2**24
        ),
    )(offsets, q, k, v, *extra)


def rest_copies(sources, targets, send_sem, recv_sem):
    me = lax.axis_index("ctx")
    half = lax.axis_size("ctx") // 4
    out = []
    for other in range(1, half):
        for part in range(2):
            mine = me // 4 if part == 0 else (me // 2) % half
            sem = len(out)
            out.append(
                remote(
                    sources[part].at[:, :, flipped_bits(mine, other)],
                    targets[part].at[other - 1],
                    send_sem.at[sem], recv_sem.at[sem],
                    {"ctx": flipped_bits(me, (4 if part == 0 else 2) * other)},
                )
            )
    return out


def last_copies(sources, targets, send_sem, recv_sem):
    me, zone = lax.axis_index("ctx"), lax.axis_index("fsdp")
    chips, groups = lax.axis_size("ctx") // 2, lax.axis_size("fsdp")
    out = []
    for other in range(1, chips):
        sem = len(out)
        out.append(
            remote(
                sources[0].at[flipped_bits(me // 2, other)], targets[0].at[other - 1],
                send_sem.at[sem], recv_sem.at[sem], {"ctx": flipped_bits(me, 2 * other)},
            )
        )
    for shift in range(1, groups):
        sem = len(out)
        there = (zone + shift) % groups
        out.append(
            remote(
                sources[1].at[there], targets[1].at[shift - 1],
                send_sem.at[sem], recv_sem.at[sem], {"fsdp": there},
            )
        )
    return out


def attend_backward_kernel(
    cross, heads, conts, scale, carried, offs_ref, q_ref, k_ref, v_ref, do_ref, att_ref,
    lse_ref, *refs,
):
    sources, refs = refs[:2], refs[2:]
    if cross:
        moved_ref, dk_ref, dv_ref, *refs = refs
    else:
        moved_ref, stage, *refs = refs
    targets, refs = refs[:2], refs[2:]
    if cross:
        stage, *refs = refs
    (
        do_all, key_t, delta, dq_sum, dk_sum, dv_sum,
        send_sem, recv_sem, own_sem, do_send, do_recv, do_own, carry_send, carry_recv,
    ) = refs
    me, count = lax.axis_index("ctx"), lax.axis_size("ctx")
    tiles = count
    key_tiles = k_ref.shape[0] // TILE
    prompt = tiles * TILE - conts * CONT
    prompt_tiles = prompt // TILE
    greet(others("ctx") + ([] if cross else others("fsdp")))
    put, got, put_done = exchange(do_ref, do_all, do_send, do_recv, do_own)
    for step in range(count):
        put((me + step) % count)
    carry_copies = carried(sources, targets, carry_send, carry_recv)
    for copy in carry_copies:
        copy.start()
    send, arrived, sent = exchange(stage, moved_ref, send_sem, recv_sem, own_sem)
    dk_sum[...] = jnp.zeros_like(dk_sum)
    dv_sum[...] = jnp.zeros_like(dv_sum)
    for tile in range(key_tiles):
        at = pl.ds(tile * TILE, TILE)
        key_t[:, at] = transposed(k_ref[at, :])

    def query_tile(step, carry):
        i = (me + step) % count if cross else tiles - 1 - step
        q = q_ref[tile_rows(i), :]
        got(i)
        do = do_all[i]
        q_masked = [head_lanes(head, q) for head in range(heads)]
        do_masked = [head_lanes(head, do) for head in range(heads)]
        both = do.astype(F32).T * att_ref[:, tile_rows(i)]
        for head in range(heads):
            delta[head : head + 1, :] = jnp.sum(
                both[64 * head : 64 * head + 64], axis=0, keepdims=True
            )
        dq_sum[...] = jnp.zeros_like(dq_sum)

        def key_step(j, shown):
            at = tile_rows(j)
            k, v = k_ref[at, :], v_ref[at, :]
            for head in range(heads):
                scores = nt(k, q_masked[head])
                weights = jnp.exp(scores - lse_ref[head : head + 1, tile_rows(i)])
                if shown is not None:
                    weights = jnp.where(shown, weights, 0.0)
                weight_grad = nt(v, do_masked[head])
                score_grad = (weights * (weight_grad - delta[head : head + 1, :])).astype(BF)
                dv_sum[at, :] += nn(weights.astype(BF), do_masked[head])
                dk_sum[at, :] += nn(score_grad, q_masked[head])
                own = slice(64 * head, 64 * head + 64)
                dq_sum[own, :] += nn(key_t[own, at], score_grad)

        def plain(j, carry):
            key_step(j, None)
            return carry

        if cross:
            lax.fori_loop(0, key_tiles, plain, 0)
        elif conts == 1:
            key_step(i, visible(0, 0, TILE, TILE, 0, None))
            lax.fori_loop(0, i, plain, 0)
        else:
            cont = jnp.maximum(i * TILE - prompt, 0) // CONT
            inside = i * TILE < prompt
            own = jnp.where(inside, 0, prompt + cont * CONT)
            limit = offs_ref[0, cont]

            def one(j, carry):
                key_step(j, visible(j * TILE, i * TILE, TILE, TILE, own, limit))
                return carry

            lax.fori_loop(jnp.where(inside, 0, own // TILE), i + 1, one, 0)
            lax.fori_loop(0, jnp.where(inside, 0, prompt_tiles), one, 0)

        dq = dq_sum[...].T.astype(BF).astype(F32)
        stage[i, :, :128] = (dq * scale).astype(BF)
        if not cross:
            stage[i, :, 128:256] = dk_sum[tile_rows(i), :].astype(BF)
            stage[i, :, 256:] = dv_sum[tile_rows(i), :].astype(BF)
        send(i)
        return carry

    lax.fori_loop(0, tiles, query_tile, 0)
    if cross:
        dk_ref[...] = dk_sum[...].astype(BF)
        dv_ref[...] = dv_sum[...].astype(BF)
    for step in range(count):
        arrived((me + step) % count)
    sent()
    put_done()
    for copy in carry_copies:
        copy.wait_send()
        copy.wait_recv()


def attend_backward(cross, heads, scale, offsets, q, k, v, do, att, lse, sources, target_shapes):
    count = lax.axis_size("ctx")
    vmem = pl.BlockSpec(memory_space=pltpu.VMEM)
    hbm = pl.BlockSpec(memory_space=pl.ANY)
    dma = pltpu.SemaphoreType.DMA
    keys = k.shape[0]
    wide = 128 if cross else 384
    moved = jax.ShapeDtypeStruct((count, TILE, wide), BF)
    if cross:
        local = [jax.ShapeDtypeStruct((keys, 128), BF)] * 2
        carries = 2 * max(count // 4 - 1, 1)
    else:
        local = [jax.ShapeDtypeStruct((count, TILE, wide), BF)]
        carries = count // 2 - 1 + lax.axis_size("fsdp") - 1
    targets = [jax.ShapeDtypeStruct(shape, BF) for shape in target_shapes]
    return pl.pallas_call(
        functools.partial(
            attend_backward_kernel, cross, heads, offsets.shape[1], scale,
            rest_copies if cross else last_copies,
        ),
        out_shape=[moved] + local + targets,
        in_specs=[pl.BlockSpec(memory_space=pltpu.SMEM)] + [vmem] * 6 + [hbm] * 2,
        out_specs=[hbm] + [vmem] * len(local) + [hbm] * 2,
        scratch_shapes=([pltpu.VMEM((count, TILE, wide), BF)] if cross else [])
        + [
            pltpu.VMEM((count, TILE, 128), BF),
            pltpu.VMEM((128, keys), BF),
            pltpu.VMEM((8, TILE), F32),
            pltpu.VMEM((128, TILE), F32),
            pltpu.VMEM((keys, 128), F32),
            pltpu.VMEM((keys, 128), F32),
            dma((count,)), dma((count,)), dma,
            dma((count,)), dma((count,)), dma,
            dma((carries,)), dma((carries,)),
        ],
        compiler_params=pltpu.CompilerParams(
            vmem_limit_bytes=VMEM_BYTES, collective_id=3 if cross else 4,
            has_side_effects=True,
        ),
        cost_estimate=pl.CostEstimate(
            flops=60 * 10**9, bytes_accessed=2**23, transcendentals=2**24
        ),
    )(offsets, q, k, v, do, att, lse, *sources)


def project_kernel(
    own, scale, tokens_ref, small_ref, head_ref, normed_ref, q_ref, k_ref, v_ref,
    small_all, head_all, all_tokens, staged, token_send, token_recv, part_send, part_recv,
    own_sem, stage_sem,
):
    me, zone = lax.axis_index("ctx"), lax.axis_index("fsdp")
    count, groups = lax.axis_size("ctx"), lax.axis_size("fsdp")
    chips = count // 2
    shard = small_ref.shape[1]
    sibling = {"ctx": flipped_bits(me, 1)}
    near = [flipped_bits(me, 2 * other) for other in range(1, chips)]
    greet([sibling] + [{"ctx": there} for there in near] + others("fsdp"))

    parts = []
    for shift in range(1, groups):
        there = {"fsdp": (zone + shift) % groups}
        for index, (source, target) in enumerate(((small_ref, small_all), (head_ref, head_all))):
            parts.append(
                remote(source, target.at[zone], part_send.at[index, shift - 1],
                       part_recv.at[index, shift - 1], there)
            )
    local = [
        pltpu.make_async_copy(small_ref, small_all.at[zone], own_sem.at[0]),
        pltpu.make_async_copy(head_ref, head_all.at[zone], own_sem.at[1]),
        pltpu.make_async_copy(tokens_ref, all_tokens.at[me], own_sem.at[2]),
    ]
    for copy in local:
        copy.start()
    for copy in parts:
        copy.start()

    def direct(there, block):
        return remote(tokens_ref, all_tokens.at[block], token_send.at[there],
                      token_recv.at[block], {"ctx": there})

    def passed(block):
        return remote(
            all_tokens.at[block], all_tokens.at[block], token_send.at[flipped_bits(block, 1)],
            token_recv.at[block], sibling,
        )

    for there in near + [flipped_bits(me, 1)]:
        direct(there, me).start()
    for copy in local:
        copy.wait()
    for copy in parts:
        copy.wait_recv()

    def row(index):
        pieces = [small_all[z].astype(F32)[index : index + 1] for z in range(groups)]
        return jnp.concatenate(pieces, axis=1)

    gain, shift = row(0), row(3)
    mine = small_all[me // (shard // own)].astype(F32)
    q_shift = jnp.where(me % 2 == 0, mine[6:7, :own], mine[6:7, own : 2 * own])
    v_shift = jnp.where(me % 2 == 0, mine[7:8, :own], mine[7:8, own : 2 * own])
    if own < 128:
        for ref in (q_ref, k_ref, v_ref):
            ref[...] = jnp.zeros_like(ref)

    def save(block, place):
        return pltpu.make_async_copy(staged.at[place], normed_ref.at[block], stage_sem.at[place])

    order = [me, flipped_bits(me, 1)] + near + [flipped_bits(there, 1) for there in near]
    for step, block in enumerate(order):
        place = step % 2
        if step == 1:
            direct(block, block).wait_recv()
        elif step >= 2:
            if step <= chips:
                direct(block, block).wait_recv()
                passed(block).start()
            else:
                passed(block).wait_recv()
        if step >= 2:
            save(order[step - 2], place).wait()
        unit, _ = normalize(all_tokens[block].astype(F32))
        staged[place] = (unit * gain + shift).astype(BF)
        save(block, place).start()
        total = jnp.zeros((staged.shape[1], 3 * own), F32)
        for z in range(groups):
            total = total + nn(staged[place, :, z * shard : z * shard + shard], head_all[z])
        q_ref[block, :, :own] = (scale * (total[:, :own] + q_shift)).astype(BF)
        k_ref[block, :, :own] = total[:, own : 2 * own].astype(BF)
        v_ref[block, :, :own] = (total[:, 2 * own :] + v_shift).astype(BF)
    for step in (count - 2, count - 1):
        save(order[step], step % 2).wait()
    for copy in parts:
        copy.wait_send()
    for there in near + [flipped_bits(me, 1)]:
        direct(there, me).wait_send()
    for there in near:
        passed(there).wait_send()


def project(own, scale, tokens, small, head_in):
    count, groups = lax.axis_size("ctx"), lax.axis_size("fsdp")
    rows, width = tokens.shape
    vmem = pl.BlockSpec(memory_space=pltpu.VMEM)
    hbm = pl.BlockSpec(memory_space=pl.ANY)
    dma = pltpu.SemaphoreType.DMA
    lanes = jax.ShapeDtypeStruct((count, rows, 128), BF)
    return pl.pallas_call(
        functools.partial(project_kernel, own, scale),
        out_shape=(
            jax.ShapeDtypeStruct((count, rows, width), BF),
            lanes, lanes, lanes,
            jax.ShapeDtypeStruct((groups,) + small.shape, BF),
            jax.ShapeDtypeStruct((groups,) + head_in.shape, BF),
        ),
        in_specs=[hbm, hbm, hbm],
        out_specs=(hbm,) + (vmem,) * 5,
        scratch_shapes=[
            pltpu.VMEM((count, rows, width), BF),
            pltpu.VMEM((2, rows, width), BF),
            dma((count,)), dma((count,)),
            dma((2, groups - 1)), dma((2, groups - 1)),
            dma((3,)), dma((2,)),
        ],
        compiler_params=pltpu.CompilerParams(
            vmem_limit_bytes=VMEM_BYTES, collective_id=5, has_side_effects=True
        ),
        cost_estimate=pl.CostEstimate(
            flops=50 * 10**9, bytes_accessed=2**25, transcendentals=0
        ),
    )(tokens, small, head_in)


def ffn_kernel(
    steps, groups, n_ref, dy_ref, base_ref, bias_ref, win_ref, wout_ref,
    out_ref, gn_ref, gb_ref, in_ref, sum_ref,
    n_t, own_in, own_out, post_in, post_out, got_in, got_out,
    keep_in, keep_out, flow_in, flow_out, near_in, near_out,
    send_sem, recv_sem, flow_send, flow_recv, save_sem,
):
    f = pl.program_id(0)
    me = lax.axis_index("ctx")
    count = lax.axis_size("ctx")
    chips = count // 2
    core = me % 2
    low_bit = (me // 2) % 2
    high_bit = me // chips
    cols = keep_in.shape[2]
    slot = f % 2
    sibling = {"ctx": flipped_bits(me, 1)}
    low = {"ctx": flipped_bits(me, 2)}
    high = {"ctx": flipped_bits(me, chips)}

    def copies(step, place):
        return (
            remote(post_in.at[place], got_in.at[step], send_sem.at[0, place],
                   recv_sem.at[0, step], sibling),
            remote(post_out.at[place], got_out.at[step], send_sem.at[1, place],
                   recv_sem.at[1, step], sibling),
        )

    def flows(step, place):
        return (
            remote(flow_in.at[place], near_in.at[step], flow_send.at[0, place],
                   flow_recv.at[0, step], low),
            remote(flow_out.at[place], near_out.at[step], flow_send.at[1, place],
                   flow_recv.at[1, step], high),
        )

    @pl.when(f == 0)
    def _():
        greet([sibling, low, high])
        n_t[...] = transposed(n_ref[...])
        gn_ref[...] = jnp.zeros_like(gn_ref)
        out_ref[...] = base_ref[...]

    @pl.when(f < steps)
    def _():
        @pl.when(f >= 2)
        def _():
            for copy in copies(jnp.maximum(f - 2, 0), slot):
                copy.wait_send()

        pre = nn(n_ref[...], win_ref[...]) + bias_ref[0, :1]
        below = 0.5 * (1.0 + lax.erf(pre * (1.0 / math.sqrt(2.0))))
        hidden = (pre * below).astype(BF)
        out_ref[...] += nn(hidden, wout_ref[...])
        slope = below + pre * (jnp.exp(-0.5 * pre * pre) * (1.0 / math.sqrt(2.0 * math.pi)))
        dy = dy_ref[...]
        grad_pre = (nt(dy, wout_ref[...]) * slope).astype(BF)
        gb_ref[0] = jnp.broadcast_to(
            jnp.sum(grad_pre.astype(F32), axis=0, keepdims=True), gb_ref.shape[1:]
        )
        gn_ref[...] += nt(grad_pre, win_ref[...])

        def split(part, keep, post, half):
            left, right = part[:, :half], part[:, half:]
            keep[slot] = jnp.where(core == 0, left, right)
            post[slot] = jnp.where(core == 0, right, left).astype(BF)

        first, second = copies(jnp.minimum(f, steps - 1), slot)
        split(nn(n_t[...], grad_pre), own_in, post_in, cols)
        first.start()
        split(tn(hidden, dy), own_out, post_out, 2 * cols)
        second.start()

    @pl.when(f > 0)
    def _():
        past = jnp.maximum(f - 1, 0)
        place = (f + 1) % 2
        for copy in copies(past, place):
            copy.wait_recv()

        @pl.when(f >= 3)
        def _():
            for copy in flows(jnp.maximum(f - 3, 0), place):
                copy.wait_send()

        unit = keep_in.shape[1] // (groups * (chips // 2))
        for slab in range(groups * (chips // 2)):
            for kept in (True, False):
                take = low_bit if kept else 1 - low_bit
                rows = pl.ds(pl.multiple_of((2 * slab + take) * unit, unit), unit)
                both = own_in[place, rows, :] + got_in[past, rows, :].astype(F32)
                at = slice(unit * slab, unit * slab + unit)
                if kept:
                    keep_in[past, at, :] = both.astype(BF)
                else:
                    flow_in[place, at, :] = both.astype(BF)
        unit = n_t.shape[0] // groups // 2
        for slab in range(own_out.shape[1] // (2 * unit)):
            for kept in (True, False):
                take = high_bit if kept else 1 - high_bit
                rows = pl.ds(pl.multiple_of((2 * slab + take) * unit, unit), unit)
                both = own_out[place, rows, :] + got_out[past, rows, :].astype(F32)
                at = slice(unit * slab, unit * slab + unit)
                for half in range(2):
                    value = both[:, half * cols : half * cols + cols].astype(BF)
                    if kept:
                        keep_out[past, half, at, :] = value
                    else:
                        flow_out[place, half, at, :] = value
        for copy in flows(past, place):
            copy.start()

    @pl.when(f == steps)
    def _():
        for back in (2, 1):
            for copy in copies(steps - back, (steps - back) % 2):
                copy.wait_send()
            for copy in flows(steps - back, (steps - back) % 2):
                copy.wait_send()
        per = steps // sum_ref.shape[0]
        height = keep_out.shape[2]

        def saves(step):
            rows = pl.ds(pl.multiple_of((step % per) * height, height), height)
            return (
                pltpu.make_async_copy(
                    keep_in.at[step], in_ref.at[step], save_sem.at[0, step]
                ),
                pltpu.make_async_copy(
                    keep_out.at[step], sum_ref.at[step // per, :, rows], save_sem.at[1, step]
                ),
            )

        def join(step, carry):
            for copy in flows(step, step % 2):
                copy.wait_recv()
            keep_in[step] = (
                keep_in[step].astype(F32) + near_in[step].astype(F32)
            ).astype(BF)
            keep_out[step] = (
                keep_out[step].astype(F32) + near_out[step].astype(F32)
            ).astype(BF)
            for copy in saves(step):
                copy.start()
            return carry

        def saved(step, carry):
            for copy in saves(step):
                copy.wait()
            return carry

        lax.fori_loop(0, steps, join, 0)
        lax.fori_loop(0, steps, saved, 0)


def ffn(normed, dy, base, bias, weights):
    rows, width = normed.shape
    hidden = weights.shape[1] // 2
    groups = lax.axis_size("fsdp")
    step = 512
    cols = step // 2
    steps = hidden // step
    per = width // step
    last = steps - 1

    def now(f):
        return jnp.minimum(f, last)

    whole = lambda f: (0, 0)
    hbm = pl.BlockSpec(memory_space=pl.ANY)
    dma = pltpu.SemaphoreType.DMA
    once = pl.BlockSpec((rows, width), whole, pipeline_mode=pl.Buffered(1))
    return pl.pallas_call(
        functools.partial(ffn_kernel, steps, groups),
        grid=(steps + 1,),
        out_shape=(
            jax.ShapeDtypeStruct((rows, width), F32),
            jax.ShapeDtypeStruct((rows, width), F32),
            jax.ShapeDtypeStruct((steps, 8, step), F32),
            jax.ShapeDtypeStruct((steps, width // 2, cols), BF),
            jax.ShapeDtypeStruct((hidden // width, 2, width // 2, cols), BF),
        ),
        in_specs=[
            once, once, once,
            pl.BlockSpec((1, 8, step), lambda f: (now(f), 0, 0)),
            pl.BlockSpec((width, step), lambda f: (0, now(f))),
            pl.BlockSpec(
                (step, width), lambda f: (now(f) % per, hidden // width + now(f) // per)
            ),
        ],
        out_specs=(
            pl.BlockSpec((rows, width), whole),
            pl.BlockSpec((rows, width), whole),
            pl.BlockSpec((1, 8, step), lambda f: (now(f), 0, 0)),
            hbm, hbm,
        ),
        scratch_shapes=[
            pltpu.VMEM((width, rows), BF),
            pltpu.VMEM((2, width, cols), F32),
            pltpu.VMEM((2, step, 2 * cols), F32),
            pltpu.VMEM((2, width, cols), BF),
            pltpu.VMEM((2, step, 2 * cols), BF),
            pltpu.VMEM((steps, width, cols), BF),
            pltpu.VMEM((steps, step, 2 * cols), BF),
            pltpu.VMEM((steps, width // 2, cols), BF),
            pltpu.VMEM((steps, 2, step // 2, cols), BF),
            pltpu.VMEM((2, width // 2, cols), BF),
            pltpu.VMEM((2, 2, step // 2, cols), BF),
            pltpu.VMEM((steps, width // 2, cols), BF),
            pltpu.VMEM((steps, 2, step // 2, cols), BF),
            dma((2, 2)), dma((2, steps)), dma((2, 2)), dma((2, steps)), dma((2, steps)),
        ],
        compiler_params=pltpu.CompilerParams(
            vmem_limit_bytes=60 * 2**20, collective_id=0, has_side_effects=True
        ),
        cost_estimate=pl.CostEstimate(
            flops=30 * 10**9, bytes_accessed=2**26, transcendentals=2**22
        ),
    )(normed, dy, base, bias, weights, weights)


def token_grad_kernel(
    own, moved_ref, wq_ref, wk_ref, wv_ref, tokens_ref, gain_ref, first_ref, out_ref
):
    step = pl.program_id(0)

    @pl.when(step == 0)
    def _():
        out_ref[...] = jnp.zeros_like(out_ref)

    grads = moved_ref[0]
    total = out_ref[...]
    for part, weight in enumerate((wq_ref, wk_ref, wv_ref)):
        total = total + nt(grads[:, part * 128 : part * 128 + own], weight[...])
    out_ref[...] = total

    @pl.when(step == pl.num_programs(0) - 1)
    def _():
        unit, scale = normalize(tokens_ref[...].astype(F32))
        q = gain_ref[...] * out_ref[...]
        mean = jnp.mean(q, axis=-1, keepdims=True)
        slant = jnp.mean(q * unit, axis=-1, keepdims=True)
        out_ref[...] = first_ref[...] + scale * (q - mean - unit * slant)


def token_grad(moved, weights, tokens, gain, first):
    ctx, rows, wide = moved.shape
    width = tokens.shape[1]
    own = width // ctx
    if own < 128:
        cut = moved.reshape(ctx, rows, 3, 128)[:, :, :, :own]
        grads = jnp.transpose(cut, (1, 2, 0, 3)).reshape(rows, 3 * width)
        unit, scale = normalize(tokens.astype(F32))
        return first + normalize_back(unit, scale, gain, nt(grads, weights))[0]
    whole = pl.BlockSpec((rows, width), lambda s: (0, 0))
    return pl.pallas_call(
        functools.partial(token_grad_kernel, own),
        grid=(ctx,),
        out_shape=jax.ShapeDtypeStruct((rows, width), F32),
        in_specs=[
            pl.BlockSpec((1, rows, wide), lambda s: (s, 0, 0)),
            pl.BlockSpec((width, own), lambda s: (0, s)),
            pl.BlockSpec((width, own), lambda s: (0, ctx + s)),
            pl.BlockSpec((width, own), lambda s: (0, 2 * ctx + s)),
            whole,
            pl.BlockSpec((1, width), lambda s: (0, 0)),
            whole,
        ],
        out_specs=whole,
        compiler_params=pltpu.CompilerParams(vmem_limit_bytes=VMEM_BYTES),
        cost_estimate=pl.CostEstimate(flops=10**10, bytes_accessed=2**24, transcendentals=0),
    )(moved, weights, weights, weights, tokens, gain, first)


def place_ffn_kernel(groups, sum_ref, in_ref, out_ref):
    chips, _, lead, part, cols = sum_ref.shape
    steps = lead // 2
    depth, hidden = in_ref.shape
    blocks = hidden // (depth * groups)
    per = steps // blocks
    span = min(depth, cols)
    for chip in range(chips):
        rows = slice(chip * part, chip * part + part)
        for core in range(2):
            for f in range(steps):
                value = sum_ref[chip, core, f].astype(F32)
                for piece in range(cols // span):
                    unit = (f % per) * 2 * cols + core * cols + piece * span
                    at = (unit // depth * blocks + f // per) * depth + unit % depth
                    in_ref[rows, at : at + span] = value[:, piece * span : piece * span + span]
            for slab in range(steps):
                block, half = slab // 2, slab % 2
                top = block * depth + chip * part
                at = (core * 2 + half) * cols
                out_ref[top : top + part, at : at + cols] = sum_ref[
                    chip, core, steps + slab
                ].astype(F32)


def place_ffn(sums, depth, hidden, rows, width):
    vmem = pl.BlockSpec(memory_space=pltpu.VMEM)
    return pl.pallas_call(
        functools.partial(place_ffn_kernel, width // depth),
        out_shape=(
            jax.ShapeDtypeStruct((depth, hidden), F32),
            jax.ShapeDtypeStruct((rows, width), F32),
        ),
        in_specs=[vmem],
        out_specs=(vmem, vmem),
        compiler_params=pltpu.CompilerParams(vmem_limit_bytes=VMEM_BYTES),
        cost_estimate=pl.CostEstimate(flops=0, bytes_accessed=2**24, transcendentals=0),
    )(sums)


def place_late_kernel(tall, sum_ref, self_ref, kv_ref, *refs):
    ctx, _, own = sum_ref.shape
    depth, width = refs[0].shape
    part = depth // (ctx // 2)
    for src in range(ctx):
        for k in range(5):
            target = self_ref if k < 3 else kv_ref
            at = (k if k < 3 else k - 3) * width + src * own
            top = k * tall
            target[:, at : at + own] = sum_ref[src, top : top + depth, :].astype(F32)
        for w, target in enumerate(refs):
            for block in range(width // 2 // own):
                top = 5 * tall + (w * (width // 2 // own) + block) * part
                at = (src % 2) * (width // 2) + block * own
                rows = slice(src // 2 * part, src // 2 * part + part)
                target[rows, at : at + own] = sum_ref[src, top : top + part, :].astype(F32)


def place_late(sums, tall, depth, width):
    vmem = pl.BlockSpec(memory_space=pltpu.VMEM)
    small = jax.ShapeDtypeStruct((depth, width), F32)
    return pl.pallas_call(
        functools.partial(place_late_kernel, tall),
        out_shape=(
            jax.ShapeDtypeStruct((depth, 3 * width), F32),
            jax.ShapeDtypeStruct((depth, 2 * width), F32),
            small, small, small,
        ),
        in_specs=[vmem],
        out_specs=(vmem,) * 5,
        compiler_params=pltpu.CompilerParams(vmem_limit_bytes=VMEM_BYTES),
        cost_estimate=pl.CostEstimate(flops=0, bytes_accessed=2**24, transcendentals=0),
    )(sums)


def swap(value, bit):
    count = lax.axis_size("ctx")
    return lax.ppermute(value, "ctx", [(i, i ^ bit) for i in range(count)])


def across_groups(value):
    count = lax.axis_size("fsdp")
    me = lax.axis_index("fsdp")
    total = lax.dynamic_index_in_dim(value, me, 0, keepdims=False).astype(F32)
    for shift in range(1, count):
        send = lax.dynamic_index_in_dim(value, (me + shift) % count, 0, keepdims=False)
        got = lax.ppermute(send, "fsdp", [(i, (i + shift) % count) for i in range(count)])
        total = total + got.astype(F32)
    return total


def pair_product(left, right):
    core = lax.axis_index("ctx") % 2
    half = right.shape[1] // 2
    send = tn(left, lax.dynamic_slice_in_dim(right, (1 - core) * half, half, 1)).astype(BF)
    got = swap(send, 1).astype(F32)
    kept = tn(left, lax.dynamic_slice_in_dim(right, core * half, half, 1))
    return (kept + got).astype(BF)


def ctx_gather(value):
    count = lax.axis_size("ctx")
    full = lax.all_gather(value, "ctx", axis=0)
    return full.reshape((count // 2, 2) + value.shape)


def gather_all(pieces):
    count = lax.axis_size("ctx")
    me = lax.axis_index("ctx")
    rows = pieces[0].shape[0] // count
    cut = [lax.dynamic_slice_in_dim(p, me * rows, rows, 0) for p in pieces]
    joined = jnp.concatenate(cut, axis=1)
    full = lax.all_gather(joined, ("fsdp", "ctx"), axis=0, tiled=True)
    out, at = [], 0
    for p in pieces:
        out.append(full[:, at : at + p.shape[1]])
        at += p.shape[1]
    return out


def gather_ffn(ffn_in, ffn_out):
    count = lax.axis_size("ctx")
    groups = lax.axis_size("fsdp")
    me = lax.axis_index("ctx")
    depth, hidden = ffn_in.shape
    width = ffn_out.shape[1]
    blocks = hidden // width
    rows = depth // count
    left = lax.dynamic_slice_in_dim(ffn_in, me * rows, rows, 0)
    left = left.reshape(rows, groups, blocks, depth)
    left = jnp.transpose(left, (0, 2, 1, 3)).reshape(rows, hidden)
    right = lax.dynamic_index_in_dim(
        ffn_out.reshape(blocks, count, rows, width), me, 1, keepdims=False
    )
    right = jnp.moveaxis(right, 0, 1).reshape(rows, hidden)
    joined = jnp.concatenate([left, right], axis=1)
    return lax.all_gather(joined, ("fsdp", "ctx"), axis=0, tiled=True)


def body(
    tokens, encoder_out, prompt_offsets, gains, shifts, self_in, self_out, cross_q, cross_kv,
    cross_out, ffn_in, ffn_bias, ffn_out, out_bias, cotangent,
):
    row_count, width = tokens.shape
    head_dim = width // HEADS
    scale = 1.0 / math.sqrt(head_dim)
    ctx = lax.axis_size("ctx")
    groups = lax.axis_size("fsdp")
    me = lax.axis_index("ctx")
    heads = HEADS // ctx
    own = heads * head_dim

    shard = gains.shape[1]
    small = jnp.concatenate(
        [gains, shifts, out_bias[None], ffn_bias.reshape(-1, shard)], axis=0
    )
    small_rows = small.shape[0]
    small = jnp.pad(small, ((0, 32 - small_rows), (0, 0)))

    head_in = lax.dynamic_index_in_dim(
        self_in.reshape(self_in.shape[0], 3, ctx, own), me, 2, keepdims=False
    ).reshape(-1, 3 * own)
    all_normed, queries, keys, values, small, head_in = project(
        own, scale, tokens, small, head_in
    )
    all_normed = all_normed.reshape(-1, width)
    queries, keys, values = [x.reshape(-1, 128) for x in (queries, keys, values)]
    small = small[:, :small_rows].astype(F32)
    vectors = jnp.moveaxis(small[:, :13], 0, 1).reshape(13, width)
    gain, shift, full_out_bias = vectors[:3], vectors[3:12], vectors[12]
    full_ffn_bias = small[:, 13:].reshape(-1)

    full_self_out, full_cross_q, full_cross_out = gather_all([self_out, cross_q, cross_out])
    ffn_weights = gather_ffn(ffn_in, ffn_out)
    def lanes(value):
        gap = [(0, 0)] * (value.ndim - 1) + [(0, 128 - own)]
        return value if own == 128 else jnp.pad(value, gap)

    head_kv = lax.dynamic_index_in_dim(
        cross_kv.reshape(-1, 2, ctx, own), me, 2, keepdims=False
    ).reshape(-1, 2 * own)
    mixed_heads, att_self, lse_self, all_encoder, head_kv = attend_forward(
        False, heads, prompt_offsets, queries, keys, values, (encoder_out, head_kv)
    )
    all_encoder = all_encoder.reshape(-1, width)
    head_kv = head_kv.reshape(width, 2 * own)

    def to_rows(value):
        return jnp.moveaxis(value[:, :, :own], 0, 1).reshape(row_count, width)

    def to_heads(value):
        return lanes(jnp.moveaxis(value.reshape(row_count, ctx, own), 1, 0))

    mixed = to_rows(mixed_heads)
    token_values = tokens.astype(F32)
    first = token_values + nn(mixed, full_self_out) + shift[5]
    unit_two, scale_two = normalize(first)
    normed_two = (unit_two * gain[1] + shift[1]).astype(BF)
    cross_queries = (scale * (nn(normed_two, full_cross_q) + shift[6])).astype(BF)
    enc_shift = lax.dynamic_slice_in_dim(shift[7], me * own, own, 0)
    enc_projected = nn(all_encoder, head_kv)
    enc_keys = lanes(enc_projected[:, :own].astype(BF))
    enc_values = lanes((enc_projected[:, own:] + enc_shift).astype(BF))
    cross_heads, att_cross, lse_cross, all_cross_q = attend_forward(
        True, heads, prompt_offsets, to_heads(cross_queries), enc_keys, enc_values
    )
    cross_mixed = to_rows(cross_heads)
    second = first + nn(cross_mixed, full_cross_out) + shift[8]
    unit_three, scale_three = normalize(second)
    normed_three = (unit_three * gain[2] + shift[2]).astype(BF)
    depth = ffn_in.shape[0]
    blocks = ffn_in.shape[1] // width
    order = full_ffn_bias.reshape(groups, blocks, depth)
    order = jnp.moveaxis(order, 0, 1).reshape(-1, 1, 512)
    layer_sum, grad_three, bias_parts, in_sum, out_sum = ffn(
        normed_three, cotangent, second + full_out_bias,
        jnp.broadcast_to(order, (order.shape[0], 8, 512)), ffn_weights,
    )
    layer_out = layer_sum.astype(BF)
    late_in, late_kv, grad_three = lax.optimization_barrier((self_in, cross_kv, grad_three))
    full_self_in, full_cross_kv = gather_all([late_in, late_kv])
    chips = ctx // 2
    part = depth // chips
    in_sum = in_sum.reshape(-1, groups, chips // 2, part, 256)
    out_sum = out_sum.reshape(-1, groups, chips // 2, part, 256)

    dy = cotangent.astype(F32)
    back_three = normalize_back(unit_three, scale_three, gain[2], grad_three)
    grad_second = dy + back_three[0]
    branch_two = grad_second.astype(BF)
    middle = [pair_product(cross_mixed, branch_two)]
    grad_cross_mixed = nt(branch_two, full_cross_out).astype(BF)
    got_shape = (max(chips // 2 - 1, 1),) + in_sum.shape[:2] + in_sum.shape[3:]
    cross_moved, cross_dk, cross_dv, in_got, out_got = attend_backward(
        True, heads, scale, prompt_offsets, all_cross_q.reshape(-1, 128), enc_keys, enc_values,
        to_heads(grad_cross_mixed), att_cross, lse_cross, (in_sum, out_sum),
        (got_shape, got_shape),
    )

    def joined(value, mine, dim, got):
        kept = lax.dynamic_index_in_dim(value, mine, dim, keepdims=False).astype(F32)
        return kept + jnp.sum(got.astype(F32), axis=0)

    cross_dq = to_rows(cross_moved)
    back_two = normalize_back(unit_two, scale_two, gain[1], nt(cross_dq, full_cross_q))
    grad_first = grad_second + back_two[0]
    branch_one = grad_first.astype(BF)
    grad_mixed = nt(branch_one, full_self_out).astype(BF)
    middle.append(pair_product(normed_two, cross_dq))
    middle.append(pair_product(mixed, branch_one))
    middle = jnp.stack([m.reshape(groups, chips, part, -1) for m in middle])
    middle = jnp.moveaxis(middle, 2, 0)
    ffn_sums = jnp.concatenate(
        [
            joined(in_sum, me // 4, 2, in_got),
            joined(out_sum, (me // 2) % (chips // 2), 2, out_got),
        ],
        axis=0,
    )
    ffn_sums = jnp.moveaxis(ffn_sums.astype(BF), 1, 0)
    grad_rows, full_self_in, full_cross_kv = lax.optimization_barrier(
        (to_heads(grad_mixed), full_self_in, full_cross_kv)
    )
    moved, grad_heads, middle_got, ffn_got = attend_backward(
        False, heads, scale, prompt_offsets, queries, keys, values, grad_rows,
        att_self, lse_self, (middle, ffn_sums),
        ((chips - 1,) + middle.shape[1:], (groups - 1,) + ffn_sums.shape[1:]),
    )
    zone = lax.axis_index("fsdp")
    ffn_sums = joined(ffn_sums, zone, 0, ffn_got).astype(BF)
    middle = joined(middle, me // 2, 0, middle_got).astype(BF)
    input_grad = token_grad(moved, full_self_in, tokens, gain[:1], grad_first)
    grad_heads = grad_heads.reshape(-1, 3, 128)[:, :, :own].reshape(-1, 3 * own)

    grad_ffn_in, grad_ffn_out = place_ffn(
        ctx_gather(ffn_sums), depth, ffn_in.shape[1], ffn_out.shape[0], width
    )

    grad_head_in = tn(all_normed, grad_heads)
    enc_heads = jnp.concatenate([cross_dk[:, :own], cross_dv[:, :own]], axis=1)
    grad_head_kv = tn(all_encoder, enc_heads)
    column = jnp.sum(grad_heads.astype(F32), axis=0)
    weight = head_in.reshape(width, 3 * own).astype(F32)
    grad_shift_one = jnp.sum(weight * column, axis=1)
    grad_gain_one = jnp.sum(weight * (grad_head_in - shift[0][:, None] * column), axis=1) / gain[0]

    def spread(value):
        return lax.dynamic_update_slice_in_dim(jnp.zeros((width,), F32), value, me * own, 0)

    totals = jnp.stack(
        [
            grad_gain_one, back_two[1], back_three[1],
            grad_shift_one, back_two[2], back_three[2],
            spread(column[:own]), spread(column[2 * own :]),
            jnp.sum(branch_one.astype(F32), axis=0),
            jnp.sum(cross_dq.astype(F32), axis=0),
            spread(jnp.sum(enc_heads[:, own:].astype(F32), axis=0)),
            jnp.sum(branch_two.astype(F32), axis=0),
            jnp.sum(dy, axis=0),
        ]
    )
    totals = jnp.moveaxis(totals.reshape(13, groups, shard), 1, 0).reshape(groups, -1)
    bias = jnp.moveaxis(bias_parts[:, 0].reshape(blocks, groups, depth), 0, 1)
    totals = jnp.concatenate([totals, bias.reshape(groups, -1)], axis=1)
    count = totals.shape[1]
    totals = jnp.pad(totals, ((0, 0), (0, 80 * own - count))).reshape(groups, 5, 16, own)
    late = jnp.concatenate([grad_head_in, grad_head_kv], axis=1)
    late = jnp.moveaxis(late.reshape(groups, depth, 5, own), 2, 1)
    late = jnp.concatenate([late, totals], axis=2).astype(BF)
    enc_sum = enc_heads.reshape(ctx, -1, 2 * own)
    enc_sum = lax.all_to_all(enc_sum, "ctx", split_axis=0, concat_axis=0, tiled=True)
    late, enc_sum = lax.optimization_barrier((late, enc_sum))
    late = across_groups(late).astype(BF)
    middle = across_groups(jnp.moveaxis(middle, 1, 0)).astype(BF)
    middle = jnp.moveaxis(middle.reshape(3, part, -1, own), 2, 1)
    packed = jnp.concatenate([late.reshape(-1, own), middle.reshape(-1, own)], axis=0)
    packed = lax.all_gather(packed, "ctx", axis=0)
    tall = depth + 16
    grad_self_in, grad_cross_kv, grad_cross_out, grad_cross_q, grad_self_out = place_late(
        packed, tall, depth, width
    )
    sums = packed[:, : 5 * tall].reshape(ctx, 5, tall, own)[:, :, depth:]
    sums = jnp.sum(sums.astype(F32), axis=0).reshape(-1)[:count]
    mine, grad_ffn_bias = sums[: 13 * shard].reshape(13, shard), sums[13 * shard :]

    enc_sum = jnp.transpose(enc_sum.reshape(ctx, -1, 2, own), (1, 2, 0, 3))
    grad_encoder = nt(enc_sum.reshape(-1, 2 * width), full_cross_kv)
    return (
        layer_out, input_grad, grad_encoder, mine[:3], mine[3:12], grad_self_in, grad_self_out,
        grad_cross_q, grad_cross_kv, grad_cross_out, grad_ffn_in, grad_ffn_bias, grad_ffn_out, mine[12],
    )


def solution(mesh):
    rows = P(("fsdp", "ctx"), None)
    shard = P("fsdp", None)
    thin = P(None, "fsdp")
    flat = P("fsdp")
    return jax.shard_map(
        body,
        mesh=mesh,
        in_specs=(
            rows, rows, shard, thin, thin, shard, shard, shard, shard, shard, shard, flat, shard,
            flat, rows,
        ),
        out_specs=(
            rows, rows, rows, thin, thin, shard, shard, shard, shard, shard, shard, flat, shard,
            flat,
        ),
        check_vma=False,
    )
```

```python
import functools
import math

import jax
import jax.numpy as jnp
from jax import lax
from jax.experimental import pallas as pl
from jax.experimental.pallas import tpu as pltpu
from jax.sharding import PartitionSpec as P

HEADS = 16
CONT = 2048
EPS = 1e-05
NEG = -1e30
TILE = 512
BF = jnp.bfloat16
F32 = jnp.float32
VMEM_BYTES = 56 * 2**20


def nn(left, right):
    return lax.dot_general(left, right, (((1,), (0,)), ((), ())), preferred_element_type=F32)


def nt(left, right):
    return lax.dot_general(left, right, (((1,), (1,)), ((), ())), preferred_element_type=F32)


def tn(left, right):
    return lax.dot_general(left, right, (((0,), (0,)), ((), ())), preferred_element_type=F32)


def normalize(values):
    center = values - jnp.mean(values, axis=-1, keepdims=True)
    scale = lax.rsqrt(jnp.mean(center * center, axis=-1, keepdims=True) + EPS)
    return center * scale, scale


def normalize_back(unit, scale, gain, grad):
    q = gain * grad
    back = scale * (
        q - jnp.mean(q, axis=-1, keepdims=True) - unit * jnp.mean(q * unit, axis=-1, keepdims=True)
    )
    return back, jnp.sum(grad * unit, axis=0), jnp.sum(grad, axis=0)


def head_lanes(head, array):
    lane = lax.broadcasted_iota(jnp.int32, array.shape, 1)
    keep = (lane < 64) if head == 0 else (lane >= 64)
    return jnp.where(keep, array, jnp.zeros_like(array))


def transposed(array):
    return array.astype(F32).T.astype(BF)


def visible(key_start, query_start, key_count, query_count, own_start, limit):
    key = key_start + lax.broadcasted_iota(jnp.int32, (key_count, query_count), 0)
    query = query_start + lax.broadcasted_iota(jnp.int32, (key_count, query_count), 1)
    shown = key <= query
    if limit is not None:
        shown = shown & ((key >= own_start) | (key < limit))
    return shown


def soften(scores, total, peak, value_t):
    old = peak[:1]
    new = jnp.maximum(old, jnp.max(scores, axis=0, keepdims=True))
    raised = jnp.exp(scores - new).astype(BF)
    total[...] = total[...] * jnp.exp(old - new) + nn(value_t, raised)
    peak[...] = jnp.broadcast_to(new, peak.shape)


def set_value_rows(value_t, head, columns, value):
    value_t[head, :64, columns] = value[64 * head : 64 * head + 64]
    value_t[head, 64:, columns] = jnp.ones((16, value.shape[1]), BF)


def tile_rows(tile):
    return pl.ds(pl.multiple_of(tile * TILE, TILE), TILE)


def flipped_bits(index, mask):
    out, bit = index, 1
    while bit <= mask:
        if mask & bit:
            out = out + bit - 2 * bit * ((index // bit) % 2)
        bit *= 2
    return out


def greet(peers):
    barrier = pltpu.get_barrier_semaphore()
    for peer in peers:
        pl.semaphore_signal(
            barrier, inc=1, device_id=peer, device_id_type=pl.DeviceIdType.MESH
        )
    pl.semaphore_wait(barrier, len(peers))


def others(axis):
    me, count = lax.axis_index(axis), lax.axis_size(axis)
    return [{axis: (me + step) % count} for step in range(1, count)]


def remote(source, target, send_sem, recv_sem, device):
    return pltpu.make_async_remote_copy(
        source, target, send_sem, recv_sem, device_id=device,
        device_id_type=pl.DeviceIdType.MESH,
    )


def exchange(source, target, send_sems, recv_sems, own_sem):
    me, count = lax.axis_index("ctx"), lax.axis_size("ctx")

    def copy(there, slot):
        return remote(
            source.at[there], target.at[slot], send_sems.at[there], recv_sems.at[slot],
            {"ctx": there},
        )

    def send(there):
        @pl.when(there != me)
        def _():
            copy(there, me).start()

        @pl.when(there == me)
        def _():
            pltpu.make_async_copy(source.at[me], target.at[me], own_sem).start()

    def arrived(there):
        @pl.when(there != me)
        def _():
            copy(there, there).wait_recv()

        @pl.when(there == me)
        def _():
            pltpu.make_async_copy(source.at[me], target.at[me], own_sem).wait()

    def sent():
        for step in range(1, count):
            copy((me + step) % count, me).wait_send()

    return send, arrived, sent


def plane_gather(source, store, send, recv):
    me = lax.axis_index("ctx")
    chips = lax.axis_size("ctx") // 2
    last = chips - 1
    sibling = flipped_bits(me, 1)
    near = [flipped_bits(me, 2 * other) for other in range(1, chips)]
    relay = chips == 4
    height = store.shape[1]
    cut = height // 2 if height < 32 else height // 32 * 16

    def own(index, there, block):
        return remote(source, store.at[block], send.at[index], recv.at[index], {"ctx": there})

    def passed(index, block):
        return remote(
            store.at[block], store.at[block], send.at[chips + index], recv.at[chips + index],
            {"ctx": sibling},
        )

    def half(part, there, block):
        rows = pl.ds(0, cut) if part == 0 else pl.ds(cut, height - cut)
        at = 2 * chips - 1 + part
        return remote(
            store.at[block, rows], store.at[block, rows], send.at[at], recv.at[at], {"ctx": there}
        )

    firsts = range(2) if relay else range(last)

    def start():
        for index in firsts:
            own(index, near[index], me).start()
        own(last, sibling, me).start()

    def land(index):
        block = near[index]
        if relay and index == 2:
            half(0, near[0], block).wait_recv()
            half(1, near[1], block).wait_recv()
        else:
            own(index, block, block).wait_recv()
            if relay:
                half(1 - index, near[1 - index], block).start()
        passed(index, block).start()
        return block

    def rest(index):
        if index == 0:
            own(last, sibling, sibling).wait_recv()
            return sibling
        block = flipped_bits(near[index - 1], 1)
        passed(index - 1, block).wait_recv()
        return block

    def done():
        for index in firsts:
            own(index, near[index], me).wait_send()
        own(last, sibling, me).wait_send()
        for index in range(last):
            passed(index, near[index]).wait_send()
        if relay:
            half(0, near[0], near[1]).wait_send()
            half(1, near[1], near[0]).wait_send()

    return start, land, rest, done


def attend_forward_kernel(cross, heads, conts, offs_ref, q_ref, k_ref, v_ref, *refs):
    if cross:
        mixed_ref, att_ref, lse_ref, q_out, *refs = refs
    else:
        enc_ref, kv_ref, mixed_ref, att_ref, lse_ref, enc_all, kv_all, *refs = refs
    total, peak, value_t, score_a, score_b, stage, send_sem, recv_sem, own_sem, *refs = refs
    me, count = lax.axis_index("ctx"), lax.axis_size("ctx")
    rows = att_ref.shape[1]
    tiles = rows // TILE
    key_tiles = k_ref.shape[0] // TILE
    prompt = rows - conts * CONT
    prompt_tiles = prompt // TILE
    greet(others("ctx") + ([] if cross else others("fsdp")))
    send, arrived, sent = exchange(stage, mixed_ref, send_sem, recv_sem, own_sem)
    if not cross:
        gather_send, gather_recv, gather_own, kv_send, kv_recv = refs
        enc_start, enc_land, enc_rest, enc_done = plane_gather(
            enc_ref, enc_all, gather_send, gather_recv
        )
        enc_start()
        first = group_spread(kv_ref, kv_all, kv_send, kv_recv, 0)
        local = [
            pltpu.make_async_copy(enc_ref, enc_all.at[me], gather_own.at[0]),
            pltpu.make_async_copy(kv_ref, kv_all.at[lax.axis_index("fsdp")], gather_own.at[1]),
        ]
        for copy in first + local:
            copy.start()
    if cross:
        q_all, q_send, q_recv, q_own = refs
        put, got, put_done = exchange(q_ref, q_all, q_send, q_recv, q_own)
        for step in range(count):
            put((me + step) % count)

    for tile in range(key_tiles):
        at = pl.ds(tile * TILE, TILE)
        turned = transposed(v_ref[at, :])
        for head in range(heads):
            set_value_rows(value_t, head, at, turned)

    def query_tile(step, carry):
        if cross:
            i = (me + step) % count
            got(i)
            q = q_all[i]
            q_out[i] = q
        else:
            i = (me + 1 + step) % count
            q = q_ref[tile_rows(i), :]
        masked = [head_lanes(head, q) for head in range(heads)]
        total[...] = jnp.zeros_like(total)
        peak[...] = jnp.full_like(peak, NEG)

        def score(j, target):
            k = k_ref[tile_rows(j), :]
            for head in range(heads):
                target[head] = nt(k, masked[head])

        def soft(j, source, shown=None):
            for head in range(heads):
                scores = source[head]
                if shown is not None:
                    scores = jnp.where(shown, scores, NEG)
                soften(
                    scores, total.at[head], peak.at[head], value_t[head, :, tile_rows(j)]
                )

        if cross:
            both = (score_a, score_b)
            score(0, score_a)
            for j in range(key_tiles):
                if j + 1 < key_tiles:
                    score(j + 1, both[(j + 1) % 2])
                soft(j, both[j % 2])
        elif conts == 1:
            score(i, score_a)
            diagonal = visible(0, 0, TILE, TILE, 0, None)

            @pl.when(i > 0)
            def _():
                score(i - 1, score_b)
                soft(i, score_a, diagonal)

            @pl.when(i == 0)
            def _():
                soft(i, score_a, diagonal)

            def two(t, carry):
                j = i - 1 - 2 * t
                score(jnp.maximum(j - 1, 0), score_a)
                soft(j, score_b)
                score(jnp.maximum(j - 2, 0), score_b)
                soft(j - 1, score_a)
                return carry

            lax.fori_loop(0, i // 2, two, 0)

            @pl.when(i % 2 == 1)
            def _():
                soft(0, score_b)
        else:
            cont = jnp.maximum(i * TILE - prompt, 0) // CONT
            inside = i * TILE < prompt
            own = jnp.where(inside, 0, prompt + cont * CONT)
            limit = offs_ref[0, cont]

            def one(j, carry):
                score(j, score_a)
                soft(j, score_a, visible(j * TILE, i * TILE, TILE, TILE, own, limit))
                return carry

            lax.fori_loop(jnp.where(inside, 0, own // TILE), i + 1, one, 0)
            lax.fori_loop(0, jnp.where(inside, 0, prompt_tiles), one, 0)

        for head in range(heads):
            part = total[head]
            att_ref[64 * head : 64 * head + 64, tile_rows(i)] = part[:64] / part[64:65]
            lse_ref[head : head + 1, tile_rows(i)] = peak[head][:1] + jnp.log(part[64:65])
        stage[i] = att_ref[:, tile_rows(i)].T.astype(BF)
        send(i)
        if not cross:

            @pl.when(step == tiles - 3)
            def _():
                for index in range(min(2, count // 2 - 1)):
                    enc_land(index)

        return carry

    if heads < 2:
        att_ref[...] = jnp.zeros_like(att_ref)
    lax.fori_loop(0, tiles, query_tile, 0)
    for step in range(count):
        arrived((me + step) % count)
    sent()
    if cross:
        put_done()
    else:
        for index in range(2, count // 2 - 1):
            enc_land(index)
        for index in range(count // 2):
            enc_rest(index)
        for copy in first:
            copy.wait_send()
            copy.wait_recv()
        for copy in local:
            copy.wait()
        enc_done()


def group_spread(source, target, send_sem, recv_sem, sem):
    zone, groups = lax.axis_index("fsdp"), lax.axis_size("fsdp")
    return [
        remote(
            source, target.at[zone], send_sem.at[sem + shift - 1], recv_sem.at[sem + shift - 1],
            {"fsdp": (zone + shift) % groups},
        )
        for shift in range(1, groups)
    ]


def attend_forward(cross, heads, offsets, q, k, v, extra=()):
    count = lax.axis_size("ctx")
    rows = count * TILE
    vmem = pl.BlockSpec(memory_space=pltpu.VMEM)
    hbm = pl.BlockSpec(memory_space=pl.ANY)
    dma = pltpu.SemaphoreType.DMA
    tiles = jax.ShapeDtypeStruct((count, TILE, 128), BF)
    outs = [
        tiles,
        jax.ShapeDtypeStruct((128, rows), F32),
        jax.ShapeDtypeStruct((8, rows), F32),
    ]
    scratch = [
        pltpu.VMEM((heads, 80, TILE), F32),
        pltpu.VMEM((heads, 8, TILE), F32),
        pltpu.VMEM((heads, 80, k.shape[0]), BF),
        pltpu.VMEM((heads, TILE, TILE), F32),
        pltpu.VMEM((heads, TILE, TILE), F32),
        pltpu.VMEM((count, TILE, 128), BF),
        dma((count,)), dma((count,)), dma,
    ]
    if cross:
        outs.append(tiles)
        scratch += [pltpu.VMEM((count, TILE, 128), BF), dma((count,)), dma((count,)), dma]
        places = [vmem]
    else:
        enc, kv = extra
        groups = lax.axis_size("fsdp")
        outs.append(jax.ShapeDtypeStruct((count,) + enc.shape, BF))
        outs.append(jax.ShapeDtypeStruct((groups,) + kv.shape, BF))
        scratch += [dma((count + 1,)), dma((count + 1,)), dma((2,))]
        scratch += [dma((groups - 1,)), dma((groups - 1,))]
        places = [hbm, hbm]
    return pl.pallas_call(
        functools.partial(attend_forward_kernel, cross, heads, offsets.shape[1]),
        out_shape=outs,
        in_specs=[pl.BlockSpec(memory_space=pltpu.SMEM), vmem, vmem, vmem] + [hbm] * len(extra),
        out_specs=[hbm, vmem, vmem] + places,
        scratch_shapes=scratch,
        compiler_params=pltpu.CompilerParams(
            vmem_limit_bytes=VMEM_BYTES, collective_id=2 if cross else 1,
            has_side_effects=True,
        ),
        cost_estimate=pl.CostEstimate(
            flops=40 * 10**9, bytes_accessed=2**23, transcendentals=2**24
        ),
    )(offsets, q, k, v, *extra)


def rest_copies(sources, targets, send_sem, recv_sem):
    me = lax.axis_index("ctx")
    chips = lax.axis_size("ctx") // 2
    half = chips // 2
    out = []
    for other in range(1, half):
        for part in range(2):
            mine = me // 4 if part == 0 else (me // 2) % half
            sem = len(out)
            out.append(
                remote(
                    sources[part].at[:, :, flipped_bits(mine, other)],
                    targets[part].at[other - 1],
                    send_sem.at[sem], recv_sem.at[sem],
                    {"ctx": flipped_bits(me, (4 if part == 0 else 2) * other)},
                )
            )
    out = out + chip_copies(sources[2], targets[2], send_sem, recv_sem, len(out))
    return out + group_spread(sources[3], targets[3], send_sem, recv_sem, len(out))


def chip_copies(source, target, send_sem, recv_sem, sem):
    me = lax.axis_index("ctx")
    return [
        remote(
            source.at[flipped_bits(me // 2, other)], target.at[other - 1],
            send_sem.at[sem + other - 1], recv_sem.at[sem + other - 1],
            {"ctx": flipped_bits(me, 2 * other)},
        )
        for other in range(1, lax.axis_size("ctx") // 2)
    ]


def group_copies(source, target, send_sem, recv_sem, sem):
    zone, groups = lax.axis_index("fsdp"), lax.axis_size("fsdp")
    return [
        remote(
            source.at[(zone + shift) % groups], target.at[shift - 1],
            send_sem.at[sem + shift - 1], recv_sem.at[sem + shift - 1],
            {"fsdp": (zone + shift) % groups},
        )
        for shift in range(1, groups)
    ]


def last_copies(sources, targets, send_sem, recv_sem):
    out = chip_copies(sources[0], targets[0], send_sem, recv_sem, 0)
    for source, target in zip(sources[1:4], targets[1:4]):
        out = out + group_copies(source, target, send_sem, recv_sem, len(out))
    for source, target in zip(sources[4:], targets[4:]):
        sem = len(out)
        there = {"ctx": flipped_bits(lax.axis_index("ctx"), 1)}
        out.append(remote(source, target, send_sem.at[sem], recv_sem.at[sem], there))
    return out


def attend_backward_kernel(
    cross, heads, conts, scale, carried, number, offs_ref, q_ref, k_ref, v_ref, do_ref, att_ref,
    lse_ref, *refs,
):
    sources, refs = refs[:number], refs[number:]
    if not cross:
        normed_ref, *refs = refs
    if cross:
        moved_ref, dk_ref, dv_ref, *refs = refs
    else:
        moved_ref, stage, product_ref, column_ref, *refs = refs
    targets, refs = refs[:number], refs[number:]
    if cross:
        stage, *refs = refs
    (
        do_all, key_t, delta, dq_sum, dk_sum, dv_sum,
        send_sem, recv_sem, own_sem, do_send, do_recv, do_own, carry_send, carry_recv, *refs,
    ) = refs
    if cross:
        (keep_sem,) = refs
        keep_own = pltpu.make_async_copy(
            sources[3], targets[3].at[lax.axis_index("fsdp")], keep_sem
        )
    else:
        normed, normed_sem = refs
        product_ref[...] = jnp.zeros_like(product_ref)
        column_ref[...] = jnp.zeros_like(column_ref)
    me, count = lax.axis_index("ctx"), lax.axis_size("ctx")
    tiles = count
    key_tiles = k_ref.shape[0] // TILE
    prompt = tiles * TILE - conts * CONT
    greet(others("ctx") + others("fsdp"))
    put, got, put_done = exchange(do_ref, do_all, do_send, do_recv, do_own)
    for step in range(count):
        put((me + step) % count)
    carry_copies = carried(sources, targets, carry_send, carry_recv)
    for copy in carry_copies:
        copy.start()
    if cross:
        keep_own.start()
    send, arrived, sent = exchange(stage, moved_ref, send_sem, recv_sem, own_sem)
    dq_sum[...] = jnp.zeros_like(dq_sum)
    dk_sum[...] = jnp.zeros_like(dk_sum)
    dv_sum[...] = jnp.zeros_like(dv_sum)
    for tile in range(key_tiles):
        at = pl.ds(tile * TILE, TILE)
        key_t[:, at] = transposed(k_ref[at, :])

    def ready(i):
        got(i)
        both = do_all[i].astype(F32).T * att_ref[:, tile_rows(i)]
        for head in range(heads):
            delta[head : head + 1, tile_rows(i)] = jnp.sum(
                both[64 * head : 64 * head + 64], axis=0, keepdims=True
            )

    def pair(i, j, shown):
        row, at = tile_rows(i), tile_rows(j)
        q, do, k, v = q_ref[row, :], do_all[i], k_ref[at, :], v_ref[at, :]
        for head in range(heads):
            q_own, do_own = head_lanes(head, q), head_lanes(head, do)
            weights = jnp.exp(nt(k, q_own) - lse_ref[head : head + 1, row])
            if shown is not None:
                weights = jnp.where(shown, weights, 0.0)
            weight_grad = nt(v, do_own)
            score_grad = (weights * (weight_grad - delta[head : head + 1, row])).astype(BF)
            dv_sum[at, :] += nn(weights.astype(BF), do_own)
            dk_sum[at, :] += nn(score_grad, q_own)
            own = slice(64 * head, 64 * head + 64)
            dq_sum[own, row] += nn(key_t[own, at], score_grad)

    def shown_of(i, j):
        if conts == 1:
            return None
        cont = jnp.maximum(i * TILE - prompt, 0) // CONT
        own = jnp.where(i * TILE < prompt, 0, prompt + cont * CONT)
        return visible(j * TILE, i * TILE, TILE, TILE, own, offs_ref[0, cont])

    def queries_back(i):
        return (dq_sum[:, tile_rows(i)].T.astype(BF).astype(F32) * scale).astype(BF)

    def cross_tile(step, carry):
        i = (me + step) % count
        ready(i)

        def plain(j, carry):
            pair(i, j, None)
            return carry

        lax.fori_loop(0, key_tiles, plain, 0)
        stage[i] = queries_back(i)
        send(i)
        return carry

    def self_tile(step, carry):
        i = (me + 1 + step) % count
        fetch = pltpu.make_async_copy(normed_ref.at[i], normed, normed_sem)
        fetch.start()

        @pl.when(step == 0)
        def _():
            ready(i)

        pair(i, i, visible(0, 0, TILE, TILE, 0, None) if conts == 1 else shown_of(i, i))

        def other(turn, carry):
            p = (i + turn) % count

            @pl.when(step == 0)
            def _():
                ready(p)

            high, low = jnp.maximum(i, p), jnp.minimum(i, p)
            pair(high, low, shown_of(high, low))
            return carry

        lax.fori_loop(1, count - step, other, 0)
        stage[i, :, :128] = queries_back(i)
        stage[i, :, 128:256] = dk_sum[tile_rows(i), :].astype(BF)
        stage[i, :, 256:] = dv_sum[tile_rows(i), :].astype(BF)
        send(i)
        fetch.wait()
        grads = stage[i]
        product_ref[...] += tn(normed[...], grads)
        column_ref[...] += jnp.broadcast_to(
            jnp.sum(grads.astype(F32), axis=0, keepdims=True), column_ref.shape
        )
        return carry

    lax.fori_loop(0, tiles, cross_tile if cross else self_tile, 0)
    if cross:
        dk_ref[...] = dk_sum[...].astype(BF)
        dv_ref[...] = dv_sum[...].astype(BF)
    for step in range(count):
        arrived((me + step) % count)
    sent()
    put_done()
    if cross:
        keep_own.wait()
    for copy in carry_copies:
        copy.wait_send()
        copy.wait_recv()


def attend_backward(
    cross, heads, scale, offsets, q, k, v, do, att, lse, sources, target_shapes, normed=()
):
    count = lax.axis_size("ctx")
    vmem = pl.BlockSpec(memory_space=pltpu.VMEM)
    hbm = pl.BlockSpec(memory_space=pl.ANY)
    dma = pltpu.SemaphoreType.DMA
    keys = k.shape[0]
    wide = 128 if cross else 384
    moved = jax.ShapeDtypeStruct((count, TILE, wide), BF)
    if cross:
        local = [jax.ShapeDtypeStruct((keys, 128), BF)] * 2
        carries = 2 * (count // 4 - 1) + count // 2 - 1 + lax.axis_size("fsdp") - 1
    else:
        local = [
            jax.ShapeDtypeStruct((count, TILE, wide), BF),
            jax.ShapeDtypeStruct((normed[0].shape[2], wide), F32),
            jax.ShapeDtypeStruct((8, wide), F32),
        ]
        carries = count // 2 - 1 + (lax.axis_size("fsdp") - 1) * 3 + 2
    targets = [jax.ShapeDtypeStruct(shape, BF) for shape in target_shapes]
    return pl.pallas_call(
        functools.partial(
            attend_backward_kernel, cross, heads, offsets.shape[1], scale,
            rest_copies if cross else last_copies, len(sources),
        ),
        out_shape=[moved] + local + targets,
        in_specs=[pl.BlockSpec(memory_space=pltpu.SMEM)] + [vmem] * 6
        + [hbm] * (len(sources) + len(normed)),
        out_specs=[hbm] + [vmem] * len(local) + [hbm] * len(sources),
        scratch_shapes=([pltpu.VMEM((count, TILE, wide), BF)] if cross else [])
        + [
            pltpu.VMEM((count, TILE, 128), BF),
            pltpu.VMEM((128, keys), BF),
            pltpu.VMEM((8, count * TILE), F32),
            pltpu.VMEM((128, count * TILE), F32),
            pltpu.VMEM((keys, 128), F32),
            pltpu.VMEM((keys, 128), F32),
            dma((count,)), dma((count,)), dma,
            dma((count,)), dma((count,)), dma,
            dma((carries,)), dma((carries,)),
        ]
        + ([dma] if cross else [pltpu.VMEM(normed[0].shape[1:], BF), dma]),
        compiler_params=pltpu.CompilerParams(
            vmem_limit_bytes=VMEM_BYTES, collective_id=3 if cross else 4,
            has_side_effects=True,
        ),
        cost_estimate=pl.CostEstimate(
            flops=60 * 10**9, bytes_accessed=2**23, transcendentals=2**24
        ),
    )(offsets, q, k, v, do, att, lse, *sources, *normed)


def project_kernel(
    own, scale, tokens_ref, small_ref, head_ref, normed_ref, q_ref, k_ref, v_ref,
    small_all, head_all, all_tokens, staged, token_send, token_recv, part_send, part_recv,
    own_sem, stage_sem,
):
    me, zone = lax.axis_index("ctx"), lax.axis_index("fsdp")
    count, groups = lax.axis_size("ctx"), lax.axis_size("fsdp")
    chips = count // 2
    shard = small_ref.shape[1]
    sibling = {"ctx": flipped_bits(me, 1)}
    near = [flipped_bits(me, 2 * other) for other in range(1, chips)]
    greet([sibling] + [{"ctx": there} for there in near] + others("fsdp"))

    parts = []
    for shift in range(1, groups):
        there = {"fsdp": (zone + shift) % groups}
        for index, (source, target) in enumerate(((small_ref, small_all), (head_ref, head_all))):
            parts.append(
                remote(source, target.at[zone], part_send.at[index, shift - 1],
                       part_recv.at[index, shift - 1], there)
            )
    local = [
        pltpu.make_async_copy(small_ref, small_all.at[zone], own_sem.at[0]),
        pltpu.make_async_copy(head_ref, head_all.at[zone], own_sem.at[1]),
        pltpu.make_async_copy(tokens_ref, all_tokens.at[me], own_sem.at[2]),
    ]
    for copy in local:
        copy.start()
    for copy in parts:
        copy.start()

    start, land, rest, done = plane_gather(tokens_ref, all_tokens, token_send, token_recv)
    start()
    for copy in local:
        copy.wait()
    for copy in parts:
        copy.wait_recv()

    def row(index):
        pieces = [small_all[z].astype(F32)[index : index + 1] for z in range(groups)]
        return jnp.concatenate(pieces, axis=1)

    gain, shift = row(0), row(3)
    mine = small_all[me // (shard // own)].astype(F32)
    q_shift = jnp.where(me % 2 == 0, mine[6:7, :own], mine[6:7, own : 2 * own])
    v_shift = jnp.where(me % 2 == 0, mine[7:8, :own], mine[7:8, own : 2 * own])
    if own < 128:
        for ref in (q_ref, k_ref, v_ref):
            ref[...] = jnp.zeros_like(ref)

    def save(block, place):
        return pltpu.make_async_copy(staged.at[place], normed_ref.at[block], stage_sem.at[place])

    order, ready = [], []
    for step in range(count):
        place = step % 2
        if step == 0:
            ready.append(me)
        elif step == 1:
            ready.append(rest(0))
        elif step == 2:
            for index in range(min(2, chips - 1)):
                ready.append(land(index))
        elif len(ready) == step:
            index = step - chips - 1
            if step == 4 and chips == 4:
                ready += [rest(1), rest(2)]
            elif step == 6 and chips == 4:
                ready.append(land(2))
            elif chips == 4:
                ready.append(rest(3))
            else:
                ready.append(land(step - 2) if step <= chips else rest(index + 1))
        block = ready[step]
        order.append(block)
        if step >= 2:
            save(order[step - 2], place).wait()
        unit, _ = normalize(all_tokens[block].astype(F32))
        staged[place] = (unit * gain + shift).astype(BF)
        save(block, place).start()
        total = jnp.zeros((staged.shape[1], 3 * own), F32)
        for z in range(groups):
            total = total + nn(staged[place, :, z * shard : z * shard + shard], head_all[z])
        q_ref[block, :, :own] = (scale * (total[:, :own] + q_shift)).astype(BF)
        k_ref[block, :, :own] = total[:, own : 2 * own].astype(BF)
        v_ref[block, :, :own] = (total[:, 2 * own :] + v_shift).astype(BF)
    for step in (count - 2, count - 1):
        save(order[step], step % 2).wait()
    for copy in parts:
        copy.wait_send()
    done()


def project(own, scale, tokens, small, head_in):
    count, groups = lax.axis_size("ctx"), lax.axis_size("fsdp")
    rows, width = tokens.shape
    vmem = pl.BlockSpec(memory_space=pltpu.VMEM)
    hbm = pl.BlockSpec(memory_space=pl.ANY)
    dma = pltpu.SemaphoreType.DMA
    lanes = jax.ShapeDtypeStruct((count, rows, 128), BF)
    return pl.pallas_call(
        functools.partial(project_kernel, own, scale),
        out_shape=(
            jax.ShapeDtypeStruct((count, rows, width), BF),
            lanes, lanes, lanes,
            jax.ShapeDtypeStruct((groups,) + small.shape, BF),
            jax.ShapeDtypeStruct((groups,) + head_in.shape, BF),
        ),
        in_specs=[hbm, hbm, hbm],
        out_specs=(hbm,) + (vmem,) * 5,
        scratch_shapes=[
            pltpu.VMEM((count, rows, width), BF),
            pltpu.VMEM((2, rows, width), BF),
            dma((count + 1,)), dma((count + 1,)),
            dma((2, groups - 1)), dma((2, groups - 1)),
            dma((3,)), dma((2,)),
        ],
        compiler_params=pltpu.CompilerParams(
            vmem_limit_bytes=VMEM_BYTES, collective_id=5, has_side_effects=True
        ),
        cost_estimate=pl.CostEstimate(
            flops=50 * 10**9, bytes_accessed=2**25, transcendentals=0
        ),
    )(tokens, small, head_in)


def ffn_kernel(
    steps, groups, n_ref, dy_ref, base_ref, bias_ref, win_ref, wout_ref, rows_ref,
    out_ref, gn_ref, gb_ref, in_ref, sum_ref, rows_all,
    n_t, own_in, own_out, post_in, post_out, got_in, got_out,
    keep_in, keep_out, flow_in, flow_out, near_in, near_out,
    send_sem, recv_sem, flow_send, flow_recv, save_sem, rows_send, rows_recv, rows_own,
):
    f = pl.program_id(0)
    spread = group_spread(rows_ref, rows_all, rows_send, rows_recv, 0)
    keep_rows = pltpu.make_async_copy(
        rows_ref, rows_all.at[lax.axis_index("fsdp")], rows_own
    )
    me = lax.axis_index("ctx")
    count = lax.axis_size("ctx")
    chips = count // 2
    core = me % 2
    low_bit = (me // 2) % 2
    high_bit = me // chips
    cols = keep_in.shape[2]
    slot = f % 2
    sibling = {"ctx": flipped_bits(me, 1)}
    low = {"ctx": flipped_bits(me, 2)}
    high = {"ctx": flipped_bits(me, chips)}

    def copies(step, place):
        return (
            remote(post_in.at[place], got_in.at[step], send_sem.at[0, place],
                   recv_sem.at[0, step], sibling),
            remote(post_out.at[place], got_out.at[step], send_sem.at[1, place],
                   recv_sem.at[1, step], sibling),
        )

    def flows(step, place):
        return (
            remote(flow_in.at[place], near_in.at[step], flow_send.at[0, place],
                   flow_recv.at[0, step], low),
            remote(flow_out.at[place], near_out.at[step], flow_send.at[1, place],
                   flow_recv.at[1, step], high),
        )

    @pl.when(f == 0)
    def _():
        greet([sibling, low, high] + others("fsdp"))
        for copy in spread:
            copy.start()
        keep_rows.start()
        n_t[...] = transposed(n_ref[...])
        gn_ref[...] = jnp.zeros_like(gn_ref)
        out_ref[...] = base_ref[...]

    @pl.when(f < steps)
    def _():
        @pl.when(f >= 2)
        def _():
            for copy in copies(jnp.maximum(f - 2, 0), slot):
                copy.wait_send()

        pre = nn(n_ref[...], win_ref[...]) + bias_ref[0, :1]
        below = 0.5 * (1.0 + lax.erf(pre * (1.0 / math.sqrt(2.0))))
        hidden = (pre * below).astype(BF)
        out_ref[...] += nn(hidden, wout_ref[...])
        slope = below + pre * (jnp.exp(-0.5 * pre * pre) * (1.0 / math.sqrt(2.0 * math.pi)))
        dy = dy_ref[...]
        grad_pre = (nt(dy, wout_ref[...]) * slope).astype(BF)
        gb_ref[0] = jnp.broadcast_to(
            jnp.sum(grad_pre.astype(F32), axis=0, keepdims=True), gb_ref.shape[1:]
        )
        gn_ref[...] += nt(grad_pre, win_ref[...])

        def split(part, keep, post, half):
            left, right = part[:, :half], part[:, half:]
            keep[slot] = jnp.where(core == 0, left, right)
            post[slot] = jnp.where(core == 0, right, left).astype(BF)

        first, second = copies(jnp.minimum(f, steps - 1), slot)
        split(nn(n_t[...], grad_pre), own_in, post_in, cols)
        first.start()
        split(tn(hidden, dy), own_out, post_out, 2 * cols)
        second.start()

    @pl.when(f > 0)
    def _():
        past = jnp.maximum(f - 1, 0)
        place = (f + 1) % 2
        for copy in copies(past, place):
            copy.wait_recv()

        @pl.when(f >= 3)
        def _():
            for copy in flows(jnp.maximum(f - 3, 0), place):
                copy.wait_send()

        unit = keep_in.shape[1] // (groups * (chips // 2))
        for slab in range(groups * (chips // 2)):
            for kept in (True, False):
                take = low_bit if kept else 1 - low_bit
                rows = pl.ds(pl.multiple_of((2 * slab + take) * unit, unit), unit)
                both = own_in[place, rows, :] + got_in[past, rows, :].astype(F32)
                at = slice(unit * slab, unit * slab + unit)
                if kept:
                    keep_in[past, at, :] = both.astype(BF)
                else:
                    flow_in[place, at, :] = both.astype(BF)
        unit = n_t.shape[0] // groups // 2
        for slab in range(own_out.shape[1] // (2 * unit)):
            for kept in (True, False):
                take = high_bit if kept else 1 - high_bit
                rows = pl.ds(pl.multiple_of((2 * slab + take) * unit, unit), unit)
                both = own_out[place, rows, :] + got_out[past, rows, :].astype(F32)
                at = slice(unit * slab, unit * slab + unit)
                for half in range(2):
                    value = both[:, half * cols : half * cols + cols].astype(BF)
                    if kept:
                        keep_out[past, half, at, :] = value
                    else:
                        flow_out[place, half, at, :] = value
        for copy in flows(past, place):
            copy.start()

    @pl.when(f == steps)
    def _():
        for back in (2, 1):
            for copy in copies(steps - back, (steps - back) % 2):
                copy.wait_send()
            for copy in flows(steps - back, (steps - back) % 2):
                copy.wait_send()
        per = steps // sum_ref.shape[0]
        height = keep_out.shape[2]

        def saves(step):
            rows = pl.ds(pl.multiple_of((step % per) * height, height), height)
            return (
                pltpu.make_async_copy(
                    keep_in.at[step], in_ref.at[step], save_sem.at[0, step]
                ),
                pltpu.make_async_copy(
                    keep_out.at[step], sum_ref.at[step // per, :, rows], save_sem.at[1, step]
                ),
            )

        def join(step, carry):
            for copy in flows(step, step % 2):
                copy.wait_recv()
            keep_in[step] = (
                keep_in[step].astype(F32) + near_in[step].astype(F32)
            ).astype(BF)
            keep_out[step] = (
                keep_out[step].astype(F32) + near_out[step].astype(F32)
            ).astype(BF)
            for copy in saves(step):
                copy.start()
            return carry

        def saved(step, carry):
            for copy in saves(step):
                copy.wait()
            return carry

        lax.fori_loop(0, steps, join, 0)
        lax.fori_loop(0, steps, saved, 0)
        keep_rows.wait()
        for copy in spread:
            copy.wait_send()
            copy.wait_recv()


def ffn(normed, dy, base, bias, weights, rows_part):
    rows, width = normed.shape
    hidden = weights.shape[1] // 2
    groups = lax.axis_size("fsdp")
    step = 512
    cols = step // 2
    steps = hidden // step
    per = width // step
    last = steps - 1

    def now(f):
        return jnp.minimum(f, last)

    whole = lambda f: (0, 0)
    hbm = pl.BlockSpec(memory_space=pl.ANY)
    dma = pltpu.SemaphoreType.DMA
    once = pl.BlockSpec((rows, width), whole, pipeline_mode=pl.Buffered(1))
    return pl.pallas_call(
        functools.partial(ffn_kernel, steps, groups),
        grid=(steps + 1,),
        out_shape=(
            jax.ShapeDtypeStruct((rows, width), F32),
            jax.ShapeDtypeStruct((rows, width), F32),
            jax.ShapeDtypeStruct((steps, 8, step), F32),
            jax.ShapeDtypeStruct((steps, width // 2, cols), BF),
            jax.ShapeDtypeStruct((hidden // width, 2, width // 2, cols), BF),
            jax.ShapeDtypeStruct((groups,) + rows_part.shape, BF),
        ),
        in_specs=[
            once, once, once,
            pl.BlockSpec((1, 8, step), lambda f: (now(f), 0, 0)),
            pl.BlockSpec((width, step), lambda f: (0, now(f))),
            pl.BlockSpec(
                (step, width), lambda f: (now(f) % per, hidden // width + now(f) // per)
            ),
            hbm,
        ],
        out_specs=(
            pl.BlockSpec((rows, width), whole),
            pl.BlockSpec((rows, width), whole),
            pl.BlockSpec((1, 8, step), lambda f: (now(f), 0, 0)),
            hbm, hbm, hbm,
        ),
        scratch_shapes=[
            pltpu.VMEM((width, rows), BF),
            pltpu.VMEM((2, width, cols), F32),
            pltpu.VMEM((2, step, 2 * cols), F32),
            pltpu.VMEM((2, width, cols), BF),
            pltpu.VMEM((2, step, 2 * cols), BF),
            pltpu.VMEM((steps, width, cols), BF),
            pltpu.VMEM((steps, step, 2 * cols), BF),
            pltpu.VMEM((steps, width // 2, cols), BF),
            pltpu.VMEM((steps, 2, step // 2, cols), BF),
            pltpu.VMEM((2, width // 2, cols), BF),
            pltpu.VMEM((2, 2, step // 2, cols), BF),
            pltpu.VMEM((steps, width // 2, cols), BF),
            pltpu.VMEM((steps, 2, step // 2, cols), BF),
            dma((2, 2)), dma((2, steps)), dma((2, 2)), dma((2, steps)), dma((2, steps)),
            dma((groups - 1,)), dma((groups - 1,)), dma,
        ],
        compiler_params=pltpu.CompilerParams(
            vmem_limit_bytes=60 * 2**20, collective_id=0, has_side_effects=True
        ),
        cost_estimate=pl.CostEstimate(
            flops=30 * 10**9, bytes_accessed=2**26, transcendentals=2**22
        ),
    )(normed, dy, base, bias, weights, weights, rows_part)


def finish_kernel(more, late_ref, done_ref, ffn_ref, *refs):
    if more:
        moved_ref, enc_ref, self_mine, self_other, kv_mine, kv_other, *refs = refs
    all_ffn, all_done, all_late, *refs = refs
    if more:
        token_ref, enc_grad_ref, *refs = refs
    late_own, got, send_sem, recv_sem, zone_send, zone_recv, own_sem, *refs = refs
    me, zone = lax.axis_index("ctx"), lax.axis_index("fsdp")
    count, groups = lax.axis_size("ctx"), lax.axis_size("fsdp")
    chips = count // 2
    greet(others("ctx") + others("fsdp"))
    zones = group_copies(late_ref, got, zone_send, zone_recv, 0)
    for copy in zones:
        copy.start()
    if more:
        all_moved, weights, all_enc, enc_send, enc_recv, enc_own, moved_sem, weight_sem = refs
        put, arrived, put_done = exchange(enc_ref, all_enc, enc_send, enc_recv, enc_own)
        for step in range(count):
            put((me + step) % count)
        fetch_moved = pltpu.make_async_copy(moved_ref, all_moved, moved_sem)
        fetch_moved.start()
    gathers = [
        plane_gather(source, store, send_sem.at[kind], recv_sem.at[kind])
        for kind, (source, store) in enumerate(
            ((ffn_ref, all_ffn), (done_ref, all_done), (late_own, all_late))
        )
    ]
    local = [
        pltpu.make_async_copy(source, store.at[me], own_sem.at[kind])
        for kind, (source, store) in enumerate(
            ((ffn_ref, all_ffn), (done_ref, all_done), (late_own, all_late))
        )
    ]
    for kind in range(2):
        gathers[kind][0]()
        local[kind].start()
    if more:
        width = token_ref.shape[1]
        core = me % 2

        def fetch(step):
            source = (me + step) % count
            out = []
            for k in range(5):
                at = (k if k < 3 else k - 3) * width + source * 128
                columns = pl.ds(pl.multiple_of(at, 128), 128)
                pair = (self_mine, self_other) if k < 3 else (kv_mine, kv_other)
                for index, array in enumerate(pair):
                    side = core if index == 0 else 1 - core
                    out.append(
                        pltpu.make_async_copy(
                            array.at[:, :, columns], weights.at[step % 2, k, :, side],
                            weight_sem.at[step % 2, k, index],
                        )
                    )
            return out

        for copy in fetch(0):
            copy.start()
        token_ref[...] = jnp.zeros_like(token_ref)
        enc_grad_ref[...] = jnp.zeros_like(enc_grad_ref)
        fetch_moved.wait()

        def one_source(step, carry):
            source = (me + step) % count

            @pl.when(step + 1 < count)
            def _():
                for copy in fetch(step + 1):
                    copy.start()

            for copy in fetch(step):
                copy.wait()
            grads = all_moved[source]

            def part(index):
                return weights[step % 2, index].reshape(width, 128)

            token_ref[...] += (
                nt(grads[:, :128], part(0))
                + nt(grads[:, 128:256], part(1))
                + nt(grads[:, 256:], part(2))
            )
            arrived(source)
            rows = all_enc[source]
            enc_grad_ref[...] += nt(rows[:, :128], part(3)) + nt(rows[:, 128:], part(4))
            return carry

        lax.fori_loop(0, count, one_source, 0)
    total = late_ref[zone].astype(F32)
    for shift in range(groups - 1):
        zones[shift].wait_recv()
        total = total + got[shift].astype(F32)
    late_own[...] = total.astype(BF)
    gathers[2][0]()
    local[2].start()
    for index in range(chips - 1):
        for gather in gathers:
            gather[1](index)
    for index in range(chips):
        for gather in gathers:
            gather[2](index)
    for copy in local:
        copy.wait()
    for gather in gathers:
        gather[3]()
    for copy in zones:
        copy.wait_send()
    if more:
        put_done()


def finish(late, done, ffn_sums, width, more=()):
    count, groups = lax.axis_size("ctx"), lax.axis_size("fsdp")
    vmem = pl.BlockSpec(memory_space=pltpu.VMEM)
    hbm = pl.BlockSpec(memory_space=pl.ANY)
    dma = pltpu.SemaphoreType.DMA
    outs = [
        jax.ShapeDtypeStruct((count,) + shape, BF)
        for shape in (ffn_sums.shape, done.shape, late.shape[1:])
    ]
    places = [hbm] * 3
    scratch = [
        pltpu.VMEM(late.shape[1:], BF),
        pltpu.VMEM((groups - 1,) + late.shape[1:], BF),
        dma((3, count + 1)), dma((3, count + 1)),
        dma((groups - 1,)), dma((groups - 1,)), dma((3,)),
    ]
    if more:
        moved, enc, weights = more[:3]
        outs.append(jax.ShapeDtypeStruct((moved.shape[1], width), F32))
        outs.append(jax.ShapeDtypeStruct((enc.shape[1], width), F32))
        places += [vmem, vmem]
        scratch += [
            pltpu.VMEM(moved.shape, BF),
            pltpu.VMEM((2, 5, groups, 2, weights.shape[1], 128), BF),
            pltpu.VMEM(enc.shape, BF),
            dma((count,)), dma((count,)), dma, dma, dma((2, 5, 2)),
        ]
    return pl.pallas_call(
        functools.partial(finish_kernel, bool(more)),
        out_shape=outs,
        in_specs=[vmem] + [hbm] * (2 + len(more)),
        out_specs=places,
        scratch_shapes=scratch,
        compiler_params=pltpu.CompilerParams(
            vmem_limit_bytes=VMEM_BYTES, collective_id=6, has_side_effects=True
        ),
        cost_estimate=pl.CostEstimate(
            flops=50 * 10**9, bytes_accessed=2**25, transcendentals=0
        ),
    )(late, done, ffn_sums, *more)


def place_kernel(groups, more, ffn_ref, self_refs, kv_refs, mixed_refs, out_refs, extra):
    in_ref, out_ref, self_ref, kv_ref, *weight_refs = out_refs
    cols = ffn_ref.shape[3]
    steps = ffn_ref.shape[1] // 2
    hidden = in_ref.shape[1]
    blocks = out_ref.shape[0]
    width = out_ref.shape[3]
    depth = width // groups
    per = steps // blocks
    span = min(depth, cols)
    for core in range(2):
        for f in range(steps):
            value = ffn_ref[core, f].astype(F32)
            for piece in range(cols // span):
                unit = (f % per) * 2 * cols + core * cols + piece * span
                at = (unit // depth * blocks + f // per) * depth + unit % depth
                in_ref[:, at : at + span] = value[:, piece * span : piece * span + span]
        for slab in range(steps):
            at = (core * 2 + slab % 2) * cols
            out_ref[slab // 2, 0, :, at : at + cols] = ffn_ref[core, steps + slab].astype(F32)
    for refs, target in ((self_refs, self_ref), (kv_refs, kv_ref)):
        for k, ref in enumerate(refs):
            own = ref.shape[2]
            for source in range(ref.shape[0]):
                at = k * width + source * own
                target[:, at : at + own] = ref[source].astype(F32)
    part = in_ref.shape[0]
    for (ref, count), targets in zip(mixed_refs, (weight_refs[:1], weight_refs[1:])):
        own = ref.shape[2]
        for w, target in enumerate(targets):
            for core in range(2):
                for index in range(count):
                    top = (w * count + index) * part
                    at = core * (width // 2) + index * own
                    target[:, at : at + own] = ref[core, top : top + part, :].astype(F32)
    if more:
        total_ref, tokens_ref, gain_ref, base_ref, enc_ref, token_ref, enc_out = extra
        unit, scale = normalize(tokens_ref[...].astype(F32))
        token_ref[...] = (
            base_ref[...] + normalize_back(unit, scale, gain_ref[...], total_ref[...])[0]
        )
        enc_out[...] = enc_ref[...]


def place(ffn_sums, done, late, hidden, width, more=()):
    count, groups = lax.axis_size("ctx"), lax.axis_size("fsdp")
    chips, own = count // 2, late.shape[2]
    depth = width // groups
    part = depth // chips
    blocks = hidden // width
    wide = width // 2 // own

    def lane_blocks(start, k):
        return pl.BlockSpec((count, part, own), lambda c: (0, (start + k * depth) // part + c, 0))

    in_specs = [pl.BlockSpec((2,) + ffn_sums.shape[1:], lambda c: (c, 0, 0, 0))]
    in_specs += [lane_blocks(2 * wide * part, k) for k in range(3)]
    in_specs += [lane_blocks(wide * part, k) for k in range(2)]
    in_specs += [
        pl.BlockSpec((2, wide * part, own), lambda c: (c, 0, 0)),
        pl.BlockSpec((2, 2 * wide * part, own), lambda c: (c, 0, 0)),
    ]
    row = lambda n: pl.BlockSpec((part, n), lambda c: (c, 0))
    out_specs = [
        row(hidden), pl.BlockSpec((blocks, 1, part, width), lambda c: (0, c, 0, 0)),
        row(3 * width), row(2 * width), row(width), row(width), row(width),
    ]
    out_shape = [
        jax.ShapeDtypeStruct((depth, hidden), F32),
        jax.ShapeDtypeStruct((blocks, chips, part, width), F32),
        jax.ShapeDtypeStruct((depth, 3 * width), F32),
        jax.ShapeDtypeStruct((depth, 2 * width), F32),
    ] + [jax.ShapeDtypeStruct((depth, width), F32)] * 3
    if more:
        total, _, _, _, enc = more
        tall, short = total.shape[0] // chips, enc.shape[0] // chips
        tokens_rows = pl.BlockSpec((tall, width), lambda c: (c, 0))
        enc_rows = pl.BlockSpec((short, width), lambda c: (c, 0))
        in_specs += [
            tokens_rows, tokens_rows, pl.BlockSpec((1, width), lambda c: (0, 0)), tokens_rows,
            enc_rows,
        ]
        out_specs += [tokens_rows, enc_rows]
        out_shape += [
            jax.ShapeDtypeStruct(total.shape, F32), jax.ShapeDtypeStruct(enc.shape, F32)
        ]

    def kernel(*refs):
        ffn_ref, refs = refs[0], refs[1:]
        self_refs, kv_refs, mixed, refs = refs[:3], refs[3:5], refs[5:7], refs[7:]
        extra_in, refs = refs[: len(more)], refs[len(more) :]
        place_kernel(
            groups, bool(more), ffn_ref, self_refs, kv_refs,
            ((mixed[0], wide), (mixed[1], wide)), refs[:7], extra_in + refs[7:],
        )

    return pl.pallas_call(
        kernel,
        grid=(chips,),
        out_shape=out_shape,
        in_specs=in_specs,
        out_specs=out_specs,
        compiler_params=pltpu.CompilerParams(vmem_limit_bytes=VMEM_BYTES),
        cost_estimate=pl.CostEstimate(flops=0, bytes_accessed=2**25, transcendentals=0),
    )(ffn_sums, late, late, late, done, done, done, late, *more)


def swap(value, bit):
    count = lax.axis_size("ctx")
    return lax.ppermute(value, "ctx", [(i, i ^ bit) for i in range(count)])


def pair_product(left, right):
    core = lax.axis_index("ctx") % 2
    half = right.shape[1] // 2
    send = tn(left, lax.dynamic_slice_in_dim(right, (1 - core) * half, half, 1)).astype(BF)
    got = swap(send, 1).astype(F32)
    kept = tn(left, lax.dynamic_slice_in_dim(right, core * half, half, 1))
    return (kept + got).astype(BF)


def gather_joined(pieces):
    count = lax.axis_size("ctx")
    me = lax.axis_index("ctx")
    rows = pieces[0].shape[0] // count
    cut = [lax.dynamic_slice_in_dim(p, me * rows, rows, 0) for p in pieces]
    joined = jnp.concatenate(cut, axis=1)
    return lax.all_gather(joined, ("fsdp", "ctx"), axis=0, tiled=True)


def gather_all(pieces):
    full = gather_joined(pieces)
    out, at = [], 0
    for p in pieces:
        out.append(full[:, at : at + p.shape[1]])
        at += p.shape[1]
    return out


def gather_ffn(ffn_in, ffn_out):
    count = lax.axis_size("ctx")
    groups = lax.axis_size("fsdp")
    me = lax.axis_index("ctx")
    depth, hidden = ffn_in.shape
    width = ffn_out.shape[1]
    blocks = hidden // width
    rows = depth // count
    left = lax.dynamic_slice_in_dim(ffn_in, me * rows, rows, 0)
    left = left.reshape(rows, groups, blocks, depth)
    left = jnp.transpose(left, (0, 2, 1, 3)).reshape(rows, hidden)
    right = lax.dynamic_index_in_dim(
        ffn_out.reshape(blocks, count, rows, width), me, 1, keepdims=False
    )
    right = jnp.moveaxis(right, 0, 1).reshape(rows, hidden)
    joined = jnp.concatenate([left, right], axis=1)
    return lax.all_gather(joined, ("fsdp", "ctx"), axis=0, tiled=True)


def body(
    tokens, encoder_out, prompt_offsets, gains, shifts, self_in, self_out, cross_q, cross_kv,
    cross_out, ffn_in, ffn_bias, ffn_out, out_bias, cotangent,
):
    row_count, width = tokens.shape
    head_dim = width // HEADS
    scale = 1.0 / math.sqrt(head_dim)
    ctx = lax.axis_size("ctx")
    groups = lax.axis_size("fsdp")
    me = lax.axis_index("ctx")
    heads = HEADS // ctx
    own = heads * head_dim

    shard = gains.shape[1]
    small = jnp.concatenate(
        [gains, shifts, out_bias[None], ffn_bias.reshape(-1, shard)], axis=0
    )
    small_rows = small.shape[0]
    small = jnp.pad(small, ((0, 32 - small_rows), (0, 0)))

    head_in = lax.dynamic_index_in_dim(
        self_in.reshape(self_in.shape[0], 3, ctx, own), me, 2, keepdims=False
    ).reshape(-1, 3 * own)
    all_normed, queries, keys, values, small, head_in = project(
        own, scale, tokens, small, head_in
    )
    all_normed = all_normed.reshape(-1, width)
    queries, keys, values = [x.reshape(-1, 128) for x in (queries, keys, values)]
    small = small[:, :small_rows].astype(F32)
    vectors = jnp.moveaxis(small[:, :13], 0, 1).reshape(13, width)
    gain, shift, full_out_bias = vectors[:3], vectors[3:12], vectors[12]
    full_ffn_bias = small[:, 13:].reshape(-1)

    full_self_out, full_cross_q, full_cross_out = gather_all([self_out, cross_q, cross_out])
    ffn_weights = gather_ffn(ffn_in, ffn_out)
    def lanes(value):
        gap = [(0, 0)] * (value.ndim - 1) + [(0, 128 - own)]
        return value if own == 128 else jnp.pad(value, gap)

    head_kv = lax.dynamic_index_in_dim(
        cross_kv.reshape(-1, 2, ctx, own), me, 2, keepdims=False
    ).reshape(-1, 2 * own)
    mixed_heads, att_self, lse_self, all_encoder, head_kv = attend_forward(
        False, heads, prompt_offsets, queries, keys, values, (encoder_out, head_kv)
    )
    all_encoder = all_encoder.reshape(-1, width)
    head_kv = head_kv.reshape(width, 2 * own)

    def to_rows(value):
        return jnp.moveaxis(value[:, :, :own], 0, 1).reshape(row_count, width)

    def to_heads(value):
        return lanes(jnp.moveaxis(value.reshape(row_count, ctx, own), 1, 0))

    mixed = to_rows(mixed_heads)
    token_values = tokens.astype(F32)
    first = token_values + nn(mixed, full_self_out) + shift[5]
    unit_two, scale_two = normalize(first)
    normed_two = (unit_two * gain[1] + shift[1]).astype(BF)
    cross_queries = (scale * (nn(normed_two, full_cross_q) + shift[6])).astype(BF)
    enc_shift = lax.dynamic_slice_in_dim(shift[7], me * own, own, 0)
    enc_projected = nn(all_encoder, head_kv)
    enc_keys = lanes(enc_projected[:, :own].astype(BF))
    enc_values = lanes((enc_projected[:, own:] + enc_shift).astype(BF))
    cross_heads, att_cross, lse_cross, all_cross_q = attend_forward(
        True, heads, prompt_offsets, to_heads(cross_queries), enc_keys, enc_values
    )
    cross_mixed = to_rows(cross_heads)
    second = first + nn(cross_mixed, full_cross_out) + shift[8]
    unit_three, scale_three = normalize(second)
    normed_three = (unit_three * gain[2] + shift[2]).astype(BF)
    depth = ffn_in.shape[0]
    blocks = ffn_in.shape[1] // width
    order = full_ffn_bias.reshape(groups, blocks, depth)
    order = jnp.moveaxis(order, 0, 1).reshape(-1, 1, 512)
    half_rows = depth // 2
    core = me % 2
    self_rows = lax.dynamic_slice_in_dim(self_in, core * half_rows, half_rows, 0)
    kv_rows = lax.dynamic_slice_in_dim(cross_kv, core * half_rows, half_rows, 0)
    layer_sum, grad_three, bias_parts, in_sum, out_sum, kv_mine = ffn(
        normed_three, cotangent, second + full_out_bias,
        jnp.broadcast_to(order, (order.shape[0], 8, 512)), ffn_weights, kv_rows,
    )
    layer_out = layer_sum.astype(BF)
    chips = ctx // 2
    part = depth // chips
    in_sum = in_sum.reshape(-1, groups, chips // 2, part, 256)
    out_sum = out_sum.reshape(-1, groups, chips // 2, part, 256)

    dy = cotangent.astype(F32)
    back_three = normalize_back(unit_three, scale_three, gain[2], grad_three)
    grad_second = dy + back_three[0]
    branch_two = grad_second.astype(BF)
    chip_first = lambda value: jnp.moveaxis(value.reshape(groups, chips, part, -1), 1, 0)
    cross_part = chip_first(pair_product(cross_mixed, branch_two))
    grad_cross_mixed = nt(branch_two, full_cross_out).astype(BF)
    got_shape = (max(chips // 2 - 1, 1),) + in_sum.shape[:2] + in_sum.shape[3:]
    cross_moved, cross_dk, cross_dv, in_got, out_got, cross_got, self_mine = attend_backward(
        True, heads, scale, prompt_offsets, all_cross_q.reshape(-1, 128), enc_keys, enc_values,
        to_heads(grad_cross_mixed), att_cross, lse_cross,
        (in_sum, out_sum, cross_part, self_rows),
        (got_shape, got_shape, (chips - 1,) + cross_part.shape[1:], (groups,) + self_rows.shape),
    )

    def joined(value, mine, dim, got):
        kept = lax.dynamic_index_in_dim(value, mine, dim, keepdims=False).astype(F32)
        return kept + jnp.sum(got.astype(F32), axis=0)

    cross_dq = to_rows(cross_moved)
    back_two = normalize_back(unit_two, scale_two, gain[1], nt(cross_dq, full_cross_q))
    grad_first = grad_second + back_two[0]
    branch_one = grad_first.astype(BF)
    grad_mixed = nt(branch_one, full_self_out).astype(BF)
    middle = jnp.stack(
        [
            chip_first(pair_product(normed_two, cross_dq)),
            chip_first(pair_product(mixed, branch_one)),
        ],
        axis=1,
    )
    cross_part = joined(cross_part, me // 2, 0, cross_got).astype(BF)
    enc_heads = jnp.concatenate([cross_dk[:, :own], cross_dv[:, :own]], axis=1)
    kv_part = tn(all_encoder, enc_heads).astype(BF).reshape(groups, depth, 2 * own)
    ffn_sums = jnp.concatenate(
        [
            joined(in_sum, me // 4, 2, in_got),
            joined(out_sum, (me // 2) % (chips // 2), 2, out_got),
        ],
        axis=0,
    )
    ffn_sums = jnp.moveaxis(ffn_sums.astype(BF), 1, 0)
    carried = (middle, ffn_sums, cross_part, kv_part, self_mine, kv_mine)
    moved, _, grad_head_in, column, *got = attend_backward(
        False, heads, scale, prompt_offsets, queries, keys, values, to_heads(grad_mixed),
        att_self, lse_self, carried,
        [(value.shape[0] - 1,) + value.shape[1:] for value in carried[:4]]
        + [value.shape for value in carried[4:]],
        (all_normed.reshape(ctx, row_count, width),),
    )
    grad_head_in = grad_head_in.reshape(width, 3, 128)[:, :, :own].reshape(width, 3 * own)
    column = column[0].reshape(3, 128)[:, :own].reshape(-1)
    zone = lax.axis_index("fsdp")
    middle = joined(middle, me // 2, 0, got[0]).astype(BF)
    ffn_sums, cross_part, kv_part = [
        joined(value, zone, 0, part_got).astype(BF)
        for value, part_got in zip(carried[1:4], got[1:4])
    ]
    self_other, kv_other = got[4:]
    weight = head_in.reshape(width, 3 * own).astype(F32)
    grad_shift_one = jnp.sum(weight * column, axis=1)
    grad_gain_one = jnp.sum(weight * (grad_head_in - shift[0][:, None] * column), axis=1) / gain[0]

    def spread(value):
        return lax.dynamic_update_slice_in_dim(jnp.zeros((width,), F32), value, me * own, 0)

    totals = jnp.stack(
        [
            grad_gain_one, back_two[1], back_three[1],
            grad_shift_one, back_two[2], back_three[2],
            spread(column[:own]), spread(column[2 * own :]),
            jnp.sum(branch_one.astype(F32), axis=0),
            jnp.sum(cross_dq.astype(F32), axis=0),
            spread(jnp.sum(enc_heads[:, own:].astype(F32), axis=0)),
            jnp.sum(branch_two.astype(F32), axis=0),
            jnp.sum(dy, axis=0),
        ]
    )
    totals = jnp.moveaxis(totals.reshape(13, groups, shard), 1, 0).reshape(groups, -1)
    bias = jnp.moveaxis(bias_parts[:, 0].reshape(blocks, groups, depth), 0, 1)
    totals = jnp.concatenate([totals, bias.reshape(groups, -1)], axis=1)
    count = totals.shape[1]
    totals = jnp.pad(totals, ((0, 0), (0, 48 * own - count))).reshape(groups, 48, own)

    def by_lanes(value, rows):
        lead = value.shape[:-2]
        value = jnp.moveaxis(value.reshape(lead + (rows, -1, own)), -2, -3)
        return value.reshape(lead + (-1, own))

    middle = jnp.moveaxis(by_lanes(middle, part), 1, 0).reshape(groups, -1, own)
    late = by_lanes(grad_head_in.reshape(groups, depth, 3 * own), depth)
    late = jnp.concatenate([middle, late.astype(BF), totals.astype(BF)], axis=1)
    done = jnp.concatenate([by_lanes(cross_part, part), by_lanes(kv_part, depth)], axis=0)
    enc_sum = enc_heads.reshape(ctx, -1, 2 * own)
    more = ()
    if own == 128:
        more = (moved, enc_sum, self_mine, self_other, kv_mine, kv_other)
    all_ffn, all_done, all_late, *more_sums = finish(late, done, ffn_sums, width, more)
    if more:
        more = (more_sums[0], tokens, gain[:1], grad_first, more_sums[1])
    (
        grad_ffn_in, grad_ffn_out, grad_self_in, grad_cross_kv, grad_cross_out, grad_cross_q,
        grad_self_out, *more_grads,
    ) = place(all_ffn, all_done, all_late, ffn_in.shape[1], width, more)
    grad_ffn_out = grad_ffn_out.reshape(-1, width)
    sums = jnp.sum(all_late[:, -48:].astype(F32), axis=0).reshape(-1)[:count]
    mine, grad_ffn_bias = sums[: 13 * shard].reshape(13, shard), sums[13 * shard :]
    if more:
        input_grad, grad_encoder = more_grads
    else:

        def whole(kept, other):
            pair = jnp.where(core == 0, jnp.stack([kept, other]), jnp.stack([other, kept]))
            return jnp.moveaxis(pair, 0, 1).reshape(width, -1)

        cut = moved.reshape(ctx, row_count, 3, 128)[:, :, :, :own]
        grads = jnp.transpose(cut, (1, 2, 0, 3)).reshape(row_count, 3 * width)
        unit_one, scale_one = normalize(token_values)
        grad_normed = nt(grads, whole(self_mine, self_other))
        input_grad = grad_first + normalize_back(unit_one, scale_one, gain[0], grad_normed)[0]
        enc_sum = lax.all_to_all(enc_sum, "ctx", split_axis=0, concat_axis=0, tiled=True)
        enc_sum = jnp.transpose(enc_sum.reshape(ctx, -1, 2, own), (1, 2, 0, 3))
        grad_encoder = nt(enc_sum.reshape(-1, 2 * width), whole(kv_mine, kv_other))
    return (
        layer_out, input_grad, grad_encoder, mine[:3], mine[3:12], grad_self_in, grad_self_out,
        grad_cross_q, grad_cross_kv, grad_cross_out, grad_ffn_in, grad_ffn_bias, grad_ffn_out, mine[12],
    )


def solution(mesh):
    rows = P(("fsdp", "ctx"), None)
    shard = P("fsdp", None)
    thin = P(None, "fsdp")
    flat = P("fsdp")
    return jax.shard_map(
        body,
        mesh=mesh,
        in_specs=(
            rows, rows, shard, thin, thin, shard, shard, shard, shard, shard, shard, flat, shard,
            flat, rows,
        ),
        out_specs=(
            rows, rows, rows, thin, thin, shard, shard, shard, shard, shard, shard, flat, shard,
            flat,
        ),
        check_vma=False,
    )
```

```python
import functools
import math

import jax
import jax.numpy as jnp
from jax import lax
from jax.experimental import pallas as pl
from jax.experimental.pallas import tpu as pltpu
from jax.sharding import PartitionSpec as P

HEADS = 16
CONT = 2048
EPS = 1e-05
NEG = -1e30
TILE = 512
BF = jnp.bfloat16
F32 = jnp.float32
VMEM_BYTES = 56 * 2**20


def nn(left, right):
    return lax.dot_general(left, right, (((1,), (0,)), ((), ())), preferred_element_type=F32)


def nt(left, right):
    return lax.dot_general(left, right, (((1,), (1,)), ((), ())), preferred_element_type=F32)


def tn(left, right):
    return lax.dot_general(left, right, (((0,), (0,)), ((), ())), preferred_element_type=F32)


def normalize(values):
    center = values - jnp.mean(values, axis=-1, keepdims=True)
    scale = lax.rsqrt(jnp.mean(center * center, axis=-1, keepdims=True) + EPS)
    return center * scale, scale


def normalize_back(unit, scale, gain, grad):
    q = gain * grad
    back = scale * (
        q - jnp.mean(q, axis=-1, keepdims=True) - unit * jnp.mean(q * unit, axis=-1, keepdims=True)
    )
    return back, jnp.sum(grad * unit, axis=0), jnp.sum(grad, axis=0)


def head_lanes(head, array):
    lane = lax.broadcasted_iota(jnp.int32, array.shape, 1)
    keep = (lane < 64) if head == 0 else (lane >= 64)
    return jnp.where(keep, array, jnp.zeros_like(array))


def transposed(array):
    return array.astype(F32).T.astype(BF)


def visible(key_start, query_start, key_count, query_count, own_start, limit):
    key = key_start + lax.broadcasted_iota(jnp.int32, (key_count, query_count), 0)
    query = query_start + lax.broadcasted_iota(jnp.int32, (key_count, query_count), 1)
    shown = key <= query
    if limit is not None:
        shown = shown & ((key >= own_start) | (key < limit))
    return shown


def soften(scores, total, peak, value_t):
    old = peak[:1]
    new = jnp.maximum(old, jnp.max(scores, axis=0, keepdims=True))
    raised = jnp.exp(scores - new).astype(BF)
    total[...] = total[...] * jnp.exp(old - new) + nn(value_t, raised)
    peak[...] = jnp.broadcast_to(new, peak.shape)


def set_value_rows(value_t, head, columns, value):
    value_t[head, :64, columns] = value[64 * head : 64 * head + 64]
    value_t[head, 64:, columns] = jnp.ones((16, value.shape[1]), BF)


def tile_rows(tile):
    return pl.ds(pl.multiple_of(tile * TILE, TILE), TILE)


def flipped_bits(index, mask):
    out, bit = index, 1
    while bit <= mask:
        if mask & bit:
            out = out + bit - 2 * bit * ((index // bit) % 2)
        bit *= 2
    return out


def greet(peers):
    barrier = pltpu.get_barrier_semaphore()
    for peer in peers:
        pl.semaphore_signal(
            barrier, inc=1, device_id=peer, device_id_type=pl.DeviceIdType.MESH
        )
    pl.semaphore_wait(barrier, len(peers))


def others(axis):
    me, count = lax.axis_index(axis), lax.axis_size(axis)
    return [{axis: (me + step) % count} for step in range(1, count)]


def remote(source, target, send_sem, recv_sem, device):
    return pltpu.make_async_remote_copy(
        source, target, send_sem, recv_sem, device_id=device,
        device_id_type=pl.DeviceIdType.MESH,
    )


def exchange(source, target, send_sems, recv_sems, own_sem):
    me, count = lax.axis_index("ctx"), lax.axis_size("ctx")

    def copy(there, slot):
        return remote(
            source.at[there], target.at[slot], send_sems.at[there], recv_sems.at[slot],
            {"ctx": there},
        )

    def send(there):
        @pl.when(there != me)
        def _():
            copy(there, me).start()

        @pl.when(there == me)
        def _():
            pltpu.make_async_copy(source.at[me], target.at[me], own_sem).start()

    def arrived(there):
        @pl.when(there != me)
        def _():
            copy(there, there).wait_recv()

        @pl.when(there == me)
        def _():
            pltpu.make_async_copy(source.at[me], target.at[me], own_sem).wait()

    def sent():
        for step in range(1, count):
            copy((me + step) % count, me).wait_send()

    return send, arrived, sent


def plane_gather(source, store, send, recv):
    me = lax.axis_index("ctx")
    chips = lax.axis_size("ctx") // 2
    last = chips - 1
    sibling = flipped_bits(me, 1)
    near = [flipped_bits(me, 2 * other) for other in range(1, chips)]
    relay = chips == 4
    height = store.shape[1]
    cut = height // 2 if height < 32 else height // 32 * 16

    def own(index, there, block):
        return remote(source, store.at[block], send.at[index], recv.at[index], {"ctx": there})

    def passed(index, block):
        return remote(
            store.at[block], store.at[block], send.at[chips + index], recv.at[chips + index],
            {"ctx": sibling},
        )

    def half(part, there, block):
        rows = pl.ds(0, cut) if part == 0 else pl.ds(cut, height - cut)
        at = 2 * chips - 1 + part
        return remote(
            store.at[block, rows], store.at[block, rows], send.at[at], recv.at[at], {"ctx": there}
        )

    firsts = range(2) if relay else range(last)

    def start():
        for index in firsts:
            own(index, near[index], me).start()
        own(last, sibling, me).start()

    def land(index):
        block = near[index]
        if relay and index == 2:
            half(0, near[0], block).wait_recv()
            half(1, near[1], block).wait_recv()
        else:
            own(index, block, block).wait_recv()
            if relay:
                half(1 - index, near[1 - index], block).start()
        passed(index, block).start()
        return block

    def rest(index):
        if index == 0:
            own(last, sibling, sibling).wait_recv()
            return sibling
        block = flipped_bits(near[index - 1], 1)
        passed(index - 1, block).wait_recv()
        return block

    def done():
        for index in firsts:
            own(index, near[index], me).wait_send()
        own(last, sibling, me).wait_send()
        for index in range(last):
            passed(index, near[index]).wait_send()
        if relay:
            half(0, near[0], near[1]).wait_send()
            half(1, near[1], near[0]).wait_send()

    return start, land, rest, done


def attend_forward_kernel(cross, heads, conts, offs_ref, q_ref, k_ref, v_ref, *refs):
    if cross:
        rows_ref, mixed_ref, att_ref, lse_ref, q_out, rows_all, pair_all, *refs = refs
    else:
        pair_ref, enc_ref, kv_ref, *refs = refs
        mixed_ref, att_ref, lse_ref, pair_all, enc_all, kv_all, *refs = refs
    total, peak, value_t, score_a, score_b, stage, send_sem, recv_sem, own_sem, pair_sem, *refs = refs
    me, count = lax.axis_index("ctx"), lax.axis_size("ctx")
    rows = att_ref.shape[1]
    tiles = rows // TILE
    key_tiles = k_ref.shape[0] // TILE
    prompt = rows - conts * CONT
    prompt_tiles = prompt // TILE
    greet(others("ctx") + others("fsdp"))
    send, arrived, sent = exchange(stage, mixed_ref, send_sem, recv_sem, own_sem)
    zone = lax.axis_index("fsdp")
    pair_copy = core_swap(rows_all if cross else pair_ref, pair_all, pair_sem)
    if not cross:
        gather_send, gather_recv, gather_own, kv_send, kv_recv = refs
        enc_start, enc_land, enc_rest, enc_done = plane_gather(
            enc_ref, enc_all, gather_send, gather_recv
        )
        enc_start()
        first = group_spread(kv_ref, kv_all, kv_send, kv_recv, 0)
        local = [
            pltpu.make_async_copy(enc_ref, enc_all.at[me], gather_own.at[0]),
            pltpu.make_async_copy(kv_ref, kv_all.at[zone], gather_own.at[1]),
        ]
        for copy in first + local:
            copy.start()
    if cross:
        q_all, q_send, q_recv, q_own, rows_send, rows_recv = refs
        put, got, put_done = exchange(q_ref, q_all, q_send, q_recv, q_own)
        for step in range(count):
            put((me + step) % count)
        spread = group_spread(rows_ref, rows_all, rows_send, rows_recv, 0)
        keep_rows = pltpu.make_async_copy(rows_ref, rows_all.at[zone], pair_sem.at[2])
        for copy in spread + [keep_rows]:
            copy.start()
    else:
        pair_copy.start()

    for tile in range(key_tiles):
        at = pl.ds(tile * TILE, TILE)
        turned = transposed(v_ref[at, :])
        for head in range(heads):
            set_value_rows(value_t, head, at, turned)

    def query_tile(step, carry):
        if cross:
            i = (me + step) % count
            got(i)
            q = q_all[i]
            q_out[i] = q
        else:
            i = (me + 1 + step) % count
            q = q_ref[tile_rows(i), :]
        masked = [head_lanes(head, q) for head in range(heads)]
        total[...] = jnp.zeros_like(total)
        peak[...] = jnp.full_like(peak, NEG)

        def score(j, target):
            k = k_ref[tile_rows(j), :]
            for head in range(heads):
                target[head] = nt(k, masked[head])

        def soft(j, source, shown=None):
            for head in range(heads):
                scores = source[head]
                if shown is not None:
                    scores = jnp.where(shown, scores, NEG)
                soften(
                    scores, total.at[head], peak.at[head], value_t[head, :, tile_rows(j)]
                )

        if cross:
            both = (score_a, score_b)
            score(0, score_a)
            for j in range(key_tiles):
                if j + 1 < key_tiles:
                    score(j + 1, both[(j + 1) % 2])
                soft(j, both[j % 2])
        elif conts == 1:
            score(i, score_a)
            diagonal = visible(0, 0, TILE, TILE, 0, None)

            @pl.when(i > 0)
            def _():
                score(i - 1, score_b)
                soft(i, score_a, diagonal)

            @pl.when(i == 0)
            def _():
                soft(i, score_a, diagonal)

            def two(t, carry):
                j = i - 1 - 2 * t
                score(jnp.maximum(j - 1, 0), score_a)
                soft(j, score_b)
                score(jnp.maximum(j - 2, 0), score_b)
                soft(j - 1, score_a)
                return carry

            lax.fori_loop(0, i // 2, two, 0)

            @pl.when(i % 2 == 1)
            def _():
                soft(0, score_b)
        else:
            cont = jnp.maximum(i * TILE - prompt, 0) // CONT
            inside = i * TILE < prompt
            own = jnp.where(inside, 0, prompt + cont * CONT)
            limit = offs_ref[0, cont]

            def one(j, carry):
                score(j, score_a)
                soft(j, score_a, visible(j * TILE, i * TILE, TILE, TILE, own, limit))
                return carry

            lax.fori_loop(jnp.where(inside, 0, own // TILE), i + 1, one, 0)
            lax.fori_loop(0, jnp.where(inside, 0, prompt_tiles), one, 0)

        for head in range(heads):
            part = total[head]
            att_ref[64 * head : 64 * head + 64, tile_rows(i)] = part[:64] / part[64:65]
            lse_ref[head : head + 1, tile_rows(i)] = peak[head][:1] + jnp.log(part[64:65])
        stage[i] = att_ref[:, tile_rows(i)].T.astype(BF)
        send(i)
        if cross:

            @pl.when(step == tiles - 2)
            def _():
                keep_rows.wait()
                for copy in spread:
                    copy.wait_recv()
                pair_copy.start()

        else:

            @pl.when(step == tiles - 3)
            def _():
                for index in range(min(2, count // 2 - 1)):
                    enc_land(index)

        return carry

    if heads < 2:
        att_ref[...] = jnp.zeros_like(att_ref)
    lax.fori_loop(0, tiles, query_tile, 0)
    for step in range(count):
        arrived((me + step) % count)
    sent()
    pair_copy.wait()
    if cross:
        put_done()
        for copy in spread:
            copy.wait_send()
    else:
        for index in range(2, count // 2 - 1):
            enc_land(index)
        for index in range(count // 2):
            enc_rest(index)
        for copy in first:
            copy.wait_send()
            copy.wait_recv()
        for copy in local:
            copy.wait()
        enc_done()


def core_swap(source, target, sems):
    there = {"ctx": flipped_bits(lax.axis_index("ctx"), 1)}
    return remote(source, target, sems.at[0], sems.at[1], there)


def group_spread(source, target, send_sem, recv_sem, sem):
    zone, groups = lax.axis_index("fsdp"), lax.axis_size("fsdp")
    return [
        remote(
            source, target.at[zone], send_sem.at[sem + shift - 1], recv_sem.at[sem + shift - 1],
            {"fsdp": (zone + shift) % groups},
        )
        for shift in range(1, groups)
    ]


def attend_forward(cross, heads, offsets, q, k, v, extra=()):
    count = lax.axis_size("ctx")
    rows = count * TILE
    vmem = pl.BlockSpec(memory_space=pltpu.VMEM)
    hbm = pl.BlockSpec(memory_space=pl.ANY)
    dma = pltpu.SemaphoreType.DMA
    tiles = jax.ShapeDtypeStruct((count, TILE, 128), BF)
    outs = [
        tiles,
        jax.ShapeDtypeStruct((128, rows), F32),
        jax.ShapeDtypeStruct((8, rows), F32),
    ]
    scratch = [
        pltpu.VMEM((heads, 80, TILE), F32),
        pltpu.VMEM((heads, 8, TILE), F32),
        pltpu.VMEM((heads, 80, k.shape[0]), BF),
        pltpu.VMEM((heads, TILE, TILE), F32),
        pltpu.VMEM((heads, TILE, TILE), F32),
        pltpu.VMEM((count, TILE, 128), BF),
        dma((count,)), dma((count,)), dma, dma((3,)),
    ]
    groups = lax.axis_size("fsdp")
    if cross:
        spread = jax.ShapeDtypeStruct((groups,) + extra[0].shape, BF)
        outs += [tiles, spread, spread]
        scratch += [pltpu.VMEM((count, TILE, 128), BF), dma((count,)), dma((count,)), dma]
        scratch += [dma((groups - 1,)), dma((groups - 1,))]
        places = [vmem, hbm, hbm]
    else:
        near, enc, kv = extra
        outs.append(jax.ShapeDtypeStruct(near.shape, BF))
        outs.append(jax.ShapeDtypeStruct((count,) + enc.shape, BF))
        outs.append(jax.ShapeDtypeStruct((groups,) + kv.shape, BF))
        scratch += [dma((count + 1,)), dma((count + 1,)), dma((2,))]
        scratch += [dma((groups - 1,)), dma((groups - 1,))]
        places = [hbm] * 3
    return pl.pallas_call(
        functools.partial(attend_forward_kernel, cross, heads, offsets.shape[1]),
        out_shape=outs,
        in_specs=[pl.BlockSpec(memory_space=pltpu.SMEM), vmem, vmem, vmem] + [hbm] * len(extra),
        out_specs=[hbm, vmem, vmem] + places,
        scratch_shapes=scratch,
        compiler_params=pltpu.CompilerParams(
            vmem_limit_bytes=VMEM_BYTES, collective_id=2 if cross else 1,
            has_side_effects=True,
        ),
        cost_estimate=pl.CostEstimate(
            flops=40 * 10**9, bytes_accessed=2**23, transcendentals=2**24
        ),
    )(offsets, q, k, v, *extra)


def rest_copies(sources, targets, send_sem, recv_sem):
    me = lax.axis_index("ctx")
    chips = lax.axis_size("ctx") // 2
    half = chips // 2
    out = []
    for other in range(1, half):
        for part in range(2):
            mine = me // 4 if part == 0 else (me // 2) % half
            sem = len(out)
            out.append(
                remote(
                    sources[part].at[:, :, flipped_bits(mine, other)],
                    targets[part].at[other - 1],
                    send_sem.at[sem], recv_sem.at[sem],
                    {"ctx": flipped_bits(me, (4 if part == 0 else 2) * other)},
                )
            )
    out = out + chip_copies(sources[2], targets[2], send_sem, recv_sem, len(out))
    return out + group_spread(sources[3], targets[3], send_sem, recv_sem, len(out))


def chip_copies(source, target, send_sem, recv_sem, sem):
    me = lax.axis_index("ctx")
    return [
        remote(
            source.at[flipped_bits(me // 2, other)], target.at[other - 1],
            send_sem.at[sem + other - 1], recv_sem.at[sem + other - 1],
            {"ctx": flipped_bits(me, 2 * other)},
        )
        for other in range(1, lax.axis_size("ctx") // 2)
    ]


def group_copies(source, target, send_sem, recv_sem, sem):
    zone, groups = lax.axis_index("fsdp"), lax.axis_size("fsdp")
    return [
        remote(
            source.at[(zone + shift) % groups], target.at[shift - 1],
            send_sem.at[sem + shift - 1], recv_sem.at[sem + shift - 1],
            {"fsdp": (zone + shift) % groups},
        )
        for shift in range(1, groups)
    ]


def last_copies(sources, targets, send_sem, recv_sem):
    out = chip_copies(sources[0], targets[0], send_sem, recv_sem, 0)
    for source, target in zip(sources[1:4], targets[1:4]):
        out = out + group_copies(source, target, send_sem, recv_sem, len(out))
    return out


def attend_backward_kernel(
    cross, heads, conts, scale, carried, number, offs_ref, q_ref, k_ref, v_ref, do_ref, att_ref,
    lse_ref, *refs,
):
    sources, refs = refs[:number], refs[number:]
    if not cross:
        normed_ref, *refs = refs
    if cross:
        moved_ref, dk_ref, dv_ref, *refs = refs
    else:
        moved_ref, stage, product_ref, column_ref, *refs = refs
    targets, refs = refs[:number], refs[number:]
    if cross:
        stage, *refs = refs
    (
        do_all, key_t, delta, dq_sum, dk_sum, dv_sum, score_a, score_b, grad_a, grad_b,
        send_sem, recv_sem, own_sem, do_send, do_recv, do_own, carry_send, carry_recv, *refs,
    ) = refs
    if cross:
        (keep_sem,) = refs
        keep_own = pltpu.make_async_copy(
            sources[3], targets[3].at[lax.axis_index("fsdp")], keep_sem
        )
    else:
        normed, normed_sem, *pair_sems = refs
        pair_copies = [
            core_swap(sources[4 + index], targets[4 + index], pair_sems[index])
            for index in range(2)
        ]
        product_ref[...] = jnp.zeros_like(product_ref)
        column_ref[...] = jnp.zeros_like(column_ref)
    me, count = lax.axis_index("ctx"), lax.axis_size("ctx")
    tiles = count
    key_tiles = k_ref.shape[0] // TILE
    prompt = tiles * TILE - conts * CONT
    greet(others("ctx") + others("fsdp"))
    put, got, put_done = exchange(do_ref, do_all, do_send, do_recv, do_own)
    for step in range(count):
        put((me + step) % count)
    carry_copies = carried(sources, targets, carry_send, carry_recv)
    for copy in carry_copies:
        copy.start()
    if cross:
        keep_own.start()
    else:
        for copy in pair_copies:
            copy.start()
    send, arrived, sent = exchange(stage, moved_ref, send_sem, recv_sem, own_sem)
    dq_sum[...] = jnp.zeros_like(dq_sum)
    dk_sum[...] = jnp.zeros_like(dk_sum)
    dv_sum[...] = jnp.zeros_like(dv_sum)
    for tile in range(key_tiles):
        at = pl.ds(tile * TILE, TILE)
        key_t[:, at] = transposed(k_ref[at, :])

    def ready(i):
        got(i)
        both = do_all[i].astype(F32).T * att_ref[:, tile_rows(i)]
        for head in range(heads):
            delta[head : head + 1, tile_rows(i)] = jnp.sum(
                both[64 * head : 64 * head + 64], axis=0, keepdims=True
            )

    def score(i, j, kept):
        row, at = tile_rows(i), tile_rows(j)
        q, do, k, v = q_ref[row, :], do_all[i], k_ref[at, :], v_ref[at, :]
        for head in range(heads):
            kept[0][head] = nt(k, head_lanes(head, q))
            kept[1][head] = nt(v, head_lanes(head, do))

    def settle(i, j, kept, shown=None):
        row, at = tile_rows(i), tile_rows(j)
        q, do = q_ref[row, :], do_all[i]
        for head in range(heads):
            weights = jnp.exp(kept[0][head] - lse_ref[head : head + 1, row])
            if shown is not None:
                weights = jnp.where(shown, weights, 0.0)
            score_grad = weights * (kept[1][head] - delta[head : head + 1, row])
            score_grad = score_grad.astype(BF)
            dv_sum[at, :] += nn(weights.astype(BF), head_lanes(head, do))
            dk_sum[at, :] += nn(score_grad, head_lanes(head, q))
            own = slice(64 * head, 64 * head + 64)
            dq_sum[own, row] += nn(key_t[own, at], score_grad)

    even, odd = (score_a, grad_a), (score_b, grad_b)

    def shown_of(i, j):
        if conts == 1:
            return None
        cont = jnp.maximum(i * TILE - prompt, 0) // CONT
        own = jnp.where(i * TILE < prompt, 0, prompt + cont * CONT)
        return visible(j * TILE, i * TILE, TILE, TILE, own, offs_ref[0, cont])

    def queries_back(i):
        return (dq_sum[:, tile_rows(i)].T.astype(BF).astype(F32) * scale).astype(BF)

    def cross_tile(step, carry):
        i = (me + step) % count
        ready(i)

        both = (even, odd)
        score(i, 0, even)
        for j in range(key_tiles):
            if j + 1 < key_tiles:
                score(i, j + 1, both[(j + 1) % 2])
            settle(i, j, both[j % 2])
        stage[i] = queries_back(i)
        send(i)
        return carry

    def self_tile(step, carry):
        i = (me + 1 + step) % count
        fetch = pltpu.make_async_copy(normed_ref.at[i], normed, normed_sem)
        fetch.start()

        def tiles_of(turn):
            p = (i + turn) % count
            return jnp.maximum(i, p), jnp.minimum(i, p)

        def score_turn(turn, kept):
            high, low = tiles_of(turn)
            score(high, low, kept)

        def settle_turn(turn, kept):
            high, low = tiles_of(turn)
            settle(high, low, kept, shown_of(high, low))

        diagonal = visible(0, 0, TILE, TILE, 0, None) if conts == 1 else shown_of(i, i)
        left = count - 1 - step

        @pl.when(step == 0)
        def _():
            ready(i)
            score(i, i, even)
            settle(i, i, even, diagonal)

            def fresh(turn, carry):
                ready((i + turn) % count)
                score_turn(turn, even)
                settle_turn(turn, even)
                return carry

            lax.fori_loop(1, count, fresh, 0)

        @pl.when(step > 0)
        def _():
            score(i, i, even)

            @pl.when(left > 0)
            def _():
                score_turn(1, odd)
                settle(i, i, even, diagonal)

            @pl.when(left == 0)
            def _():
                settle(i, i, even, diagonal)

            def two(turn, carry):
                at = 1 + 2 * turn
                score_turn(at + 1, even)
                settle_turn(at, odd)
                score_turn(at + 2, odd)
                settle_turn(at + 1, even)
                return carry

            lax.fori_loop(0, jnp.maximum(left - 1, 0) // 2, two, 0)

            @pl.when(left % 2 == 1)
            def _():
                settle_turn(left, odd)

            @pl.when((left > 0) & (left % 2 == 0))
            def _():
                score_turn(left, even)
                settle_turn(left - 1, odd)
                settle_turn(left, even)

        stage[i, :, :128] = queries_back(i)
        stage[i, :, 128:256] = dk_sum[tile_rows(i), :].astype(BF)
        stage[i, :, 256:] = dv_sum[tile_rows(i), :].astype(BF)
        send(i)
        fetch.wait()
        grads = stage[i]
        product_ref[...] += tn(normed[...], grads)
        column_ref[...] += jnp.broadcast_to(
            jnp.sum(grads.astype(F32), axis=0, keepdims=True), column_ref.shape
        )
        return carry

    lax.fori_loop(0, tiles, cross_tile if cross else self_tile, 0)
    if cross:
        dk_ref[...] = dk_sum[...].astype(BF)
        dv_ref[...] = dv_sum[...].astype(BF)
    for step in range(count):
        arrived((me + step) % count)
    sent()
    put_done()
    if cross:
        keep_own.wait()
    else:
        for copy in pair_copies:
            copy.wait()
    for copy in carry_copies:
        copy.wait_send()
        copy.wait_recv()


def attend_backward(
    cross, heads, scale, offsets, q, k, v, do, att, lse, sources, target_shapes, normed=()
):
    count = lax.axis_size("ctx")
    vmem = pl.BlockSpec(memory_space=pltpu.VMEM)
    hbm = pl.BlockSpec(memory_space=pl.ANY)
    dma = pltpu.SemaphoreType.DMA
    keys = k.shape[0]
    wide = 128 if cross else 384
    moved = jax.ShapeDtypeStruct((count, TILE, wide), BF)
    if cross:
        local = [jax.ShapeDtypeStruct((keys, 128), BF)] * 2
        carries = 2 * (count // 4 - 1) + count // 2 - 1 + lax.axis_size("fsdp") - 1
    else:
        local = [
            jax.ShapeDtypeStruct((count, TILE, wide), BF),
            jax.ShapeDtypeStruct((normed[0].shape[2], wide), F32),
            jax.ShapeDtypeStruct((8, wide), F32),
        ]
        carries = count // 2 - 1 + (lax.axis_size("fsdp") - 1) * 3
    targets = [jax.ShapeDtypeStruct(shape, BF) for shape in target_shapes]
    return pl.pallas_call(
        functools.partial(
            attend_backward_kernel, cross, heads, offsets.shape[1], scale,
            rest_copies if cross else last_copies, len(sources),
        ),
        out_shape=[moved] + local + targets,
        in_specs=[pl.BlockSpec(memory_space=pltpu.SMEM)] + [vmem] * 6
        + [hbm] * (len(sources) + len(normed)),
        out_specs=[hbm] + [vmem] * len(local) + [hbm] * len(sources),
        scratch_shapes=([pltpu.VMEM((count, TILE, wide), BF)] if cross else [])
        + [
            pltpu.VMEM((count, TILE, 128), BF),
            pltpu.VMEM((128, keys), BF),
            pltpu.VMEM((8, count * TILE), F32),
            pltpu.VMEM((128, count * TILE), F32),
            pltpu.VMEM((keys, 128), F32),
            pltpu.VMEM((keys, 128), F32),
        ]
        + [pltpu.VMEM((heads, TILE, TILE), F32)] * 4
        + [
            dma((count,)), dma((count,)), dma,
            dma((count,)), dma((count,)), dma,
            dma((carries,)), dma((carries,)),
        ]
        + ([dma] if cross else [pltpu.VMEM(normed[0].shape[1:], BF), dma, dma((2,)), dma((2,))]),
        compiler_params=pltpu.CompilerParams(
            vmem_limit_bytes=VMEM_BYTES, collective_id=3 if cross else 4,
            has_side_effects=True,
        ),
        cost_estimate=pl.CostEstimate(
            flops=60 * 10**9, bytes_accessed=2**23, transcendentals=2**24
        ),
    )(offsets, q, k, v, do, att, lse, *sources, *normed)


def project_kernel(
    own, scale, tokens_ref, small_ref, head_ref, rows_ref, normed_ref, q_ref, k_ref, v_ref,
    small_all, head_all, rows_all, all_tokens, staged, token_send, token_recv, part_send, part_recv,
    own_sem, stage_sem, rows_send, rows_recv,
):
    me, zone = lax.axis_index("ctx"), lax.axis_index("fsdp")
    count, groups = lax.axis_size("ctx"), lax.axis_size("fsdp")
    chips = count // 2
    spread = group_spread(rows_ref, rows_all, rows_send, rows_recv, 0)
    keep_rows = pltpu.make_async_copy(rows_ref, rows_all.at[zone], own_sem.at[3])
    shard = small_ref.shape[1]
    sibling = {"ctx": flipped_bits(me, 1)}
    near = [flipped_bits(me, 2 * other) for other in range(1, chips)]
    greet([sibling] + [{"ctx": there} for there in near] + others("fsdp"))

    parts = []
    for shift in range(1, groups):
        there = {"fsdp": (zone + shift) % groups}
        for index, (source, target) in enumerate(((small_ref, small_all), (head_ref, head_all))):
            parts.append(
                remote(source, target.at[zone], part_send.at[index, shift - 1],
                       part_recv.at[index, shift - 1], there)
            )
    local = [
        pltpu.make_async_copy(small_ref, small_all.at[zone], own_sem.at[0]),
        pltpu.make_async_copy(head_ref, head_all.at[zone], own_sem.at[1]),
        pltpu.make_async_copy(tokens_ref, all_tokens.at[me], own_sem.at[2]),
    ]
    for copy in local:
        copy.start()
    for copy in parts:
        copy.start()

    start, land, rest, done = plane_gather(tokens_ref, all_tokens, token_send, token_recv)
    start()
    for copy in spread + [keep_rows]:
        copy.start()
    for copy in local:
        copy.wait()
    for copy in parts:
        copy.wait_recv()

    def row(index):
        pieces = [small_all[z].astype(F32)[index : index + 1] for z in range(groups)]
        return jnp.concatenate(pieces, axis=1)

    gain, shift = row(0), row(3)
    mine = small_all[me // (shard // own)].astype(F32)
    q_shift = jnp.where(me % 2 == 0, mine[6:7, :own], mine[6:7, own : 2 * own])
    v_shift = jnp.where(me % 2 == 0, mine[7:8, :own], mine[7:8, own : 2 * own])
    if own < 128:
        for ref in (q_ref, k_ref, v_ref):
            ref[...] = jnp.zeros_like(ref)

    def save(block, place):
        return pltpu.make_async_copy(staged.at[place], normed_ref.at[block], stage_sem.at[place])

    order, ready = [], []
    for step in range(count):
        place = step % 2
        if step == 0:
            ready.append(me)
        elif step == 1:
            ready.append(rest(0))
        elif step == 2:
            for index in range(min(2, chips - 1)):
                ready.append(land(index))
        elif len(ready) == step:
            index = step - chips - 1
            if step == 4 and chips == 4:
                ready += [rest(1), rest(2)]
            elif step == 6 and chips == 4:
                ready.append(land(2))
            elif chips == 4:
                ready.append(rest(3))
            else:
                ready.append(land(step - 2) if step <= chips else rest(index + 1))
        block = ready[step]
        order.append(block)
        if step >= 2:
            save(order[step - 2], place).wait()
        unit, _ = normalize(all_tokens[block].astype(F32))
        staged[place] = (unit * gain + shift).astype(BF)
        save(block, place).start()
        total = jnp.zeros((staged.shape[1], 3 * own), F32)
        for z in range(groups):
            total = total + nn(staged[place, :, z * shard : z * shard + shard], head_all[z])
        q_ref[block, :, :own] = (scale * (total[:, :own] + q_shift)).astype(BF)
        k_ref[block, :, :own] = total[:, own : 2 * own].astype(BF)
        v_ref[block, :, :own] = (total[:, 2 * own :] + v_shift).astype(BF)
    for step in (count - 2, count - 1):
        save(order[step], step % 2).wait()
    for copy in parts:
        copy.wait_send()
    keep_rows.wait()
    for copy in spread:
        copy.wait_send()
        copy.wait_recv()
    done()


def project(own, scale, tokens, small, head_in, rows_part):
    count, groups = lax.axis_size("ctx"), lax.axis_size("fsdp")
    rows, width = tokens.shape
    vmem = pl.BlockSpec(memory_space=pltpu.VMEM)
    hbm = pl.BlockSpec(memory_space=pl.ANY)
    dma = pltpu.SemaphoreType.DMA
    lanes = jax.ShapeDtypeStruct((count, rows, 128), BF)
    return pl.pallas_call(
        functools.partial(project_kernel, own, scale),
        out_shape=(
            jax.ShapeDtypeStruct((count, rows, width), BF),
            lanes, lanes, lanes,
            jax.ShapeDtypeStruct((groups,) + small.shape, BF),
            jax.ShapeDtypeStruct((groups,) + head_in.shape, BF),
            jax.ShapeDtypeStruct((groups,) + rows_part.shape, BF),
        ),
        in_specs=[hbm, hbm, hbm, hbm],
        out_specs=(hbm,) + (vmem,) * 5 + (hbm,),
        scratch_shapes=[
            pltpu.VMEM((count, rows, width), BF),
            pltpu.VMEM((2, rows, width), BF),
            dma((count + 1,)), dma((count + 1,)),
            dma((2, groups - 1)), dma((2, groups - 1)),
            dma((4,)), dma((2,)), dma((groups - 1,)), dma((groups - 1,)),
        ],
        compiler_params=pltpu.CompilerParams(
            vmem_limit_bytes=VMEM_BYTES, collective_id=5, has_side_effects=True
        ),
        cost_estimate=pl.CostEstimate(
            flops=50 * 10**9, bytes_accessed=2**25, transcendentals=0
        ),
    )(tokens, small, head_in, rows_part)


def ffn_kernel(
    steps, groups, n_ref, dy_ref, base_ref, bias_ref, win_ref, wout_ref, rows_ref,
    out_ref, gn_ref, gb_ref, in_ref, sum_ref, rows_all,
    n_t, own_in, own_out, post_in, post_out, got_in, got_out,
    keep_in, keep_out, flow_in, flow_out, near_in, near_out,
    send_sem, recv_sem, flow_send, flow_recv, save_sem, rows_send, rows_recv, rows_own,
):
    f = pl.program_id(0)
    spread = group_spread(rows_ref, rows_all, rows_send, rows_recv, 0)
    keep_rows = pltpu.make_async_copy(
        rows_ref, rows_all.at[lax.axis_index("fsdp")], rows_own
    )
    me = lax.axis_index("ctx")
    count = lax.axis_size("ctx")
    chips = count // 2
    core = me % 2
    low_bit = (me // 2) % 2
    high_bit = me // chips
    cols = keep_in.shape[2]
    slot = f % 2
    sibling = {"ctx": flipped_bits(me, 1)}
    low = {"ctx": flipped_bits(me, 2)}
    high = {"ctx": flipped_bits(me, chips)}

    def copies(step, place):
        return (
            remote(post_in.at[place], got_in.at[step], send_sem.at[0, place],
                   recv_sem.at[0, step], sibling),
            remote(post_out.at[place], got_out.at[step], send_sem.at[1, place],
                   recv_sem.at[1, step], sibling),
        )

    def flows(step, place):
        return (
            remote(flow_in.at[place], near_in.at[step], flow_send.at[0, place],
                   flow_recv.at[0, step], low),
            remote(flow_out.at[place], near_out.at[step], flow_send.at[1, place],
                   flow_recv.at[1, step], high),
        )

    @pl.when(f == 0)
    def _():
        greet([sibling, low, high] + others("fsdp"))
        for copy in spread:
            copy.start()
        keep_rows.start()
        n_t[...] = transposed(n_ref[...])
        gn_ref[...] = jnp.zeros_like(gn_ref)
        out_ref[...] = base_ref[...]

    @pl.when(f < steps)
    def _():
        @pl.when(f >= 2)
        def _():
            for copy in copies(jnp.maximum(f - 2, 0), slot):
                copy.wait_send()

        pre = nn(n_ref[...], win_ref[...]) + bias_ref[0, :1]
        below = 0.5 * (1.0 + lax.erf(pre * (1.0 / math.sqrt(2.0))))
        hidden = (pre * below).astype(BF)
        out_ref[...] += nn(hidden, wout_ref[...])
        slope = below + pre * (jnp.exp(-0.5 * pre * pre) * (1.0 / math.sqrt(2.0 * math.pi)))
        dy = dy_ref[...]
        grad_pre = (nt(dy, wout_ref[...]) * slope).astype(BF)
        gb_ref[0] = jnp.broadcast_to(
            jnp.sum(grad_pre.astype(F32), axis=0, keepdims=True), gb_ref.shape[1:]
        )
        gn_ref[...] += nt(grad_pre, win_ref[...])

        def split(part, keep, post, half):
            left, right = part[:, :half], part[:, half:]
            keep[slot] = jnp.where(core == 0, left, right)
            post[slot] = jnp.where(core == 0, right, left).astype(BF)

        first, second = copies(jnp.minimum(f, steps - 1), slot)
        split(nn(n_t[...], grad_pre), own_in, post_in, cols)
        first.start()
        split(tn(hidden, dy), own_out, post_out, 2 * cols)
        second.start()

    @pl.when(f > 0)
    def _():
        past = jnp.maximum(f - 1, 0)
        place = (f + 1) % 2
        for copy in copies(past, place):
            copy.wait_recv()

        @pl.when(f >= 3)
        def _():
            for copy in flows(jnp.maximum(f - 3, 0), place):
                copy.wait_send()

        unit = keep_in.shape[1] // (groups * (chips // 2))
        for slab in range(groups * (chips // 2)):
            for kept in (True, False):
                take = low_bit if kept else 1 - low_bit
                rows = pl.ds(pl.multiple_of((2 * slab + take) * unit, unit), unit)
                both = own_in[place, rows, :] + got_in[past, rows, :].astype(F32)
                at = slice(unit * slab, unit * slab + unit)
                if kept:
                    keep_in[past, at, :] = both.astype(BF)
                else:
                    flow_in[place, at, :] = both.astype(BF)
        unit = n_t.shape[0] // groups // 2
        for slab in range(own_out.shape[1] // (2 * unit)):
            for kept in (True, False):
                take = high_bit if kept else 1 - high_bit
                rows = pl.ds(pl.multiple_of((2 * slab + take) * unit, unit), unit)
                both = own_out[place, rows, :] + got_out[past, rows, :].astype(F32)
                at = slice(unit * slab, unit * slab + unit)
                for half in range(2):
                    value = both[:, half * cols : half * cols + cols].astype(BF)
                    if kept:
                        keep_out[past, half, at, :] = value
                    else:
                        flow_out[place, half, at, :] = value
        for copy in flows(past, place):
            copy.start()

    @pl.when(f == steps)
    def _():
        for back in (2, 1):
            for copy in copies(steps - back, (steps - back) % 2):
                copy.wait_send()
            for copy in flows(steps - back, (steps - back) % 2):
                copy.wait_send()
        per = steps // sum_ref.shape[0]
        height = keep_out.shape[2]

        def saves(step):
            rows = pl.ds(pl.multiple_of((step % per) * height, height), height)
            return (
                pltpu.make_async_copy(
                    keep_in.at[step], in_ref.at[step], save_sem.at[0, step]
                ),
                pltpu.make_async_copy(
                    keep_out.at[step], sum_ref.at[step // per, :, rows], save_sem.at[1, step]
                ),
            )

        def join(step, carry):
            for copy in flows(step, step % 2):
                copy.wait_recv()
            keep_in[step] = (
                keep_in[step].astype(F32) + near_in[step].astype(F32)
            ).astype(BF)
            keep_out[step] = (
                keep_out[step].astype(F32) + near_out[step].astype(F32)
            ).astype(BF)
            for copy in saves(step):
                copy.start()
            return carry

        def saved(step, carry):
            for copy in saves(step):
                copy.wait()
            return carry

        lax.fori_loop(0, steps, join, 0)
        lax.fori_loop(0, steps, saved, 0)
        keep_rows.wait()
        for copy in spread:
            copy.wait_send()
            copy.wait_recv()


def ffn(normed, dy, base, bias, weights, rows_part):
    rows, width = normed.shape
    hidden = weights.shape[1] // 2
    groups = lax.axis_size("fsdp")
    step = 512
    cols = step // 2
    steps = hidden // step
    per = width // step
    last = steps - 1

    def now(f):
        return jnp.minimum(f, last)

    whole = lambda f: (0, 0)
    hbm = pl.BlockSpec(memory_space=pl.ANY)
    dma = pltpu.SemaphoreType.DMA
    once = pl.BlockSpec((rows, width), whole, pipeline_mode=pl.Buffered(1))
    return pl.pallas_call(
        functools.partial(ffn_kernel, steps, groups),
        grid=(steps + 1,),
        out_shape=(
            jax.ShapeDtypeStruct((rows, width), F32),
            jax.ShapeDtypeStruct((rows, width), F32),
            jax.ShapeDtypeStruct((steps, 8, step), F32),
            jax.ShapeDtypeStruct((steps, width // 2, cols), BF),
            jax.ShapeDtypeStruct((hidden // width, 2, width // 2, cols), BF),
            jax.ShapeDtypeStruct((groups,) + rows_part.shape, BF),
        ),
        in_specs=[
            once, once, once,
            pl.BlockSpec((1, 8, step), lambda f: (now(f), 0, 0)),
            pl.BlockSpec((width, step), lambda f: (0, now(f))),
            pl.BlockSpec(
                (step, width), lambda f: (now(f) % per, hidden // width + now(f) // per)
            ),
            hbm,
        ],
        out_specs=(
            pl.BlockSpec((rows, width), whole),
            pl.BlockSpec((rows, width), whole),
            pl.BlockSpec((1, 8, step), lambda f: (now(f), 0, 0)),
            hbm, hbm, hbm,
        ),
        scratch_shapes=[
            pltpu.VMEM((width, rows), BF),
            pltpu.VMEM((2, width, cols), F32),
            pltpu.VMEM((2, step, 2 * cols), F32),
            pltpu.VMEM((2, width, cols), BF),
            pltpu.VMEM((2, step, 2 * cols), BF),
            pltpu.VMEM((steps, width, cols), BF),
            pltpu.VMEM((steps, step, 2 * cols), BF),
            pltpu.VMEM((steps, width // 2, cols), BF),
            pltpu.VMEM((steps, 2, step // 2, cols), BF),
            pltpu.VMEM((2, width // 2, cols), BF),
            pltpu.VMEM((2, 2, step // 2, cols), BF),
            pltpu.VMEM((steps, width // 2, cols), BF),
            pltpu.VMEM((steps, 2, step // 2, cols), BF),
            dma((2, 2)), dma((2, steps)), dma((2, 2)), dma((2, steps)), dma((2, steps)),
            dma((groups - 1,)), dma((groups - 1,)), dma,
        ],
        compiler_params=pltpu.CompilerParams(
            vmem_limit_bytes=60 * 2**20, collective_id=0, has_side_effects=True
        ),
        cost_estimate=pl.CostEstimate(
            flops=30 * 10**9, bytes_accessed=2**26, transcendentals=2**22
        ),
    )(normed, dy, base, bias, weights, weights, rows_part)


def finish_kernel(more, late_ref, done_ref, ffn_ref, *refs):
    if more:
        moved_ref, enc_ref, *late, refs = (*refs[:6], refs[6:])
    all_ffn, all_done, all_late, *refs = refs
    if more:
        token_ref, enc_grad_ref, *refs = refs
    late_own, got, send_sem, recv_sem, zone_send, zone_recv, own_sem, *refs = refs
    me, zone = lax.axis_index("ctx"), lax.axis_index("fsdp")
    count, groups = lax.axis_size("ctx"), lax.axis_size("fsdp")
    chips = count // 2
    greet(others("ctx") + others("fsdp"))
    zones = group_copies(late_ref, got, zone_send, zone_recv, 0)
    for copy in zones:
        copy.start()
    if more:
        all_moved, weights, all_enc, enc_send, enc_recv, enc_own, moved_sem, weight_sem = refs
        put, arrived, put_done = exchange(enc_ref, all_enc, enc_send, enc_recv, enc_own)
        for step in range(count):
            put((me + step) % count)
        fetch_moved = pltpu.make_async_copy(moved_ref, all_moved, moved_sem)
        fetch_moved.start()
    gathers = [
        plane_gather(source, store, send_sem.at[kind], recv_sem.at[kind])
        for kind, (source, store) in enumerate(
            ((ffn_ref, all_ffn), (done_ref, all_done), (late_own, all_late))
        )
    ]
    local = [
        pltpu.make_async_copy(source, store.at[me], own_sem.at[kind])
        for kind, (source, store) in enumerate(
            ((ffn_ref, all_ffn), (done_ref, all_done), (late_own, all_late))
        )
    ]
    for kind in range(2):
        gathers[kind][0]()
        local[kind].start()
    if more:
        width = token_ref.shape[1]

        def fetch(step):
            source = (me + step) % count
            out = []
            for k in range(5):
                columns = pl.ds(pl.multiple_of(k * width + source * 128, 128), 128)
                for index, array in enumerate(late):
                    side = me % 2 if index < 2 else 1 - me % 2
                    out.append(
                        pltpu.make_async_copy(
                            array.at[:, :, columns], weights.at[step % 2, k, :, side, index % 2],
                            weight_sem.at[step % 2, k, index],
                        )
                    )
            return out

        for copy in fetch(0):
            copy.start()
        token_ref[...] = jnp.zeros_like(token_ref)
        enc_grad_ref[...] = jnp.zeros_like(enc_grad_ref)
        fetch_moved.wait()

        def one_source(step, carry):
            source = (me + step) % count

            @pl.when(step + 1 < count)
            def _():
                for copy in fetch(step + 1):
                    copy.start()

            for copy in fetch(step):
                copy.wait()
            grads = all_moved[source]

            def part(index):
                return weights[step % 2, index].reshape(width, 128)

            token_ref[...] += (
                nt(grads[:, :128], part(0))
                + nt(grads[:, 128:256], part(1))
                + nt(grads[:, 256:], part(2))
            )
            arrived(source)
            rows = all_enc[source]
            enc_grad_ref[...] += nt(rows[:, :128], part(3)) + nt(rows[:, 128:], part(4))
            return carry

        lax.fori_loop(0, count, one_source, 0)
    total = late_ref[zone].astype(F32)
    for shift in range(groups - 1):
        zones[shift].wait_recv()
        total = total + got[shift].astype(F32)
    late_own[...] = total.astype(BF)
    gathers[2][0]()
    local[2].start()
    for index in range(chips - 1):
        for gather in gathers:
            gather[1](index)
    for index in range(chips):
        for gather in gathers:
            gather[2](index)
    for copy in local:
        copy.wait()
    for gather in gathers:
        gather[3]()
    for copy in zones:
        copy.wait_send()
    if more:
        put_done()


def finish(late, done, ffn_sums, width, more=()):
    count, groups = lax.axis_size("ctx"), lax.axis_size("fsdp")
    vmem = pl.BlockSpec(memory_space=pltpu.VMEM)
    hbm = pl.BlockSpec(memory_space=pl.ANY)
    dma = pltpu.SemaphoreType.DMA
    outs = [
        jax.ShapeDtypeStruct((count,) + shape, BF)
        for shape in (ffn_sums.shape, done.shape, late.shape[1:])
    ]
    places = [hbm] * 3
    scratch = [
        pltpu.VMEM(late.shape[1:], BF),
        pltpu.VMEM((groups - 1,) + late.shape[1:], BF),
        dma((3, count + 1)), dma((3, count + 1)),
        dma((groups - 1,)), dma((groups - 1,)), dma((3,)),
    ]
    if more:
        moved, enc, weights = more[:3]
        outs.append(jax.ShapeDtypeStruct((moved.shape[1], width), F32))
        outs.append(jax.ShapeDtypeStruct((enc.shape[1], width), F32))
        places += [vmem, vmem]
        scratch += [
            pltpu.VMEM(moved.shape, BF),
            pltpu.VMEM((2, 5, groups, 2, 2, weights.shape[1], 128), BF),
            pltpu.VMEM(enc.shape, BF),
            dma((count,)), dma((count,)), dma, dma, dma((2, 5, 4)),
        ]
    return pl.pallas_call(
        functools.partial(finish_kernel, bool(more)),
        out_shape=outs,
        in_specs=[vmem] + [hbm] * (2 + len(more)),
        out_specs=places,
        scratch_shapes=scratch,
        compiler_params=pltpu.CompilerParams(
            vmem_limit_bytes=VMEM_BYTES, collective_id=6, has_side_effects=True
        ),
        cost_estimate=pl.CostEstimate(
            flops=50 * 10**9, bytes_accessed=2**25, transcendentals=0
        ),
    )(late, done, ffn_sums, *more)


def place_kernel(groups, more, ffn_ref, self_refs, kv_refs, mixed_refs, out_refs, extra):
    in_ref, out_ref, self_ref, kv_ref, *weight_refs = out_refs
    cols = ffn_ref.shape[3]
    steps = ffn_ref.shape[1] // 2
    hidden = in_ref.shape[1]
    blocks = out_ref.shape[0]
    width = out_ref.shape[3]
    depth = width // groups
    per = steps // blocks
    span = min(depth, cols)
    for core in range(2):
        for f in range(steps):
            value = ffn_ref[core, f].astype(F32)
            for piece in range(cols // span):
                unit = (f % per) * 2 * cols + core * cols + piece * span
                at = (unit // depth * blocks + f // per) * depth + unit % depth
                in_ref[:, at : at + span] = value[:, piece * span : piece * span + span]
        for slab in range(steps):
            at = (core * 2 + slab % 2) * cols
            out_ref[slab // 2, 0, :, at : at + cols] = ffn_ref[core, steps + slab].astype(F32)
    for refs, target in ((self_refs, self_ref), (kv_refs, kv_ref)):
        for k, ref in enumerate(refs):
            own = ref.shape[2]
            for source in range(ref.shape[0]):
                at = k * width + source * own
                target[:, at : at + own] = ref[source].astype(F32)
    part = in_ref.shape[0]
    for (ref, count), targets in zip(mixed_refs, (weight_refs[:1], weight_refs[1:])):
        own = ref.shape[2]
        for w, target in enumerate(targets):
            for core in range(2):
                for index in range(count):
                    top = (w * count + index) * part
                    at = core * (width // 2) + index * own
                    target[:, at : at + own] = ref[core, top : top + part, :].astype(F32)
    if more:
        total_ref, tokens_ref, gain_ref, base_ref, enc_ref, token_ref, enc_out = extra
        unit, scale = normalize(tokens_ref[...].astype(F32))
        token_ref[...] = (
            base_ref[...] + normalize_back(unit, scale, gain_ref[...], total_ref[...])[0]
        )
        enc_out[...] = enc_ref[...]


def place(ffn_sums, done, late, hidden, width, more=()):
    count, groups = lax.axis_size("ctx"), lax.axis_size("fsdp")
    chips, own = count // 2, late.shape[2]
    depth = width // groups
    part = depth // chips
    blocks = hidden // width
    wide = width // 2 // own

    def lane_blocks(start, k):
        return pl.BlockSpec((count, part, own), lambda c: (0, (start + k * depth) // part + c, 0))

    in_specs = [pl.BlockSpec((2,) + ffn_sums.shape[1:], lambda c: (c, 0, 0, 0))]
    in_specs += [lane_blocks(2 * wide * part, k) for k in range(3)]
    in_specs += [lane_blocks(wide * part, k) for k in range(2)]
    in_specs += [
        pl.BlockSpec((2, wide * part, own), lambda c: (c, 0, 0)),
        pl.BlockSpec((2, 2 * wide * part, own), lambda c: (c, 0, 0)),
    ]
    row = lambda n: pl.BlockSpec((part, n), lambda c: (c, 0))
    out_specs = [
        row(hidden), pl.BlockSpec((blocks, 1, part, width), lambda c: (0, c, 0, 0)),
        row(3 * width), row(2 * width), row(width), row(width), row(width),
    ]
    out_shape = [
        jax.ShapeDtypeStruct((depth, hidden), F32),
        jax.ShapeDtypeStruct((blocks, chips, part, width), F32),
        jax.ShapeDtypeStruct((depth, 3 * width), F32),
        jax.ShapeDtypeStruct((depth, 2 * width), F32),
    ] + [jax.ShapeDtypeStruct((depth, width), F32)] * 3
    if more:
        total, _, _, _, enc = more
        tall, short = total.shape[0] // chips, enc.shape[0] // chips
        tokens_rows = pl.BlockSpec((tall, width), lambda c: (c, 0))
        enc_rows = pl.BlockSpec((short, width), lambda c: (c, 0))
        in_specs += [
            tokens_rows, tokens_rows, pl.BlockSpec((1, width), lambda c: (0, 0)), tokens_rows,
            enc_rows,
        ]
        out_specs += [tokens_rows, enc_rows]
        out_shape += [
            jax.ShapeDtypeStruct(total.shape, F32), jax.ShapeDtypeStruct(enc.shape, F32)
        ]

    def kernel(*refs):
        ffn_ref, refs = refs[0], refs[1:]
        self_refs, kv_refs, mixed, refs = refs[:3], refs[3:5], refs[5:7], refs[7:]
        extra_in, refs = refs[: len(more)], refs[len(more) :]
        place_kernel(
            groups, bool(more), ffn_ref, self_refs, kv_refs,
            ((mixed[0], wide), (mixed[1], wide)), refs[:7], extra_in + refs[7:],
        )

    return pl.pallas_call(
        kernel,
        grid=(chips,),
        out_shape=out_shape,
        in_specs=in_specs,
        out_specs=out_specs,
        compiler_params=pltpu.CompilerParams(vmem_limit_bytes=VMEM_BYTES),
        cost_estimate=pl.CostEstimate(flops=0, bytes_accessed=2**25, transcendentals=0),
    )(ffn_sums, late, late, late, done, done, done, late, *more)


def swap(value, bit):
    count = lax.axis_size("ctx")
    return lax.ppermute(value, "ctx", [(i, i ^ bit) for i in range(count)])


def pair_product(left, right):
    core = lax.axis_index("ctx") % 2
    half = right.shape[1] // 2
    send = tn(left, lax.dynamic_slice_in_dim(right, (1 - core) * half, half, 1)).astype(BF)
    got = swap(send, 1).astype(F32)
    kept = tn(left, lax.dynamic_slice_in_dim(right, core * half, half, 1))
    return (kept + got).astype(BF)


def gather_ffn(ffn_in, ffn_out):
    count = lax.axis_size("ctx")
    groups = lax.axis_size("fsdp")
    me = lax.axis_index("ctx")
    depth, hidden = ffn_in.shape
    width = ffn_out.shape[1]
    blocks = hidden // width
    rows = depth // count
    left = lax.dynamic_slice_in_dim(ffn_in, me * rows, rows, 0)
    left = left.reshape(rows, groups, blocks, depth)
    left = jnp.transpose(left, (0, 2, 1, 3)).reshape(rows, hidden)
    right = lax.dynamic_index_in_dim(
        ffn_out.reshape(blocks, count, rows, width), me, 1, keepdims=False
    )
    right = jnp.moveaxis(right, 0, 1).reshape(rows, hidden)
    joined = jnp.concatenate([left, right], axis=1)
    return lax.all_gather(joined, ("fsdp", "ctx"), axis=0, tiled=True)


def body(
    tokens, encoder_out, prompt_offsets, gains, shifts, self_in, self_out, cross_q, cross_kv,
    cross_out, ffn_in, ffn_bias, ffn_out, out_bias, cotangent,
):
    row_count, width = tokens.shape
    head_dim = width // HEADS
    scale = 1.0 / math.sqrt(head_dim)
    ctx = lax.axis_size("ctx")
    groups = lax.axis_size("fsdp")
    me = lax.axis_index("ctx")
    heads = HEADS // ctx
    own = heads * head_dim

    shard = gains.shape[1]
    small = jnp.concatenate(
        [gains, shifts, out_bias[None], ffn_bias.reshape(-1, shard)], axis=0
    )
    small_rows = small.shape[0]
    small = jnp.pad(small, ((0, 32 - small_rows), (0, 0)))

    head_in = lax.dynamic_index_in_dim(
        self_in.reshape(self_in.shape[0], 3, ctx, own), me, 2, keepdims=False
    ).reshape(-1, 3 * own)
    half_rows = self_in.shape[0] // 2
    core = me % 2

    def half_of(*weights):
        cut = [lax.dynamic_slice_in_dim(w, core * half_rows, half_rows, 0) for w in weights]
        return jnp.concatenate(cut, axis=1)

    all_normed, queries, keys, values, small, head_in, near_rows = project(
        own, scale, tokens, small, head_in, half_of(self_out, cross_q)
    )
    all_normed = all_normed.reshape(-1, width)
    queries, keys, values = [x.reshape(-1, 128) for x in (queries, keys, values)]
    small = small[:, :small_rows].astype(F32)
    vectors = jnp.moveaxis(small[:, :13], 0, 1).reshape(13, width)
    gain, shift, full_out_bias = vectors[:3], vectors[3:12], vectors[12]
    full_ffn_bias = small[:, 13:].reshape(-1)

    def lanes(value):
        gap = [(0, 0)] * (value.ndim - 1) + [(0, 128 - own)]
        return value if own == 128 else jnp.pad(value, gap)

    head_kv = lax.dynamic_index_in_dim(
        cross_kv.reshape(-1, 2, ctx, own), me, 2, keepdims=False
    ).reshape(-1, 2 * own)
    (queries, ffn_in, ffn_out) = lax.optimization_barrier((queries, ffn_in, ffn_out))
    ffn_weights = gather_ffn(ffn_in, ffn_out)
    mixed_heads, att_self, lse_self, near_other, all_encoder, head_kv = attend_forward(
        False, heads, prompt_offsets, queries, keys, values, (near_rows, encoder_out, head_kv),
    )

    def both_cores(mine, other):
        shape = (mine.shape[0], 2) + mine.shape[1:]
        full = lax.dynamic_update_index_in_dim(jnp.zeros(shape, BF), mine, core, 1)
        full = lax.dynamic_update_index_in_dim(full, other, 1 - core, 1)
        return full.reshape(width, -1)

    near_weights = both_cores(near_rows, near_other)
    full_self_out, full_cross_q = near_weights[:, :width], near_weights[:, width:]
    all_encoder = all_encoder.reshape(-1, width)
    head_kv = head_kv.reshape(width, 2 * own)

    def to_rows(value):
        return jnp.moveaxis(value[:, :, :own], 0, 1).reshape(row_count, width)

    def to_heads(value):
        return lanes(jnp.moveaxis(value.reshape(row_count, ctx, own), 1, 0))

    mixed = to_rows(mixed_heads)
    token_values = tokens.astype(F32)
    first = token_values + nn(mixed, full_self_out) + shift[5]
    unit_two, scale_two = normalize(first)
    normed_two = (unit_two * gain[1] + shift[1]).astype(BF)
    cross_queries = (scale * (nn(normed_two, full_cross_q) + shift[6])).astype(BF)
    enc_shift = lax.dynamic_slice_in_dim(shift[7], me * own, own, 0)
    enc_projected = nn(all_encoder, head_kv)
    enc_keys = lanes(enc_projected[:, :own].astype(BF))
    enc_values = lanes((enc_projected[:, own:] + enc_shift).astype(BF))
    cross_heads, att_cross, lse_cross, all_cross_q, far_rows, far_other = attend_forward(
        True, heads, prompt_offsets, to_heads(cross_queries), enc_keys, enc_values,
        (half_of(cross_out),),
    )
    full_cross_out = both_cores(far_rows, far_other)
    cross_mixed = to_rows(cross_heads)
    second = first + nn(cross_mixed, full_cross_out) + shift[8]
    unit_three, scale_three = normalize(second)
    normed_three = (unit_three * gain[2] + shift[2]).astype(BF)
    depth = ffn_in.shape[0]
    blocks = ffn_in.shape[1] // width
    order = full_ffn_bias.reshape(groups, blocks, depth)
    order = jnp.moveaxis(order, 0, 1).reshape(-1, 1, 512)
    late_rows = half_of(self_in, cross_kv)
    quarter = half_rows // 2
    layer_sum, grad_three, bias_parts, in_sum, out_sum, late_first = ffn(
        normed_three, cotangent, second + full_out_bias,
        jnp.broadcast_to(order, (order.shape[0], 8, 512)), ffn_weights, late_rows[:quarter],
    )
    layer_out = layer_sum.astype(BF)
    chips = ctx // 2
    part = depth // chips
    in_sum = in_sum.reshape(-1, groups, chips // 2, part, 256)
    out_sum = out_sum.reshape(-1, groups, chips // 2, part, 256)

    dy = cotangent.astype(F32)
    back_three = normalize_back(unit_three, scale_three, gain[2], grad_three)
    grad_second = dy + back_three[0]
    branch_two = grad_second.astype(BF)
    chip_first = lambda value: jnp.moveaxis(value.reshape(groups, chips, part, -1), 1, 0)
    cross_part = chip_first(pair_product(cross_mixed, branch_two))
    grad_cross_mixed = nt(branch_two, full_cross_out).astype(BF)
    got_shape = (max(chips // 2 - 1, 1),) + in_sum.shape[:2] + in_sum.shape[3:]
    cross_moved, cross_dk, cross_dv, in_got, out_got, cross_got, late_second = attend_backward(
        True, heads, scale, prompt_offsets, all_cross_q.reshape(-1, 128), enc_keys, enc_values,
        to_heads(grad_cross_mixed), att_cross, lse_cross,
        (in_sum, out_sum, cross_part, late_rows[quarter:]),
        (got_shape, got_shape, (chips - 1,) + cross_part.shape[1:], late_first.shape),
    )

    def joined(value, mine, dim, got):
        kept = lax.dynamic_index_in_dim(value, mine, dim, keepdims=False).astype(F32)
        return kept + jnp.sum(got.astype(F32), axis=0)

    cross_dq = to_rows(cross_moved)
    back_two = normalize_back(unit_two, scale_two, gain[1], nt(cross_dq, full_cross_q))
    grad_first = grad_second + back_two[0]
    branch_one = grad_first.astype(BF)
    grad_mixed = nt(branch_one, full_self_out).astype(BF)
    middle = jnp.stack(
        [
            chip_first(pair_product(normed_two, cross_dq)),
            chip_first(pair_product(mixed, branch_one)),
        ],
        axis=1,
    )
    cross_part = joined(cross_part, me // 2, 0, cross_got).astype(BF)
    enc_heads = jnp.concatenate([cross_dk[:, :own], cross_dv[:, :own]], axis=1)
    kv_part = tn(all_encoder, enc_heads).astype(BF).reshape(groups, depth, 2 * own)
    ffn_sums = jnp.concatenate(
        [
            joined(in_sum, me // 4, 2, in_got),
            joined(out_sum, (me // 2) % (chips // 2), 2, out_got),
        ],
        axis=0,
    )
    ffn_sums = jnp.moveaxis(ffn_sums.astype(BF), 1, 0)
    carried = (middle, ffn_sums, cross_part, kv_part, late_first, late_second)
    moved, _, grad_head_in, column, *got = attend_backward(
        False, heads, scale, prompt_offsets, queries, keys, values, to_heads(grad_mixed),
        att_self, lse_self, carried,
        [(value.shape[0] - 1,) + value.shape[1:] for value in carried[:4]]
        + [value.shape for value in carried[4:]],
        (all_normed.reshape(ctx, row_count, width),),
    )
    grad_head_in = grad_head_in.reshape(width, 3, 128)[:, :, :own].reshape(width, 3 * own)
    column = column[0].reshape(3, 128)[:, :own].reshape(-1)
    zone = lax.axis_index("fsdp")
    middle = joined(middle, me // 2, 0, got[0]).astype(BF)
    ffn_sums, cross_part, kv_part = [
        joined(value, zone, 0, part_got).astype(BF)
        for value, part_got in zip(carried[1:4], got[1:4])
    ]
    other_first, other_second = got[4:]
    weight = head_in.reshape(width, 3 * own).astype(F32)
    grad_shift_one = jnp.sum(weight * column, axis=1)
    grad_gain_one = jnp.sum(weight * (grad_head_in - shift[0][:, None] * column), axis=1) / gain[0]

    def spread(value):
        return lax.dynamic_update_slice_in_dim(jnp.zeros((width,), F32), value, me * own, 0)

    totals = jnp.stack(
        [
            grad_gain_one, back_two[1], back_three[1],
            grad_shift_one, back_two[2], back_three[2],
            spread(column[:own]), spread(column[2 * own :]),
            jnp.sum(branch_one.astype(F32), axis=0),
            jnp.sum(cross_dq.astype(F32), axis=0),
            spread(jnp.sum(enc_heads[:, own:].astype(F32), axis=0)),
            jnp.sum(branch_two.astype(F32), axis=0),
            jnp.sum(dy, axis=0),
        ]
    )
    totals = jnp.moveaxis(totals.reshape(13, groups, shard), 1, 0).reshape(groups, -1)
    bias = jnp.moveaxis(bias_parts[:, 0].reshape(blocks, groups, depth), 0, 1)
    totals = jnp.concatenate([totals, bias.reshape(groups, -1)], axis=1)
    count = totals.shape[1]
    totals = jnp.pad(totals, ((0, 0), (0, 48 * own - count))).reshape(groups, 48, own)

    def by_lanes(value, rows):
        lead = value.shape[:-2]
        value = jnp.moveaxis(value.reshape(lead + (rows, -1, own)), -2, -3)
        return value.reshape(lead + (-1, own))

    middle = jnp.moveaxis(by_lanes(middle, part), 1, 0).reshape(groups, -1, own)
    late = by_lanes(grad_head_in.reshape(groups, depth, 3 * own), depth)
    late = jnp.concatenate([middle, late.astype(BF), totals.astype(BF)], axis=1)
    done = jnp.concatenate([by_lanes(cross_part, part), by_lanes(kv_part, depth)], axis=0)
    enc_sum = enc_heads.reshape(ctx, -1, 2 * own)
    more = ()
    if own == 128:
        more = (moved, enc_sum, late_first, late_second, other_first, other_second)
    all_ffn, all_done, all_late, *more_sums = finish(late, done, ffn_sums, width, more)
    if more:
        more = (more_sums[0], tokens, gain[:1], grad_first, more_sums[1])
    (
        grad_ffn_in, grad_ffn_out, grad_self_in, grad_cross_kv, grad_cross_out, grad_cross_q,
        grad_self_out, *more_grads,
    ) = place(all_ffn, all_done, all_late, ffn_in.shape[1], width, more)
    grad_ffn_out = grad_ffn_out.reshape(-1, width)
    sums = jnp.sum(all_late[:, -48:].astype(F32), axis=0).reshape(-1)[:count]
    mine, grad_ffn_bias = sums[: 13 * shard].reshape(13, shard), sums[13 * shard :]
    if more:
        input_grad, grad_encoder = more_grads
    else:

        late_mine = jnp.concatenate([late_first, late_second], axis=1)
        late_other = jnp.concatenate([other_first, other_second], axis=1)
        late_weights = both_cores(late_mine, late_other)
        cut = moved.reshape(ctx, row_count, 3, 128)[:, :, :, :own]
        grads = jnp.transpose(cut, (1, 2, 0, 3)).reshape(row_count, 3 * width)
        unit_one, scale_one = normalize(token_values)
        grad_normed = nt(grads, late_weights[:, : 3 * width])
        input_grad = grad_first + normalize_back(unit_one, scale_one, gain[0], grad_normed)[0]
        enc_sum = lax.all_to_all(enc_sum, "ctx", split_axis=0, concat_axis=0, tiled=True)
        enc_sum = jnp.transpose(enc_sum.reshape(ctx, -1, 2, own), (1, 2, 0, 3))
        grad_encoder = nt(enc_sum.reshape(-1, 2 * width), late_weights[:, 3 * width :])
    return (
        layer_out, input_grad, grad_encoder, mine[:3], mine[3:12], grad_self_in, grad_self_out,
        grad_cross_q, grad_cross_kv, grad_cross_out, grad_ffn_in, grad_ffn_bias, grad_ffn_out, mine[12],
    )


def solution(mesh):
    rows = P(("fsdp", "ctx"), None)
    shard = P("fsdp", None)
    thin = P(None, "fsdp")
    flat = P("fsdp")
    return jax.shard_map(
        body,
        mesh=mesh,
        in_specs=(
            rows, rows, shard, thin, thin, shard, shard, shard, shard, shard, shard, flat, shard,
            flat, rows,
        ),
        out_specs=(
            rows, rows, rows, thin, thin, shard, shard, shard, shard, shard, shard, flat, shard,
            flat,
        ),
        check_vma=False,
    )
```

```python
import functools
import math

import jax
import jax.numpy as jnp
from jax import lax
from jax.experimental import pallas as pl
from jax.experimental.pallas import tpu as pltpu
from jax.sharding import PartitionSpec as P

HEADS = 16
CONT = 2048
EPS = 1e-05
NEG = -1e30
TILE = 512
BF = jnp.bfloat16
F32 = jnp.float32
VMEM_BYTES = 56 * 2**20


def nn(left, right):
    return lax.dot_general(left, right, (((1,), (0,)), ((), ())), preferred_element_type=F32)


def nt(left, right):
    return lax.dot_general(left, right, (((1,), (1,)), ((), ())), preferred_element_type=F32)


def tn(left, right):
    return lax.dot_general(left, right, (((0,), (0,)), ((), ())), preferred_element_type=F32)


def normalize(values):
    center = values - jnp.mean(values, axis=-1, keepdims=True)
    scale = lax.rsqrt(jnp.mean(center * center, axis=-1, keepdims=True) + EPS)
    return center * scale, scale


def normalize_back(unit, scale, gain, grad):
    q = gain * grad
    back = scale * (
        q - jnp.mean(q, axis=-1, keepdims=True) - unit * jnp.mean(q * unit, axis=-1, keepdims=True)
    )
    return back, jnp.sum(grad * unit, axis=0), jnp.sum(grad, axis=0)


def head_lanes(head, array):
    lane = lax.broadcasted_iota(jnp.int32, array.shape, 1)
    keep = (lane < 64) if head == 0 else (lane >= 64)
    return jnp.where(keep, array, jnp.zeros_like(array))


def transposed(array):
    return array.astype(F32).T.astype(BF)


def visible(key_start, query_start, key_count, query_count, own_start, limit):
    key = key_start + lax.broadcasted_iota(jnp.int32, (key_count, query_count), 0)
    query = query_start + lax.broadcasted_iota(jnp.int32, (key_count, query_count), 1)
    shown = key <= query
    if limit is not None:
        shown = shown & ((key >= own_start) | (key < limit))
    return shown


def soften(scores, total, peak, value_t):
    old = peak[:1]
    new = jnp.maximum(old, jnp.max(scores, axis=0, keepdims=True))
    raised = jnp.exp(scores - new).astype(BF)
    total[...] = total[...] * jnp.exp(old - new) + nn(value_t, raised)
    peak[...] = jnp.broadcast_to(new, peak.shape)


def set_value_rows(value_t, head, columns, value):
    value_t[head, :64, columns] = value[64 * head : 64 * head + 64]
    value_t[head, 64:, columns] = jnp.ones((16, value.shape[1]), BF)


def tile_rows(tile):
    return pl.ds(pl.multiple_of(tile * TILE, TILE), TILE)


def flipped_bits(index, mask):
    out, bit = index, 1
    while bit <= mask:
        if mask & bit:
            out = out + bit - 2 * bit * ((index // bit) % 2)
        bit *= 2
    return out


def greet(peers):
    barrier = pltpu.get_barrier_semaphore()
    for peer in peers:
        pl.semaphore_signal(
            barrier, inc=1, device_id=peer, device_id_type=pl.DeviceIdType.MESH
        )
    pl.semaphore_wait(barrier, len(peers))


def others(axis):
    me, count = lax.axis_index(axis), lax.axis_size(axis)
    return [{axis: (me + step) % count} for step in range(1, count)]


def remote(source, target, send_sem, recv_sem, device):
    return pltpu.make_async_remote_copy(
        source, target, send_sem, recv_sem, device_id=device,
        device_id_type=pl.DeviceIdType.MESH,
    )


def exchange(source, target, send_sems, recv_sems, own_sem):
    me, count = lax.axis_index("ctx"), lax.axis_size("ctx")

    def copy(there, slot):
        return remote(
            source.at[there], target.at[slot], send_sems.at[there], recv_sems.at[slot],
            {"ctx": there},
        )

    def send(there):
        @pl.when(there != me)
        def _():
            copy(there, me).start()

        @pl.when(there == me)
        def _():
            pltpu.make_async_copy(source.at[me], target.at[me], own_sem).start()

    def arrived(there):
        @pl.when(there != me)
        def _():
            copy(there, there).wait_recv()

        @pl.when(there == me)
        def _():
            pltpu.make_async_copy(source.at[me], target.at[me], own_sem).wait()

    def sent():
        for step in range(1, count):
            copy((me + step) % count, me).wait_send()

    return send, arrived, sent


def plane_gather(source, store, send, recv):
    me = lax.axis_index("ctx")
    chips = lax.axis_size("ctx") // 2
    last = chips - 1
    sibling = flipped_bits(me, 1)
    near = [flipped_bits(me, 2 * other) for other in range(1, chips)]
    relay = chips == 4
    height = store.shape[1]
    cut = height // 2 if height < 32 else height // 32 * 16

    def own(index, there, block):
        return remote(source, store.at[block], send.at[index], recv.at[index], {"ctx": there})

    def passed(index, block):
        return remote(
            store.at[block], store.at[block], send.at[chips + index], recv.at[chips + index],
            {"ctx": sibling},
        )

    def half(part, there, block):
        rows = pl.ds(0, cut) if part == 0 else pl.ds(cut, height - cut)
        at = 2 * chips - 1 + part
        return remote(
            store.at[block, rows], store.at[block, rows], send.at[at], recv.at[at], {"ctx": there}
        )

    firsts = range(2) if relay else range(last)

    def start():
        for index in firsts:
            own(index, near[index], me).start()
        own(last, sibling, me).start()

    def land(index):
        block = near[index]
        if relay and index == 2:
            half(0, near[0], block).wait_recv()
            half(1, near[1], block).wait_recv()
        else:
            own(index, block, block).wait_recv()
            if relay:
                half(1 - index, near[1 - index], block).start()
        passed(index, block).start()
        return block

    def rest(index):
        if index == 0:
            own(last, sibling, sibling).wait_recv()
            return sibling
        block = flipped_bits(near[index - 1], 1)
        passed(index - 1, block).wait_recv()
        return block

    def done():
        for index in firsts:
            own(index, near[index], me).wait_send()
        own(last, sibling, me).wait_send()
        for index in range(last):
            passed(index, near[index]).wait_send()
        if relay:
            half(0, near[0], near[1]).wait_send()
            half(1, near[1], near[0]).wait_send()

    return start, land, rest, done


def attend_forward_kernel(cross, heads, conts, offs_ref, q_ref, k_ref, v_ref, *refs):
    if cross:
        rows_ref, mixed_ref, att_ref, lse_ref, q_out, rows_all, pair_all, *refs = refs
    else:
        pair_ref, enc_ref, kv_ref, *refs = refs
        mixed_ref, att_ref, lse_ref, pair_all, enc_all, kv_all, *refs = refs
    total, peak, value_t, score_a, score_b, stage, send_sem, recv_sem, own_sem, pair_sem, *refs = refs
    me, count = lax.axis_index("ctx"), lax.axis_size("ctx")
    rows = att_ref.shape[1]
    tiles = rows // TILE
    key_tiles = k_ref.shape[0] // TILE
    prompt = rows - conts * CONT
    prompt_tiles = prompt // TILE
    greet(others("ctx") + others("fsdp"))
    send, arrived, sent = exchange(stage, mixed_ref, send_sem, recv_sem, own_sem)
    zone = lax.axis_index("fsdp")
    pair_copy = core_swap(rows_all if cross else pair_ref, pair_all, pair_sem)
    if not cross:
        gather_send, gather_recv, gather_own, kv_send, kv_recv = refs
        enc_start, enc_land, enc_rest, enc_done = plane_gather(
            enc_ref, enc_all, gather_send, gather_recv
        )
        enc_start()
        first = group_spread(kv_ref, kv_all, kv_send, kv_recv, 0)
        local = [
            pltpu.make_async_copy(enc_ref, enc_all.at[me], gather_own.at[0]),
            pltpu.make_async_copy(kv_ref, kv_all.at[zone], gather_own.at[1]),
        ]
        for copy in first + local:
            copy.start()
    if cross:
        q_all, q_send, q_recv, q_own, rows_send, rows_recv = refs
        put, got, put_done = exchange(q_ref, q_all, q_send, q_recv, q_own)
        for step in range(count):
            put((me + step) % count)
        spread = group_spread(rows_ref, rows_all, rows_send, rows_recv, 0)
        keep_rows = pltpu.make_async_copy(rows_ref, rows_all.at[zone], pair_sem.at[2])
        for copy in spread + [keep_rows]:
            copy.start()
    else:
        pair_copy.start()

    for tile in range(key_tiles):
        at = pl.ds(tile * TILE, TILE)
        turned = transposed(v_ref[at, :])
        for head in range(heads):
            set_value_rows(value_t, head, at, turned)

    def query_tile(step, carry):
        if cross:
            i = (me + step) % count
            got(i)
            q = q_all[i]
            q_out[i] = q
        else:
            i = (me + 1 + step) % count
            q = q_ref[tile_rows(i), :]
        masked = [head_lanes(head, q) for head in range(heads)]
        total[...] = jnp.zeros_like(total)
        peak[...] = jnp.full_like(peak, NEG)

        def score(j, target):
            k = k_ref[tile_rows(j), :]
            for head in range(heads):
                target[head] = nt(k, masked[head])

        def soft(j, source, shown=None):
            for head in range(heads):
                scores = source[head]
                if shown is not None:
                    scores = jnp.where(shown, scores, NEG)
                soften(
                    scores, total.at[head], peak.at[head], value_t[head, :, tile_rows(j)]
                )

        if cross:
            both = (score_a, score_b)
            score(0, score_a)
            for j in range(key_tiles):
                if j + 1 < key_tiles:
                    score(j + 1, both[(j + 1) % 2])
                soft(j, both[j % 2])
        elif conts == 1:
            score(i, score_a)
            diagonal = visible(0, 0, TILE, TILE, 0, None)

            @pl.when(i > 0)
            def _():
                score(i - 1, score_b)
                soft(i, score_a, diagonal)

            @pl.when(i == 0)
            def _():
                soft(i, score_a, diagonal)

            def two(t, carry):
                j = i - 1 - 2 * t
                score(jnp.maximum(j - 1, 0), score_a)
                soft(j, score_b)
                score(jnp.maximum(j - 2, 0), score_b)
                soft(j - 1, score_a)
                return carry

            lax.fori_loop(0, i // 2, two, 0)

            @pl.when(i % 2 == 1)
            def _():
                soft(0, score_b)
        else:
            cont = jnp.maximum(i * TILE - prompt, 0) // CONT
            inside = i * TILE < prompt
            own = jnp.where(inside, 0, prompt + cont * CONT)
            limit = offs_ref[0, cont]

            def one(j, carry):
                score(j, score_a)
                soft(j, score_a, visible(j * TILE, i * TILE, TILE, TILE, own, limit))
                return carry

            lax.fori_loop(jnp.where(inside, 0, own // TILE), i + 1, one, 0)
            lax.fori_loop(0, jnp.where(inside, 0, prompt_tiles), one, 0)

        for head in range(heads):
            part = total[head]
            att_ref[64 * head : 64 * head + 64, tile_rows(i)] = part[:64] / part[64:65]
            lse_ref[head : head + 1, tile_rows(i)] = peak[head][:1] + jnp.log(part[64:65])
        stage[i] = att_ref[:, tile_rows(i)].T.astype(BF)
        send(i)
        if cross:

            @pl.when(step == tiles - 2)
            def _():
                keep_rows.wait()
                for copy in spread:
                    copy.wait_recv()
                pair_copy.start()

        else:

            @pl.when(step == tiles - 3)
            def _():
                for index in range(min(2, count // 2 - 1)):
                    enc_land(index)

        return carry

    if heads < 2:
        att_ref[...] = jnp.zeros_like(att_ref)
    lax.fori_loop(0, tiles, query_tile, 0)
    for step in range(count):
        arrived((me + step) % count)
    sent()
    pair_copy.wait()
    if cross:
        put_done()
        for copy in spread:
            copy.wait_send()
    else:
        for index in range(2, count // 2 - 1):
            enc_land(index)
        for index in range(count // 2):
            enc_rest(index)
        for copy in first:
            copy.wait_send()
            copy.wait_recv()
        for copy in local:
            copy.wait()
        enc_done()


def chain_spread(source, target, send, recv):
    zone, groups = lax.axis_index("fsdp"), lax.axis_size("fsdp")

    def copy(way, stage):
        step = 1 - 2 * way
        block = jnp.clip(zone - step * stage, 0, groups - 1)
        at = way * groups + stage
        return remote(
            source if stage == 0 else target.at[block], target.at[block],
            send.at[at], recv.at[at], {"fsdp": jnp.clip(zone + step, 0, groups - 1)},
        )

    def arrival(way, stage):
        step = 1 - 2 * way
        block = jnp.clip(zone - step * (stage + 1), 0, groups - 1)
        at = way * groups + stage
        return remote(
            target.at[block], target.at[block], send.at[at], recv.at[at],
            {"fsdp": jnp.clip(zone + step, 0, groups - 1)},
        )

    def sends(way, stage):
        return (zone + 1 < groups) & (zone >= stage) if way == 0 else (
            (zone > 0) & (zone + stage < groups)
        )

    def comes(way, stage):
        return zone >= stage + 1 if way == 0 else zone + stage + 1 < groups

    def send_all(stage):
        for way in range(2):

            @pl.when(sends(way, stage))
            def _():
                copy(way, stage).start()

    def wait_all(stage):
        for way in range(2):

            @pl.when(comes(way, stage))
            def _():
                arrival(way, stage).wait_recv()

    def start():
        send_all(0)

    def advance(stage):
        wait_all(stage - 1)
        send_all(stage)

    def finish():
        wait_all(groups - 2)
        for stage in range(groups - 1):
            for way in range(2):

                @pl.when(sends(way, stage))
                def _():
                    copy(way, stage).wait_send()

    return start, advance, finish


def core_swap(source, target, sems):
    there = {"ctx": flipped_bits(lax.axis_index("ctx"), 1)}
    return remote(source, target, sems.at[0], sems.at[1], there)


def group_spread(source, target, send_sem, recv_sem, sem):
    zone, groups = lax.axis_index("fsdp"), lax.axis_size("fsdp")
    return [
        remote(
            source, target.at[zone], send_sem.at[sem + shift - 1], recv_sem.at[sem + shift - 1],
            {"fsdp": (zone + shift) % groups},
        )
        for shift in range(1, groups)
    ]


def attend_forward(cross, heads, offsets, q, k, v, extra=()):
    count = lax.axis_size("ctx")
    rows = count * TILE
    vmem = pl.BlockSpec(memory_space=pltpu.VMEM)
    hbm = pl.BlockSpec(memory_space=pl.ANY)
    dma = pltpu.SemaphoreType.DMA
    tiles = jax.ShapeDtypeStruct((count, TILE, 128), BF)
    outs = [
        tiles,
        jax.ShapeDtypeStruct((128, rows), F32),
        jax.ShapeDtypeStruct((8, rows), F32),
    ]
    scratch = [
        pltpu.VMEM((heads, 80, TILE), F32),
        pltpu.VMEM((heads, 8, TILE), F32),
        pltpu.VMEM((heads, 80, k.shape[0]), BF),
        pltpu.VMEM((heads, TILE, TILE), F32),
        pltpu.VMEM((heads, TILE, TILE), F32),
        pltpu.VMEM((count, TILE, 128), BF),
        dma((count,)), dma((count,)), dma, dma((3,)),
    ]
    groups = lax.axis_size("fsdp")
    if cross:
        spread = jax.ShapeDtypeStruct((groups,) + extra[0].shape, BF)
        outs += [tiles, spread, spread]
        scratch += [pltpu.VMEM((count, TILE, 128), BF), dma((count,)), dma((count,)), dma]
        scratch += [dma((groups - 1,)), dma((groups - 1,))]
        places = [vmem, hbm, hbm]
    else:
        near, enc, kv = extra
        outs.append(jax.ShapeDtypeStruct(near.shape, BF))
        outs.append(jax.ShapeDtypeStruct((count,) + enc.shape, BF))
        outs.append(jax.ShapeDtypeStruct((groups,) + kv.shape, BF))
        scratch += [dma((count + 1,)), dma((count + 1,)), dma((2,))]
        scratch += [dma((groups - 1,)), dma((groups - 1,))]
        places = [hbm] * 3
    return pl.pallas_call(
        functools.partial(attend_forward_kernel, cross, heads, offsets.shape[1]),
        out_shape=outs,
        in_specs=[pl.BlockSpec(memory_space=pltpu.SMEM), vmem, vmem, vmem] + [hbm] * len(extra),
        out_specs=[hbm, vmem, vmem] + places,
        scratch_shapes=scratch,
        compiler_params=pltpu.CompilerParams(
            vmem_limit_bytes=VMEM_BYTES, collective_id=2 if cross else 1,
            has_side_effects=True,
        ),
        cost_estimate=pl.CostEstimate(
            flops=40 * 10**9, bytes_accessed=2**23, transcendentals=2**24
        ),
    )(offsets, q, k, v, *extra)


def rest_copies(sources, targets, send_sem, recv_sem):
    me = lax.axis_index("ctx")
    chips = lax.axis_size("ctx") // 2
    half = chips // 2
    out = []
    for other in range(1, half):
        for part in range(2):
            mine = me // 4 if part == 0 else (me // 2) % half
            sem = len(out)
            out.append(
                remote(
                    sources[part].at[:, :, flipped_bits(mine, other)],
                    targets[part].at[other - 1],
                    send_sem.at[sem], recv_sem.at[sem],
                    {"ctx": flipped_bits(me, (4 if part == 0 else 2) * other)},
                )
            )
    return out + chip_copies(sources[2], targets[2], send_sem, recv_sem, len(out))


def chip_copies(source, target, send_sem, recv_sem, sem):
    me = lax.axis_index("ctx")
    return [
        remote(
            source.at[flipped_bits(me // 2, other)], target.at[other - 1],
            send_sem.at[sem + other - 1], recv_sem.at[sem + other - 1],
            {"ctx": flipped_bits(me, 2 * other)},
        )
        for other in range(1, lax.axis_size("ctx") // 2)
    ]


def group_copies(source, target, send_sem, recv_sem, sem):
    zone, groups = lax.axis_index("fsdp"), lax.axis_size("fsdp")
    return [
        remote(
            source.at[(zone + shift) % groups], target.at[shift - 1],
            send_sem.at[sem + shift - 1], recv_sem.at[sem + shift - 1],
            {"fsdp": (zone + shift) % groups},
        )
        for shift in range(1, groups)
    ]


def last_copies(sources, targets, send_sem, recv_sem):
    out = chip_copies(sources[0], targets[0], send_sem, recv_sem, 0)
    for source, target in zip(sources[1:4], targets[1:4]):
        out = out + group_copies(source, target, send_sem, recv_sem, len(out))
    return out


def attend_backward_kernel(
    cross, heads, conts, scale, carried, number, offs_ref, q_ref, k_ref, v_ref, do_ref, att_ref,
    lse_ref, *refs,
):
    sources, refs = refs[:number], refs[number:]
    if not cross:
        normed_ref, *refs = refs
    if cross:
        moved_ref, dk_ref, dv_ref, *refs = refs
    else:
        moved_ref, stage, product_ref, column_ref, *refs = refs
    targets, refs = refs[:number], refs[number:]
    if cross:
        stage, *refs = refs
    (
        do_all, key_t, delta, dq_sum, dk_sum, dv_sum, score_a, score_b, grad_a, grad_b,
        send_sem, recv_sem, own_sem, do_send, do_recv, do_own, carry_send, carry_recv, *refs,
    ) = refs
    if cross:
        keep_sem, chain_send, chain_recv = refs
        chain_start, chain_advance, chain_finish = chain_spread(
            sources[3], targets[3], chain_send, chain_recv
        )
        keep_own = pltpu.make_async_copy(
            sources[3], targets[3].at[lax.axis_index("fsdp")], keep_sem
        )
    else:
        normed, normed_sem, *pair_sems = refs
        pair_copies = [
            core_swap(sources[4 + index], targets[4 + index], pair_sems[index])
            for index in range(2)
        ]
        product_ref[...] = jnp.zeros_like(product_ref)
        column_ref[...] = jnp.zeros_like(column_ref)
    me, count = lax.axis_index("ctx"), lax.axis_size("ctx")
    tiles = count
    key_tiles = k_ref.shape[0] // TILE
    prompt = tiles * TILE - conts * CONT
    greet(others("ctx") + others("fsdp"))
    put, got, put_done = exchange(do_ref, do_all, do_send, do_recv, do_own)
    for step in range(count):
        put((me + step) % count)
    carry_copies = carried(sources, targets, carry_send, carry_recv)
    for copy in carry_copies:
        copy.start()
    if cross:
        chain_start()
        keep_own.start()
    else:
        for copy in pair_copies:
            copy.start()
    send, arrived, sent = exchange(stage, moved_ref, send_sem, recv_sem, own_sem)
    dq_sum[...] = jnp.zeros_like(dq_sum)
    dk_sum[...] = jnp.zeros_like(dk_sum)
    dv_sum[...] = jnp.zeros_like(dv_sum)
    for tile in range(key_tiles):
        at = pl.ds(tile * TILE, TILE)
        key_t[:, at] = transposed(k_ref[at, :])

    def ready(i):
        got(i)
        both = do_all[i].astype(F32).T * att_ref[:, tile_rows(i)]
        for head in range(heads):
            delta[head : head + 1, tile_rows(i)] = jnp.sum(
                both[64 * head : 64 * head + 64], axis=0, keepdims=True
            )

    def score(i, j, kept):
        row, at = tile_rows(i), tile_rows(j)
        q, do, k, v = q_ref[row, :], do_all[i], k_ref[at, :], v_ref[at, :]
        for head in range(heads):
            kept[0][head] = nt(k, head_lanes(head, q))
            kept[1][head] = nt(v, head_lanes(head, do))

    def settle(i, j, kept, shown=None):
        row, at = tile_rows(i), tile_rows(j)
        q, do = q_ref[row, :], do_all[i]
        for head in range(heads):
            weights = jnp.exp(kept[0][head] - lse_ref[head : head + 1, row])
            if shown is not None:
                weights = jnp.where(shown, weights, 0.0)
            score_grad = weights * (kept[1][head] - delta[head : head + 1, row])
            score_grad = score_grad.astype(BF)
            dv_sum[at, :] += nn(weights.astype(BF), head_lanes(head, do))
            dk_sum[at, :] += nn(score_grad, head_lanes(head, q))
            own = slice(64 * head, 64 * head + 64)
            dq_sum[own, row] += nn(key_t[own, at], score_grad)

    even, odd = (score_a, grad_a), (score_b, grad_b)

    def shown_of(i, j):
        if conts == 1:
            return None
        cont = jnp.maximum(i * TILE - prompt, 0) // CONT
        own = jnp.where(i * TILE < prompt, 0, prompt + cont * CONT)
        return visible(j * TILE, i * TILE, TILE, TILE, own, offs_ref[0, cont])

    def queries_back(i):
        return (dq_sum[:, tile_rows(i)].T.astype(BF).astype(F32) * scale).astype(BF)

    def cross_tile(step, carry):
        i = (me + step) % count
        ready(i)

        for hop in range(1, min(3, lax.axis_size("fsdp") - 1)):

            @pl.when(step == 2 * hop + 1)
            def _():
                chain_advance(hop)

        both = (even, odd)
        score(i, 0, even)
        for j in range(key_tiles):
            if j + 1 < key_tiles:
                score(i, j + 1, both[(j + 1) % 2])
            settle(i, j, both[j % 2])
        stage[i] = queries_back(i)
        send(i)
        return carry

    def self_tile(step, carry):
        i = (me + 1 + step) % count
        fetch = pltpu.make_async_copy(normed_ref.at[i], normed, normed_sem)
        fetch.start()

        def tiles_of(turn):
            p = (i + turn) % count
            return jnp.maximum(i, p), jnp.minimum(i, p)

        def score_turn(turn, kept):
            high, low = tiles_of(turn)
            score(high, low, kept)

        def settle_turn(turn, kept):
            high, low = tiles_of(turn)
            settle(high, low, kept, shown_of(high, low))

        diagonal = visible(0, 0, TILE, TILE, 0, None) if conts == 1 else shown_of(i, i)
        left = count - 1 - step

        @pl.when(step == 0)
        def _():
            ready(i)
            score(i, i, even)
            settle(i, i, even, diagonal)

            def fresh(turn, carry):
                ready((i + turn) % count)
                score_turn(turn, even)
                settle_turn(turn, even)
                return carry

            lax.fori_loop(1, count, fresh, 0)

        @pl.when(step > 0)
        def _():
            score(i, i, even)

            @pl.when(left > 0)
            def _():
                score_turn(1, odd)
                settle(i, i, even, diagonal)

            @pl.when(left == 0)
            def _():
                settle(i, i, even, diagonal)

            def two(turn, carry):
                at = 1 + 2 * turn
                score_turn(at + 1, even)
                settle_turn(at, odd)
                score_turn(at + 2, odd)
                settle_turn(at + 1, even)
                return carry

            lax.fori_loop(0, jnp.maximum(left - 1, 0) // 2, two, 0)

            @pl.when(left % 2 == 1)
            def _():
                settle_turn(left, odd)

            @pl.when((left > 0) & (left % 2 == 0))
            def _():
                score_turn(left, even)
                settle_turn(left - 1, odd)
                settle_turn(left, even)

        stage[i, :, :128] = queries_back(i)
        stage[i, :, 128:256] = dk_sum[tile_rows(i), :].astype(BF)
        stage[i, :, 256:] = dv_sum[tile_rows(i), :].astype(BF)
        send(i)
        fetch.wait()
        grads = stage[i]
        product_ref[...] += tn(normed[...], grads)
        column_ref[...] += jnp.broadcast_to(
            jnp.sum(grads.astype(F32), axis=0, keepdims=True), column_ref.shape
        )
        return carry

    lax.fori_loop(0, tiles, cross_tile if cross else self_tile, 0)
    if cross:
        dk_ref[...] = dk_sum[...].astype(BF)
        dv_ref[...] = dv_sum[...].astype(BF)
    for step in range(count):
        arrived((me + step) % count)
    sent()
    put_done()
    if cross:
        keep_own.wait()
        for hop in range(3, lax.axis_size("fsdp") - 1):
            chain_advance(hop)
        chain_finish()
    else:
        for copy in pair_copies:
            copy.wait()
    for copy in carry_copies:
        copy.wait_send()
        copy.wait_recv()


def attend_backward(
    cross, heads, scale, offsets, q, k, v, do, att, lse, sources, target_shapes, normed=()
):
    count = lax.axis_size("ctx")
    vmem = pl.BlockSpec(memory_space=pltpu.VMEM)
    hbm = pl.BlockSpec(memory_space=pl.ANY)
    dma = pltpu.SemaphoreType.DMA
    keys = k.shape[0]
    wide = 128 if cross else 384
    moved = jax.ShapeDtypeStruct((count, TILE, wide), BF)
    if cross:
        local = [jax.ShapeDtypeStruct((keys, 128), BF)] * 2
        carries = 2 * (count // 4 - 1) + count // 2 - 1
    else:
        local = [
            jax.ShapeDtypeStruct((count, TILE, wide), BF),
            jax.ShapeDtypeStruct((normed[0].shape[2], wide), F32),
            jax.ShapeDtypeStruct((8, wide), F32),
        ]
        carries = count // 2 - 1 + (lax.axis_size("fsdp") - 1) * 3
    targets = [jax.ShapeDtypeStruct(shape, BF) for shape in target_shapes]
    return pl.pallas_call(
        functools.partial(
            attend_backward_kernel, cross, heads, offsets.shape[1], scale,
            rest_copies if cross else last_copies, len(sources),
        ),
        out_shape=[moved] + local + targets,
        in_specs=[pl.BlockSpec(memory_space=pltpu.SMEM)] + [vmem] * 6
        + [hbm] * (len(sources) + len(normed)),
        out_specs=[hbm] + [vmem] * len(local) + [hbm] * len(sources),
        scratch_shapes=([pltpu.VMEM((count, TILE, wide), BF)] if cross else [])
        + [
            pltpu.VMEM((count, TILE, 128), BF),
            pltpu.VMEM((128, keys), BF),
            pltpu.VMEM((8, count * TILE), F32),
            pltpu.VMEM((128, count * TILE), F32),
            pltpu.VMEM((keys, 128), F32),
            pltpu.VMEM((keys, 128), F32),
        ]
        + [pltpu.VMEM((heads, TILE, TILE), F32)] * 4
        + [
            dma((count,)), dma((count,)), dma,
            dma((count,)), dma((count,)), dma,
            dma((carries,)), dma((carries,)),
        ]
        + ([dma] + [dma((2 * lax.axis_size("fsdp"),))] * 2 if cross else [pltpu.VMEM(normed[0].shape[1:], BF), dma, dma((2,)), dma((2,))]),
        compiler_params=pltpu.CompilerParams(
            vmem_limit_bytes=VMEM_BYTES, collective_id=3 if cross else 4,
            has_side_effects=True,
        ),
        cost_estimate=pl.CostEstimate(
            flops=60 * 10**9, bytes_accessed=2**23, transcendentals=2**24
        ),
    )(offsets, q, k, v, do, att, lse, *sources, *normed)


def project_kernel(
    own, scale, tokens_ref, small_ref, head_ref, rows_ref, normed_ref, q_ref, k_ref, v_ref,
    small_all, head_all, rows_all, all_tokens, staged, token_send, token_recv, part_send, part_recv,
    own_sem, stage_sem, rows_send, rows_recv,
):
    me, zone = lax.axis_index("ctx"), lax.axis_index("fsdp")
    count, groups = lax.axis_size("ctx"), lax.axis_size("fsdp")
    chips = count // 2
    chain_start, chain_advance, chain_finish = chain_spread(
        rows_ref, rows_all, rows_send, rows_recv
    )
    keep_rows = pltpu.make_async_copy(rows_ref, rows_all.at[zone], own_sem.at[3])
    shard = small_ref.shape[1]
    sibling = {"ctx": flipped_bits(me, 1)}
    near = [flipped_bits(me, 2 * other) for other in range(1, chips)]
    greet([sibling] + [{"ctx": there} for there in near] + others("fsdp"))

    parts = []
    for shift in range(1, groups):
        there = {"fsdp": (zone + shift) % groups}
        for index, (source, target) in enumerate(((small_ref, small_all), (head_ref, head_all))):
            parts.append(
                remote(source, target.at[zone], part_send.at[index, shift - 1],
                       part_recv.at[index, shift - 1], there)
            )
    local = [
        pltpu.make_async_copy(small_ref, small_all.at[zone], own_sem.at[0]),
        pltpu.make_async_copy(head_ref, head_all.at[zone], own_sem.at[1]),
        pltpu.make_async_copy(tokens_ref, all_tokens.at[me], own_sem.at[2]),
    ]
    for copy in local:
        copy.start()
    for copy in parts:
        copy.start()

    start, land, rest, done = plane_gather(tokens_ref, all_tokens, token_send, token_recv)
    start()
    chain_start()
    keep_rows.start()
    for copy in local:
        copy.wait()
    for copy in parts:
        copy.wait_recv()

    def row(index):
        pieces = [small_all[z].astype(F32)[index : index + 1] for z in range(groups)]
        return jnp.concatenate(pieces, axis=1)

    gain, shift = row(0), row(3)
    mine = small_all[me // (shard // own)].astype(F32)
    q_shift = jnp.where(me % 2 == 0, mine[6:7, :own], mine[6:7, own : 2 * own])
    v_shift = jnp.where(me % 2 == 0, mine[7:8, :own], mine[7:8, own : 2 * own])
    if own < 128:
        for ref in (q_ref, k_ref, v_ref):
            ref[...] = jnp.zeros_like(ref)

    def save(block, place):
        return pltpu.make_async_copy(staged.at[place], normed_ref.at[block], stage_sem.at[place])

    order, ready = [], []
    for step in range(count):
        place = step % 2
        if step in (2, 4) and step // 2 <= groups - 2:
            chain_advance(step // 2)
        if step == 0:
            ready.append(me)
        elif step == 1:
            ready.append(rest(0))
        elif step == 2:
            for index in range(min(2, chips - 1)):
                ready.append(land(index))
        elif len(ready) == step:
            index = step - chips - 1
            if step == 4 and chips == 4:
                ready += [rest(1), rest(2)]
            elif step == 6 and chips == 4:
                ready.append(land(2))
            elif chips == 4:
                ready.append(rest(3))
            else:
                ready.append(land(step - 2) if step <= chips else rest(index + 1))
        block = ready[step]
        order.append(block)
        if step >= 2:
            save(order[step - 2], place).wait()
        unit, _ = normalize(all_tokens[block].astype(F32))
        staged[place] = (unit * gain + shift).astype(BF)
        save(block, place).start()
        total = jnp.zeros((staged.shape[1], 3 * own), F32)
        for z in range(groups):
            total = total + nn(staged[place, :, z * shard : z * shard + shard], head_all[z])
        q_ref[block, :, :own] = (scale * (total[:, :own] + q_shift)).astype(BF)
        k_ref[block, :, :own] = total[:, own : 2 * own].astype(BF)
        v_ref[block, :, :own] = (total[:, 2 * own :] + v_shift).astype(BF)
    for step in (count - 2, count - 1):
        save(order[step], step % 2).wait()
    for copy in parts:
        copy.wait_send()
    keep_rows.wait()
    for stage in range(3, groups - 1):
        chain_advance(stage)
    chain_finish()
    done()


def project(own, scale, tokens, small, head_in, rows_part):
    count, groups = lax.axis_size("ctx"), lax.axis_size("fsdp")
    rows, width = tokens.shape
    vmem = pl.BlockSpec(memory_space=pltpu.VMEM)
    hbm = pl.BlockSpec(memory_space=pl.ANY)
    dma = pltpu.SemaphoreType.DMA
    lanes = jax.ShapeDtypeStruct((count, rows, 128), BF)
    return pl.pallas_call(
        functools.partial(project_kernel, own, scale),
        out_shape=(
            jax.ShapeDtypeStruct((count, rows, width), BF),
            lanes, lanes, lanes,
            jax.ShapeDtypeStruct((groups,) + small.shape, BF),
            jax.ShapeDtypeStruct((groups,) + head_in.shape, BF),
            jax.ShapeDtypeStruct((groups,) + rows_part.shape, BF),
        ),
        in_specs=[hbm, hbm, hbm, hbm],
        out_specs=(hbm,) + (vmem,) * 5 + (hbm,),
        scratch_shapes=[
            pltpu.VMEM((count, rows, width), BF),
            pltpu.VMEM((2, rows, width), BF),
            dma((count + 1,)), dma((count + 1,)),
            dma((2, groups - 1)), dma((2, groups - 1)),
            dma((4,)), dma((2,)), dma((2 * groups,)), dma((2 * groups,)),
        ],
        compiler_params=pltpu.CompilerParams(
            vmem_limit_bytes=VMEM_BYTES, collective_id=5, has_side_effects=True
        ),
        cost_estimate=pl.CostEstimate(
            flops=50 * 10**9, bytes_accessed=2**25, transcendentals=0
        ),
    )(tokens, small, head_in, rows_part)


def ffn_kernel(
    steps, groups, n_ref, dy_ref, base_ref, bias_ref, win_ref, wout_ref, rows_ref,
    out_ref, gn_ref, gb_ref, in_ref, sum_ref, rows_all,
    n_t, own_in, own_out, post_in, post_out, got_in, got_out,
    keep_in, keep_out, flow_in, flow_out, near_in, near_out,
    send_sem, recv_sem, flow_send, flow_recv, save_sem, rows_send, rows_recv, rows_own,
):
    f = pl.program_id(0)
    spread = group_spread(rows_ref, rows_all, rows_send, rows_recv, 0)
    keep_rows = pltpu.make_async_copy(
        rows_ref, rows_all.at[lax.axis_index("fsdp")], rows_own
    )
    me = lax.axis_index("ctx")
    count = lax.axis_size("ctx")
    chips = count // 2
    core = me % 2
    low_bit = (me // 2) % 2
    high_bit = me // chips
    cols = keep_in.shape[2]
    slot = f % 2
    sibling = {"ctx": flipped_bits(me, 1)}
    low = {"ctx": flipped_bits(me, 2)}
    high = {"ctx": flipped_bits(me, chips)}

    def copies(step, place):
        return (
            remote(post_in.at[place], got_in.at[step], send_sem.at[0, place],
                   recv_sem.at[0, step], sibling),
            remote(post_out.at[place], got_out.at[step], send_sem.at[1, place],
                   recv_sem.at[1, step], sibling),
        )

    def flows(step, place):
        return (
            remote(flow_in.at[place], near_in.at[step], flow_send.at[0, place],
                   flow_recv.at[0, step], low),
            remote(flow_out.at[place], near_out.at[step], flow_send.at[1, place],
                   flow_recv.at[1, step], high),
        )

    @pl.when(f == 0)
    def _():
        greet([sibling, low, high] + others("fsdp"))
        for copy in spread:
            copy.start()
        keep_rows.start()
        n_t[...] = transposed(n_ref[...])
        gn_ref[...] = jnp.zeros_like(gn_ref)
        out_ref[...] = base_ref[...]

    @pl.when(f < steps)
    def _():
        @pl.when(f >= 2)
        def _():
            for copy in copies(jnp.maximum(f - 2, 0), slot):
                copy.wait_send()

        pre = nn(n_ref[...], win_ref[...]) + bias_ref[0, :1]
        below = 0.5 * (1.0 + lax.erf(pre * (1.0 / math.sqrt(2.0))))
        hidden = (pre * below).astype(BF)
        out_ref[...] += nn(hidden, wout_ref[...])
        slope = below + pre * (jnp.exp(-0.5 * pre * pre) * (1.0 / math.sqrt(2.0 * math.pi)))
        dy = dy_ref[...]
        grad_pre = (nt(dy, wout_ref[...]) * slope).astype(BF)
        gb_ref[0] = jnp.broadcast_to(
            jnp.sum(grad_pre.astype(F32), axis=0, keepdims=True), gb_ref.shape[1:]
        )
        gn_ref[...] += nt(grad_pre, win_ref[...])

        def split(part, keep, post, half):
            left, right = part[:, :half], part[:, half:]
            keep[slot] = jnp.where(core == 0, left, right)
            post[slot] = jnp.where(core == 0, right, left).astype(BF)

        first, second = copies(jnp.minimum(f, steps - 1), slot)
        split(nn(n_t[...], grad_pre), own_in, post_in, cols)
        first.start()
        split(tn(hidden, dy), own_out, post_out, 2 * cols)
        second.start()

    @pl.when(f > 0)
    def _():
        past = jnp.maximum(f - 1, 0)
        place = (f + 1) % 2
        for copy in copies(past, place):
            copy.wait_recv()

        @pl.when(f >= 3)
        def _():
            for copy in flows(jnp.maximum(f - 3, 0), place):
                copy.wait_send()

        unit = keep_in.shape[1] // (groups * (chips // 2))
        for slab in range(groups * (chips // 2)):
            for kept in (True, False):
                take = low_bit if kept else 1 - low_bit
                rows = pl.ds(pl.multiple_of((2 * slab + take) * unit, unit), unit)
                both = own_in[place, rows, :] + got_in[past, rows, :].astype(F32)
                at = slice(unit * slab, unit * slab + unit)
                if kept:
                    keep_in[past, at, :] = both.astype(BF)
                else:
                    flow_in[place, at, :] = both.astype(BF)
        unit = n_t.shape[0] // groups // 2
        for slab in range(own_out.shape[1] // (2 * unit)):
            for kept in (True, False):
                take = high_bit if kept else 1 - high_bit
                rows = pl.ds(pl.multiple_of((2 * slab + take) * unit, unit), unit)
                both = own_out[place, rows, :] + got_out[past, rows, :].astype(F32)
                at = slice(unit * slab, unit * slab + unit)
                for half in range(2):
                    value = both[:, half * cols : half * cols + cols].astype(BF)
                    if kept:
                        keep_out[past, half, at, :] = value
                    else:
                        flow_out[place, half, at, :] = value
        for copy in flows(past, place):
            copy.start()

    @pl.when(f == steps)
    def _():
        for back in (2, 1):
            for copy in copies(steps - back, (steps - back) % 2):
                copy.wait_send()
            for copy in flows(steps - back, (steps - back) % 2):
                copy.wait_send()
        per = steps // sum_ref.shape[0]
        height = keep_out.shape[2]

        def saves(step):
            rows = pl.ds(pl.multiple_of((step % per) * height, height), height)
            return (
                pltpu.make_async_copy(
                    keep_in.at[step], in_ref.at[step], save_sem.at[0, step]
                ),
                pltpu.make_async_copy(
                    keep_out.at[step], sum_ref.at[step // per, :, rows], save_sem.at[1, step]
                ),
            )

        def join(step, carry):
            for copy in flows(step, step % 2):
                copy.wait_recv()
            keep_in[step] = (
                keep_in[step].astype(F32) + near_in[step].astype(F32)
            ).astype(BF)
            keep_out[step] = (
                keep_out[step].astype(F32) + near_out[step].astype(F32)
            ).astype(BF)
            for copy in saves(step):
                copy.start()
            return carry

        def saved(step, carry):
            for copy in saves(step):
                copy.wait()
            return carry

        lax.fori_loop(0, steps, join, 0)
        lax.fori_loop(0, steps, saved, 0)
        keep_rows.wait()
        for copy in spread:
            copy.wait_send()
            copy.wait_recv()


def ffn(normed, dy, base, bias, weights, rows_part):
    rows, width = normed.shape
    hidden = weights.shape[1] // 2
    groups = lax.axis_size("fsdp")
    step = 512
    cols = step // 2
    steps = hidden // step
    per = width // step
    last = steps - 1

    def now(f):
        return jnp.minimum(f, last)

    whole = lambda f: (0, 0)
    hbm = pl.BlockSpec(memory_space=pl.ANY)
    dma = pltpu.SemaphoreType.DMA
    once = pl.BlockSpec((rows, width), whole, pipeline_mode=pl.Buffered(1))
    return pl.pallas_call(
        functools.partial(ffn_kernel, steps, groups),
        grid=(steps + 1,),
        out_shape=(
            jax.ShapeDtypeStruct((rows, width), F32),
            jax.ShapeDtypeStruct((rows, width), F32),
            jax.ShapeDtypeStruct((steps, 8, step), F32),
            jax.ShapeDtypeStruct((steps, width // 2, cols), BF),
            jax.ShapeDtypeStruct((hidden // width, 2, width // 2, cols), BF),
            jax.ShapeDtypeStruct((groups,) + rows_part.shape, BF),
        ),
        in_specs=[
            once, once, once,
            pl.BlockSpec((1, 8, step), lambda f: (now(f), 0, 0)),
            pl.BlockSpec((width, step), lambda f: (0, now(f))),
            pl.BlockSpec(
                (step, width), lambda f: (now(f) % per, hidden // width + now(f) // per)
            ),
            hbm,
        ],
        out_specs=(
            pl.BlockSpec((rows, width), whole),
            pl.BlockSpec((rows, width), whole),
            pl.BlockSpec((1, 8, step), lambda f: (now(f), 0, 0)),
            hbm, hbm, hbm,
        ),
        scratch_shapes=[
            pltpu.VMEM((width, rows), BF),
            pltpu.VMEM((2, width, cols), F32),
            pltpu.VMEM((2, step, 2 * cols), F32),
            pltpu.VMEM((2, width, cols), BF),
            pltpu.VMEM((2, step, 2 * cols), BF),
            pltpu.VMEM((steps, width, cols), BF),
            pltpu.VMEM((steps, step, 2 * cols), BF),
            pltpu.VMEM((steps, width // 2, cols), BF),
            pltpu.VMEM((steps, 2, step // 2, cols), BF),
            pltpu.VMEM((2, width // 2, cols), BF),
            pltpu.VMEM((2, 2, step // 2, cols), BF),
            pltpu.VMEM((steps, width // 2, cols), BF),
            pltpu.VMEM((steps, 2, step // 2, cols), BF),
            dma((2, 2)), dma((2, steps)), dma((2, 2)), dma((2, steps)), dma((2, steps)),
            dma((groups - 1,)), dma((groups - 1,)), dma,
        ],
        compiler_params=pltpu.CompilerParams(
            vmem_limit_bytes=60 * 2**20, collective_id=0, has_side_effects=True
        ),
        cost_estimate=pl.CostEstimate(
            flops=30 * 10**9, bytes_accessed=2**26, transcendentals=2**22
        ),
    )(normed, dy, base, bias, weights, weights, rows_part)


def branch_kernel(query, *refs):
    if query:
        moved_ref, query_ref, normed_ref, *refs = refs
    else:
        grad_ref, *refs = refs
    (
        values_ref, gain_ref, base_ref, mixed_ref, weight_ref,
        total_ref, do_ref, sums_ref, send_ref, keep_ref,
    ) = refs
    core = lax.axis_index("ctx") % 2

    def rows_of(ref):
        pieces = [ref[index] for index in range(ref.shape[0])]
        return pieces[0] if len(pieces) == 1 else jnp.concatenate(pieces, axis=1)

    def column_sum(row, value):
        sums_ref[row : row + 1, :] = jnp.sum(value, axis=0, keepdims=True)

    sums_ref[...] = jnp.zeros_like(sums_ref)
    products = []
    if query:
        cq = rows_of(moved_ref)
        grad = nt(cq, query_ref[...])
        column_sum(3, cq.astype(F32))
        products.append((normed_ref[...], cq))
    else:
        grad = grad_ref[...]
    unit, scale = normalize(values_ref[...])
    q = gain_ref[...] * grad
    back = scale * (
        q - jnp.mean(q, axis=-1, keepdims=True) - unit * jnp.mean(q * unit, axis=-1, keepdims=True)
    )
    column_sum(0, grad * unit)
    column_sum(1, grad)
    total = base_ref[...].astype(F32) + back
    total_ref[...] = total
    branch = total.astype(BF)
    column_sum(2, branch.astype(F32))
    do = nt(branch, weight_ref[...]).astype(BF)
    own = do_ref.shape[2]
    for index in range(do_ref.shape[0]):
        do_ref[index] = do[:, index * own : index * own + own]
    products.append((rows_of(mixed_ref), branch))
    half = keep_ref.shape[2]
    for index, (left, right) in enumerate(products):
        low, high = tn(left, right[:, :half]), tn(left, right[:, half:])
        keep_ref[index] = jnp.where(core == 0, low, high).astype(BF)
        send_ref[index] = jnp.where(core == 0, high, low).astype(BF)


def branch(grad, values, gain, base, mixed, weight, query=()):
    rows, width = values.shape
    number = 2 if query else 1
    vmem = pl.BlockSpec(memory_space=pltpu.VMEM)
    half = jax.ShapeDtypeStruct((number, width, width // 2), BF)
    operands = (grad, *query, values, gain, base, mixed, weight)
    return pl.pallas_call(
        functools.partial(branch_kernel, bool(query)),
        out_shape=(
            jax.ShapeDtypeStruct((rows, width), F32),
            jax.ShapeDtypeStruct(mixed.shape, BF),
            jax.ShapeDtypeStruct((8, width), F32),
            half, half,
        ),
        in_specs=[vmem] * len(operands),
        out_specs=(vmem,) * 5,
        compiler_params=pltpu.CompilerParams(vmem_limit_bytes=VMEM_BYTES),
        cost_estimate=pl.CostEstimate(
            flops=10**10, bytes_accessed=2**24, transcendentals=0
        ),
    )(*operands)


def finish_kernel(more, late_ref, done_ref, ffn_ref, *refs):
    if more:
        moved_ref, enc_ref, *late, refs = (*refs[:6], refs[6:])
    all_ffn, all_done, all_late, *refs = refs
    if more:
        token_ref, enc_grad_ref, *refs = refs
    late_own, got, send_sem, recv_sem, zone_send, zone_recv, own_sem, *refs = refs
    me, zone = lax.axis_index("ctx"), lax.axis_index("fsdp")
    count, groups = lax.axis_size("ctx"), lax.axis_size("fsdp")
    chips = count // 2
    greet(others("ctx") + others("fsdp"))
    zones = group_copies(late_ref, got, zone_send, zone_recv, 0)
    for copy in zones:
        copy.start()
    if more:
        all_moved, weights, all_enc, enc_send, enc_recv, enc_own, moved_sem, weight_sem = refs
        put, arrived, put_done = exchange(enc_ref, all_enc, enc_send, enc_recv, enc_own)
        for step in range(count):
            put((me + step) % count)
        fetch_moved = pltpu.make_async_copy(moved_ref, all_moved, moved_sem)
        fetch_moved.start()
    gathers = [
        plane_gather(source, store, send_sem.at[kind], recv_sem.at[kind])
        for kind, (source, store) in enumerate(
            ((ffn_ref, all_ffn), (done_ref, all_done), (late_own, all_late))
        )
    ]
    local = [
        pltpu.make_async_copy(source, store.at[me], own_sem.at[kind])
        for kind, (source, store) in enumerate(
            ((ffn_ref, all_ffn), (done_ref, all_done), (late_own, all_late))
        )
    ]
    for kind in range(2):
        gathers[kind][0]()
        local[kind].start()
    if more:
        width = token_ref.shape[1]

        def fetch(step):
            source = (me + step) % count
            out = []
            for k in range(5):
                columns = pl.ds(pl.multiple_of(k * width + source * 128, 128), 128)
                for index, array in enumerate(late):
                    side = me % 2 if index < 2 else 1 - me % 2
                    out.append(
                        pltpu.make_async_copy(
                            array.at[:, :, columns], weights.at[step % 2, k, :, side, index % 2],
                            weight_sem.at[step % 2, k, index],
                        )
                    )
            return out

        for copy in fetch(0):
            copy.start()
        token_ref[...] = jnp.zeros_like(token_ref)
        enc_grad_ref[...] = jnp.zeros_like(enc_grad_ref)
        fetch_moved.wait()

        def one_source(step, carry):
            source = (me + step) % count

            @pl.when(step + 1 < count)
            def _():
                for copy in fetch(step + 1):
                    copy.start()

            for copy in fetch(step):
                copy.wait()
            grads = all_moved[source]

            def part(index):
                return weights[step % 2, index].reshape(width, 128)

            token_ref[...] += (
                nt(grads[:, :128], part(0))
                + nt(grads[:, 128:256], part(1))
                + nt(grads[:, 256:], part(2))
            )
            arrived(source)
            rows = all_enc[source]
            enc_grad_ref[...] += nt(rows[:, :128], part(3)) + nt(rows[:, 128:], part(4))
            return carry

        lax.fori_loop(0, count, one_source, 0)
    total = late_ref[zone].astype(F32)
    for shift in range(groups - 1):
        zones[shift].wait_recv()
        total = total + got[shift].astype(F32)
    late_own[...] = total.astype(BF)
    gathers[2][0]()
    local[2].start()
    for index in range(chips - 1):
        for gather in gathers:
            gather[1](index)
    for index in range(chips):
        for gather in gathers:
            gather[2](index)
    for copy in local:
        copy.wait()
    for gather in gathers:
        gather[3]()
    for copy in zones:
        copy.wait_send()
    if more:
        put_done()


def finish(late, done, ffn_sums, width, more=()):
    count, groups = lax.axis_size("ctx"), lax.axis_size("fsdp")
    vmem = pl.BlockSpec(memory_space=pltpu.VMEM)
    hbm = pl.BlockSpec(memory_space=pl.ANY)
    dma = pltpu.SemaphoreType.DMA
    outs = [
        jax.ShapeDtypeStruct((count,) + shape, BF)
        for shape in (ffn_sums.shape, done.shape, late.shape[1:])
    ]
    places = [hbm] * 3
    scratch = [
        pltpu.VMEM(late.shape[1:], BF),
        pltpu.VMEM((groups - 1,) + late.shape[1:], BF),
        dma((3, count + 1)), dma((3, count + 1)),
        dma((groups - 1,)), dma((groups - 1,)), dma((3,)),
    ]
    if more:
        moved, enc, weights = more[:3]
        outs.append(jax.ShapeDtypeStruct((moved.shape[1], width), F32))
        outs.append(jax.ShapeDtypeStruct((enc.shape[1], width), F32))
        places += [vmem, vmem]
        scratch += [
            pltpu.VMEM(moved.shape, BF),
            pltpu.VMEM((2, 5, groups, 2, 2, weights.shape[1], 128), BF),
            pltpu.VMEM(enc.shape, BF),
            dma((count,)), dma((count,)), dma, dma, dma((2, 5, 4)),
        ]
    return pl.pallas_call(
        functools.partial(finish_kernel, bool(more)),
        out_shape=outs,
        in_specs=[vmem] + [hbm] * (2 + len(more)),
        out_specs=places,
        scratch_shapes=scratch,
        compiler_params=pltpu.CompilerParams(
            vmem_limit_bytes=VMEM_BYTES, collective_id=6, has_side_effects=True
        ),
        cost_estimate=pl.CostEstimate(
            flops=50 * 10**9, bytes_accessed=2**25, transcendentals=0
        ),
    )(late, done, ffn_sums, *more)


def place_kernel(groups, more, ffn_ref, self_refs, kv_refs, mixed_refs, out_refs, extra):
    in_ref, out_ref, self_ref, kv_ref, *weight_refs = out_refs
    cols = ffn_ref.shape[3]
    steps = ffn_ref.shape[1] // 2
    hidden = in_ref.shape[1]
    blocks = out_ref.shape[0]
    width = out_ref.shape[3]
    depth = width // groups
    per = steps // blocks
    span = min(depth, cols)
    for core in range(2):
        for f in range(steps):
            value = ffn_ref[core, f].astype(F32)
            for piece in range(cols // span):
                unit = (f % per) * 2 * cols + core * cols + piece * span
                at = (unit // depth * blocks + f // per) * depth + unit % depth
                in_ref[:, at : at + span] = value[:, piece * span : piece * span + span]
        for slab in range(steps):
            at = (core * 2 + slab % 2) * cols
            out_ref[slab // 2, 0, :, at : at + cols] = ffn_ref[core, steps + slab].astype(F32)
    for refs, target in ((self_refs, self_ref), (kv_refs, kv_ref)):
        for k, ref in enumerate(refs):
            own = ref.shape[2]
            for source in range(ref.shape[0]):
                at = k * width + source * own
                target[:, at : at + own] = ref[source].astype(F32)
    part = in_ref.shape[0]
    for (ref, count), targets in zip(mixed_refs, (weight_refs[:1], weight_refs[1:])):
        own = ref.shape[2]
        for w, target in enumerate(targets):
            for core in range(2):
                for index in range(count):
                    top = (w * count + index) * part
                    at = core * (width // 2) + index * own
                    target[:, at : at + own] = ref[core, top : top + part, :].astype(F32)
    if more:
        total_ref, tokens_ref, gain_ref, base_ref, enc_ref, token_ref, enc_out = extra
        unit, scale = normalize(tokens_ref[...].astype(F32))
        token_ref[...] = (
            base_ref[...] + normalize_back(unit, scale, gain_ref[...], total_ref[...])[0]
        )
        enc_out[...] = enc_ref[...]


def place(ffn_sums, done, late, hidden, width, more=()):
    count, groups = lax.axis_size("ctx"), lax.axis_size("fsdp")
    chips, own = count // 2, late.shape[2]
    depth = width // groups
    part = depth // chips
    blocks = hidden // width
    wide = width // 2 // own

    def lane_blocks(start, k):
        return pl.BlockSpec((count, part, own), lambda c: (0, (start + k * depth) // part + c, 0))

    in_specs = [pl.BlockSpec((2,) + ffn_sums.shape[1:], lambda c: (c, 0, 0, 0))]
    in_specs += [lane_blocks(2 * wide * part, k) for k in range(3)]
    in_specs += [lane_blocks(wide * part, k) for k in range(2)]
    in_specs += [
        pl.BlockSpec((2, wide * part, own), lambda c: (c, 0, 0)),
        pl.BlockSpec((2, 2 * wide * part, own), lambda c: (c, 0, 0)),
    ]
    row = lambda n: pl.BlockSpec((part, n), lambda c: (c, 0))
    out_specs = [
        row(hidden), pl.BlockSpec((blocks, 1, part, width), lambda c: (0, c, 0, 0)),
        row(3 * width), row(2 * width), row(width), row(width), row(width),
    ]
    out_shape = [
        jax.ShapeDtypeStruct((depth, hidden), F32),
        jax.ShapeDtypeStruct((blocks, chips, part, width), F32),
        jax.ShapeDtypeStruct((depth, 3 * width), F32),
        jax.ShapeDtypeStruct((depth, 2 * width), F32),
    ] + [jax.ShapeDtypeStruct((depth, width), F32)] * 3
    if more:
        total, _, _, _, enc = more
        tall, short = total.shape[0] // chips, enc.shape[0] // chips
        tokens_rows = pl.BlockSpec((tall, width), lambda c: (c, 0))
        enc_rows = pl.BlockSpec((short, width), lambda c: (c, 0))
        in_specs += [
            tokens_rows, tokens_rows, pl.BlockSpec((1, width), lambda c: (0, 0)), tokens_rows,
            enc_rows,
        ]
        out_specs += [tokens_rows, enc_rows]
        out_shape += [
            jax.ShapeDtypeStruct(total.shape, F32), jax.ShapeDtypeStruct(enc.shape, F32)
        ]

    def kernel(*refs):
        ffn_ref, refs = refs[0], refs[1:]
        self_refs, kv_refs, mixed, refs = refs[:3], refs[3:5], refs[5:7], refs[7:]
        extra_in, refs = refs[: len(more)], refs[len(more) :]
        place_kernel(
            groups, bool(more), ffn_ref, self_refs, kv_refs,
            ((mixed[0], wide), (mixed[1], wide)), refs[:7], extra_in + refs[7:],
        )

    return pl.pallas_call(
        kernel,
        grid=(chips,),
        out_shape=out_shape,
        in_specs=in_specs,
        out_specs=out_specs,
        compiler_params=pltpu.CompilerParams(vmem_limit_bytes=VMEM_BYTES),
        cost_estimate=pl.CostEstimate(flops=0, bytes_accessed=2**25, transcendentals=0),
    )(ffn_sums, late, late, late, done, done, done, late, *more)


def swap(value, bit):
    count = lax.axis_size("ctx")
    return lax.ppermute(value, "ctx", [(i, i ^ bit) for i in range(count)])


def pair_sum(send, keep):
    return (keep.astype(F32) + swap(send, 1).astype(F32)).astype(BF)


def gather_ffn(ffn_in, ffn_out):
    count = lax.axis_size("ctx")
    groups = lax.axis_size("fsdp")
    me = lax.axis_index("ctx")
    depth, hidden = ffn_in.shape
    width = ffn_out.shape[1]
    blocks = hidden // width
    rows = depth // count
    left = lax.dynamic_slice_in_dim(ffn_in, me * rows, rows, 0)
    left = left.reshape(rows, groups, blocks, depth)
    left = jnp.transpose(left, (0, 2, 1, 3)).reshape(rows, hidden)
    right = lax.dynamic_index_in_dim(
        ffn_out.reshape(blocks, count, rows, width), me, 1, keepdims=False
    )
    right = jnp.moveaxis(right, 0, 1).reshape(rows, hidden)
    joined = jnp.concatenate([left, right], axis=1)
    return lax.all_gather(joined, ("fsdp", "ctx"), axis=0, tiled=True)


def body(
    tokens, encoder_out, prompt_offsets, gains, shifts, self_in, self_out, cross_q, cross_kv,
    cross_out, ffn_in, ffn_bias, ffn_out, out_bias, cotangent,
):
    row_count, width = tokens.shape
    head_dim = width // HEADS
    scale = 1.0 / math.sqrt(head_dim)
    ctx = lax.axis_size("ctx")
    groups = lax.axis_size("fsdp")
    me = lax.axis_index("ctx")
    heads = HEADS // ctx
    own = heads * head_dim

    shard = gains.shape[1]
    small = jnp.concatenate(
        [gains, shifts, out_bias[None], ffn_bias.reshape(-1, shard)], axis=0
    )
    small_rows = small.shape[0]
    small = jnp.pad(small, ((0, 32 - small_rows), (0, 0)))

    head_in = lax.dynamic_index_in_dim(
        self_in.reshape(self_in.shape[0], 3, ctx, own), me, 2, keepdims=False
    ).reshape(-1, 3 * own)
    half_rows = self_in.shape[0] // 2
    core = me % 2

    def half_of(*weights):
        cut = [lax.dynamic_slice_in_dim(w, core * half_rows, half_rows, 0) for w in weights]
        return jnp.concatenate(cut, axis=1)

    all_normed, queries, keys, values, small, head_in, near_rows = project(
        own, scale, tokens, small, head_in, half_of(self_out, cross_q)
    )
    all_normed = all_normed.reshape(-1, width)
    queries, keys, values = [x.reshape(-1, 128) for x in (queries, keys, values)]
    small = small[:, :small_rows].astype(F32)
    vectors = jnp.moveaxis(small[:, :13], 0, 1).reshape(13, width)
    gain, shift, full_out_bias = vectors[:3], vectors[3:12], vectors[12]
    full_ffn_bias = small[:, 13:].reshape(-1)

    def lanes(value):
        gap = [(0, 0)] * (value.ndim - 1) + [(0, 128 - own)]
        return value if own == 128 else jnp.pad(value, gap)

    head_kv = lax.dynamic_index_in_dim(
        cross_kv.reshape(-1, 2, ctx, own), me, 2, keepdims=False
    ).reshape(-1, 2 * own)
    (queries, ffn_in, ffn_out) = lax.optimization_barrier((queries, ffn_in, ffn_out))
    ffn_weights = gather_ffn(ffn_in, ffn_out)
    mixed_heads, att_self, lse_self, near_other, all_encoder, head_kv = attend_forward(
        False, heads, prompt_offsets, queries, keys, values, (near_rows, encoder_out, head_kv),
    )

    def both_cores(mine, other):
        shape = (mine.shape[0], 2) + mine.shape[1:]
        full = lax.dynamic_update_index_in_dim(jnp.zeros(shape, BF), mine, core, 1)
        full = lax.dynamic_update_index_in_dim(full, other, 1 - core, 1)
        return full.reshape(width, -1)

    near_weights = both_cores(near_rows, near_other)
    full_self_out, full_cross_q = near_weights[:, :width], near_weights[:, width:]
    all_encoder = all_encoder.reshape(-1, width)
    head_kv = head_kv.reshape(width, 2 * own)

    def to_rows(value):
        return jnp.moveaxis(value[:, :, :own], 0, 1).reshape(row_count, width)

    def to_heads(value):
        return lanes(jnp.moveaxis(value.reshape(row_count, ctx, own), 1, 0))

    mixed = to_rows(mixed_heads)
    token_values = tokens.astype(F32)
    first = token_values + nn(mixed, full_self_out) + shift[5]
    normed_two = (normalize(first)[0] * gain[1] + shift[1]).astype(BF)
    cross_queries = (scale * (nn(normed_two, full_cross_q) + shift[6])).astype(BF)
    enc_shift = lax.dynamic_slice_in_dim(shift[7], me * own, own, 0)
    enc_projected = nn(all_encoder, head_kv)
    enc_keys = lanes(enc_projected[:, :own].astype(BF))
    enc_values = lanes((enc_projected[:, own:] + enc_shift).astype(BF))
    cross_heads, att_cross, lse_cross, all_cross_q, far_rows, far_other = attend_forward(
        True, heads, prompt_offsets, to_heads(cross_queries), enc_keys, enc_values,
        (half_of(cross_out),),
    )
    full_cross_out = both_cores(far_rows, far_other)
    cross_mixed = to_rows(cross_heads)
    second = first + nn(cross_mixed, full_cross_out) + shift[8]
    normed_three = (normalize(second)[0] * gain[2] + shift[2]).astype(BF)
    depth = ffn_in.shape[0]
    blocks = ffn_in.shape[1] // width
    order = full_ffn_bias.reshape(groups, blocks, depth)
    order = jnp.moveaxis(order, 0, 1).reshape(-1, 1, 512)
    late_rows = half_of(self_in, cross_kv)
    quarter = half_rows // 2
    layer_sum, grad_three, bias_parts, in_sum, out_sum, late_first = ffn(
        normed_three, cotangent, second + full_out_bias,
        jnp.broadcast_to(order, (order.shape[0], 8, 512)), ffn_weights, late_rows[:quarter],
    )
    layer_out = layer_sum.astype(BF)
    chips = ctx // 2
    part = depth // chips
    in_sum = in_sum.reshape(-1, groups, chips // 2, part, 256)
    out_sum = out_sum.reshape(-1, groups, chips // 2, part, 256)

    dy = cotangent.astype(F32)
    chip_first = lambda value: jnp.moveaxis(value.reshape(groups, chips, part, -1), 1, 0)

    def stacked(value):
        return value if own == 128 else to_rows(value)[None]

    def tiles_of(value):
        return value if own == 128 else to_heads(value[0])

    grad_second, cross_do, sums_two, send, keep = branch(
        grad_three, second, gain[2:3], cotangent, stacked(cross_heads), full_cross_out
    )
    cross_part = chip_first(pair_sum(send, keep)[0])
    got_shape = (max(chips // 2 - 1, 1),) + in_sum.shape[:2] + in_sum.shape[3:]
    cross_moved, cross_dk, cross_dv, in_got, out_got, cross_got, late_second = attend_backward(
        True, heads, scale, prompt_offsets, all_cross_q.reshape(-1, 128), enc_keys, enc_values,
        tiles_of(cross_do), att_cross, lse_cross,
        (in_sum, out_sum, cross_part, late_rows[quarter:]),
        (got_shape, got_shape, (chips - 1,) + cross_part.shape[1:], late_first.shape),
    )

    def joined(value, mine, dim, got):
        kept = lax.dynamic_index_in_dim(value, mine, dim, keepdims=False).astype(F32)
        return kept + jnp.sum(got.astype(F32), axis=0)

    grad_first, self_do, sums_one, send, keep = branch(
        stacked(cross_moved), first, gain[1:2], grad_second, stacked(mixed_heads), full_self_out,
        (full_cross_q, normed_two),
    )
    middle = pair_sum(send, keep)
    middle = jnp.moveaxis(middle.reshape(2, groups, chips, part, -1), 2, 0)
    cross_part = joined(cross_part, me // 2, 0, cross_got).astype(BF)
    enc_heads = jnp.concatenate([cross_dk[:, :own], cross_dv[:, :own]], axis=1)
    kv_part = tn(all_encoder, enc_heads).astype(BF).reshape(groups, depth, 2 * own)
    ffn_sums = jnp.concatenate(
        [
            joined(in_sum, me // 4, 2, in_got),
            joined(out_sum, (me // 2) % (chips // 2), 2, out_got),
        ],
        axis=0,
    )
    ffn_sums = jnp.moveaxis(ffn_sums.astype(BF), 1, 0)
    carried = (middle, ffn_sums, cross_part, kv_part, late_first, late_second)
    moved, _, grad_head_in, column, *got = attend_backward(
        False, heads, scale, prompt_offsets, queries, keys, values, tiles_of(self_do),
        att_self, lse_self, carried,
        [(value.shape[0] - 1,) + value.shape[1:] for value in carried[:4]]
        + [value.shape for value in carried[4:]],
        (all_normed.reshape(ctx, row_count, width),),
    )
    grad_head_in = grad_head_in.reshape(width, 3, 128)[:, :, :own].reshape(width, 3 * own)
    column = column[0].reshape(3, 128)[:, :own].reshape(-1)
    zone = lax.axis_index("fsdp")
    middle = joined(middle, me // 2, 0, got[0]).astype(BF)
    ffn_sums, cross_part, kv_part = [
        joined(value, zone, 0, part_got).astype(BF)
        for value, part_got in zip(carried[1:4], got[1:4])
    ]
    other_first, other_second = got[4:]
    weight = head_in.reshape(width, 3 * own).astype(F32)
    grad_shift_one = jnp.sum(weight * column, axis=1)
    grad_gain_one = jnp.sum(weight * (grad_head_in - shift[0][:, None] * column), axis=1) / gain[0]

    def spread(value):
        return lax.dynamic_update_slice_in_dim(jnp.zeros((width,), F32), value, me * own, 0)

    totals = jnp.stack(
        [
            grad_gain_one, sums_one[0], sums_two[0],
            grad_shift_one, sums_one[1], sums_two[1],
            spread(column[:own]), spread(column[2 * own :]),
            sums_one[2],
            sums_one[3],
            spread(jnp.sum(enc_heads[:, own:].astype(F32), axis=0)),
            sums_two[2],
            jnp.sum(dy, axis=0),
        ]
    )
    totals = jnp.moveaxis(totals.reshape(13, groups, shard), 1, 0).reshape(groups, -1)
    bias = jnp.moveaxis(bias_parts[:, 0].reshape(blocks, groups, depth), 0, 1)
    totals = jnp.concatenate([totals, bias.reshape(groups, -1)], axis=1)
    count = totals.shape[1]
    totals = jnp.pad(totals, ((0, 0), (0, 48 * own - count))).reshape(groups, 48, own)

    def by_lanes(value, rows):
        lead = value.shape[:-2]
        value = jnp.moveaxis(value.reshape(lead + (rows, -1, own)), -2, -3)
        return value.reshape(lead + (-1, own))

    middle = jnp.moveaxis(by_lanes(middle, part), 1, 0).reshape(groups, -1, own)
    late = by_lanes(grad_head_in.reshape(groups, depth, 3 * own), depth)
    late = jnp.concatenate([middle, late.astype(BF), totals.astype(BF)], axis=1)
    done = jnp.concatenate([by_lanes(cross_part, part), by_lanes(kv_part, depth)], axis=0)
    enc_sum = enc_heads.reshape(ctx, -1, 2 * own)
    more = ()
    if own == 128:
        more = (moved, enc_sum, late_first, late_second, other_first, other_second)
    all_ffn, all_done, all_late, *more_sums = finish(late, done, ffn_sums, width, more)
    if more:
        more = (more_sums[0], tokens, gain[:1], grad_first, more_sums[1])
    (
        grad_ffn_in, grad_ffn_out, grad_self_in, grad_cross_kv, grad_cross_out, grad_cross_q,
        grad_self_out, *more_grads,
    ) = place(all_ffn, all_done, all_late, ffn_in.shape[1], width, more)
    grad_ffn_out = grad_ffn_out.reshape(-1, width)
    sums = jnp.sum(all_late[:, -48:].astype(F32), axis=0).reshape(-1)[:count]
    mine, grad_ffn_bias = sums[: 13 * shard].reshape(13, shard), sums[13 * shard :]
    if more:
        input_grad, grad_encoder = more_grads
    else:

        late_mine = jnp.concatenate([late_first, late_second], axis=1)
        late_other = jnp.concatenate([other_first, other_second], axis=1)
        late_weights = both_cores(late_mine, late_other)
        cut = moved.reshape(ctx, row_count, 3, 128)[:, :, :, :own]
        grads = jnp.transpose(cut, (1, 2, 0, 3)).reshape(row_count, 3 * width)
        unit_one, scale_one = normalize(token_values)
        grad_normed = nt(grads, late_weights[:, : 3 * width])
        input_grad = grad_first + normalize_back(unit_one, scale_one, gain[0], grad_normed)[0]
        enc_sum = lax.all_to_all(enc_sum, "ctx", split_axis=0, concat_axis=0, tiled=True)
        enc_sum = jnp.transpose(enc_sum.reshape(ctx, -1, 2, own), (1, 2, 0, 3))
        grad_encoder = nt(enc_sum.reshape(-1, 2 * width), late_weights[:, 3 * width :])
    return (
        layer_out, input_grad, grad_encoder, mine[:3], mine[3:12], grad_self_in, grad_self_out,
        grad_cross_q, grad_cross_kv, grad_cross_out, grad_ffn_in, grad_ffn_bias, grad_ffn_out, mine[12],
    )


def solution(mesh):
    rows = P(("fsdp", "ctx"), None)
    shard = P("fsdp", None)
    thin = P(None, "fsdp")
    flat = P("fsdp")
    return jax.shard_map(
        body,
        mesh=mesh,
        in_specs=(
            rows, rows, shard, thin, thin, shard, shard, shard, shard, shard, shard, flat, shard,
            flat, rows,
        ),
        out_specs=(
            rows, rows, rows, thin, thin, shard, shard, shard, shard, shard, shard, flat, shard,
            flat,
        ),
        check_vma=False,
    )
```

```python
import functools
import math

import jax
import jax.numpy as jnp
from jax import lax
from jax.experimental import pallas as pl
from jax.experimental.pallas import tpu as pltpu
from jax.sharding import PartitionSpec as P

HEADS = 16
CONT = 2048
EPS = 1e-05
NEG = -1e30
TILE = 512
BF = jnp.bfloat16
F32 = jnp.float32
VMEM_BYTES = 56 * 2**20


def nn(left, right):
    return lax.dot_general(left, right, (((1,), (0,)), ((), ())), preferred_element_type=F32)


def nt(left, right):
    return lax.dot_general(left, right, (((1,), (1,)), ((), ())), preferred_element_type=F32)


def tn(left, right):
    return lax.dot_general(left, right, (((0,), (0,)), ((), ())), preferred_element_type=F32)


def normalize(values):
    center = values - jnp.mean(values, axis=-1, keepdims=True)
    scale = lax.rsqrt(jnp.mean(center * center, axis=-1, keepdims=True) + EPS)
    return center * scale, scale


def normalize_back(unit, scale, gain, grad):
    q = gain * grad
    back = scale * (
        q - jnp.mean(q, axis=-1, keepdims=True) - unit * jnp.mean(q * unit, axis=-1, keepdims=True)
    )
    return back, jnp.sum(grad * unit, axis=0), jnp.sum(grad, axis=0)


def head_lanes(head, array):
    lane = lax.broadcasted_iota(jnp.int32, array.shape, 1)
    keep = (lane < 64) if head == 0 else (lane >= 64)
    return jnp.where(keep, array, jnp.zeros_like(array))


def transposed(array):
    return array.astype(F32).T.astype(BF)


def visible(key_start, query_start, key_count, query_count, own_start, limit):
    key = key_start + lax.broadcasted_iota(jnp.int32, (key_count, query_count), 0)
    query = query_start + lax.broadcasted_iota(jnp.int32, (key_count, query_count), 1)
    shown = key <= query
    if limit is not None:
        shown = shown & ((key >= own_start) | (key < limit))
    return shown


def soften(scores, total, peak, value_t):
    old = peak[:1]
    new = jnp.maximum(old, jnp.max(scores, axis=0, keepdims=True))
    raised = jnp.exp(scores - new).astype(BF)
    total[...] = total[...] * jnp.exp(old - new) + nn(value_t, raised)
    peak[...] = jnp.broadcast_to(new, peak.shape)


def set_value_rows(value_t, head, columns, value):
    value_t[head, :64, columns] = value[64 * head : 64 * head + 64]
    value_t[head, 64:, columns] = jnp.ones((16, value.shape[1]), BF)


def tile_rows(tile):
    return pl.ds(pl.multiple_of(tile * TILE, TILE), TILE)


def flipped_bits(index, mask):
    out, bit = index, 1
    while bit <= mask:
        if mask & bit:
            out = out + bit - 2 * bit * ((index // bit) % 2)
        bit *= 2
    return out


def greet(peers):
    barrier = pltpu.get_barrier_semaphore()
    for peer in peers:
        pl.semaphore_signal(
            barrier, inc=1, device_id=peer, device_id_type=pl.DeviceIdType.MESH
        )
    pl.semaphore_wait(barrier, len(peers))


def others(axis):
    me, count = lax.axis_index(axis), lax.axis_size(axis)
    return [{axis: (me + step) % count} for step in range(1, count)]


def remote(source, target, send_sem, recv_sem, device):
    return pltpu.make_async_remote_copy(
        source, target, send_sem, recv_sem, device_id=device,
        device_id_type=pl.DeviceIdType.MESH,
    )


def exchange(source, target, send_sems, recv_sems, own_sem):
    me, count = lax.axis_index("ctx"), lax.axis_size("ctx")

    def copy(there, slot):
        return remote(
            source.at[there], target.at[slot], send_sems.at[there], recv_sems.at[slot],
            {"ctx": there},
        )

    def send(there):
        @pl.when(there != me)
        def _():
            copy(there, me).start()

        @pl.when(there == me)
        def _():
            pltpu.make_async_copy(source.at[me], target.at[me], own_sem).start()

    def arrived(there):
        @pl.when(there != me)
        def _():
            copy(there, there).wait_recv()

        @pl.when(there == me)
        def _():
            pltpu.make_async_copy(source.at[me], target.at[me], own_sem).wait()

    def sent():
        for step in range(1, count):
            copy((me + step) % count, me).wait_send()

    return send, arrived, sent


def plane_gather(source, store, send, recv):
    me = lax.axis_index("ctx")
    chips = lax.axis_size("ctx") // 2
    last = chips - 1
    sibling = flipped_bits(me, 1)
    near = [flipped_bits(me, 2 * other) for other in range(1, chips)]
    relay = chips == 4
    height = store.shape[1]
    cut = height // 2 if height < 32 else height // 32 * 16

    def own(index, there, block):
        return remote(source, store.at[block], send.at[index], recv.at[index], {"ctx": there})

    def passed(index, block):
        return remote(
            store.at[block], store.at[block], send.at[chips + index], recv.at[chips + index],
            {"ctx": sibling},
        )

    def half(part, there, block):
        rows = pl.ds(0, cut) if part == 0 else pl.ds(cut, height - cut)
        at = 2 * chips - 1 + part
        return remote(
            store.at[block, rows], store.at[block, rows], send.at[at], recv.at[at], {"ctx": there}
        )

    firsts = range(2) if relay else range(last)

    def start():
        for index in firsts:
            own(index, near[index], me).start()
        own(last, sibling, me).start()

    def land(index):
        block = near[index]
        if relay and index == 2:
            half(0, near[0], block).wait_recv()
            half(1, near[1], block).wait_recv()
        else:
            own(index, block, block).wait_recv()
            if relay:
                half(1 - index, near[1 - index], block).start()
        passed(index, block).start()
        return block

    def rest(index):
        if index == 0:
            own(last, sibling, sibling).wait_recv()
            return sibling
        block = flipped_bits(near[index - 1], 1)
        passed(index - 1, block).wait_recv()
        return block

    def done():
        for index in firsts:
            own(index, near[index], me).wait_send()
        own(last, sibling, me).wait_send()
        for index in range(last):
            passed(index, near[index]).wait_send()
        if relay:
            half(0, near[0], near[1]).wait_send()
            half(1, near[1], near[0]).wait_send()

    return start, land, rest, done


def attend_forward_kernel(cross, heads, conts, offs_ref, q_ref, k_ref, v_ref, *refs):
    if cross:
        rows_ref, mixed_ref, att_ref, lse_ref, q_out, rows_all, pair_all, *refs = refs
    else:
        pair_ref, enc_ref, kv_ref, *refs = refs
        mixed_ref, att_ref, lse_ref, pair_all, enc_all, kv_all, *refs = refs
    total, peak, value_t, score_a, score_b, stage, send_sem, recv_sem, own_sem, pair_sem, *refs = refs
    me, count = lax.axis_index("ctx"), lax.axis_size("ctx")
    rows = att_ref.shape[1]
    tiles = rows // TILE
    key_tiles = k_ref.shape[0] // TILE
    prompt = rows - conts * CONT
    prompt_tiles = prompt // TILE
    greet(others("ctx") + others("fsdp"))
    send, arrived, sent = exchange(stage, mixed_ref, send_sem, recv_sem, own_sem)
    zone = lax.axis_index("fsdp")
    pair_copy = core_swap(rows_all if cross else pair_ref, pair_all, pair_sem)
    if not cross:
        gather_send, gather_recv, gather_own, kv_send, kv_recv = refs
        enc_start, enc_land, enc_rest, enc_done = plane_gather(
            enc_ref, enc_all, gather_send, gather_recv
        )
        enc_start()
        first = group_spread(kv_ref, kv_all, kv_send, kv_recv, 0)
        local = [
            pltpu.make_async_copy(enc_ref, enc_all.at[me], gather_own.at[0]),
            pltpu.make_async_copy(kv_ref, kv_all.at[zone], gather_own.at[1]),
        ]
        for copy in first + local:
            copy.start()
    if cross:
        q_all, q_send, q_recv, q_own, rows_send, rows_recv = refs
        put, got, put_done = exchange(q_ref, q_all, q_send, q_recv, q_own)
        for step in range(count):
            put((me + step) % count)
        spread = group_spread(rows_ref, rows_all, rows_send, rows_recv, 0)
        keep_rows = pltpu.make_async_copy(rows_ref, rows_all.at[zone], pair_sem.at[2])
        for copy in spread + [keep_rows]:
            copy.start()
    else:
        pair_copy.start()

    for tile in range(key_tiles):
        at = pl.ds(tile * TILE, TILE)
        turned = transposed(v_ref[at, :])
        for head in range(heads):
            set_value_rows(value_t, head, at, turned)

    def query_tile(step, carry):
        if cross:
            i = (me + step) % count
            got(i)
            q = q_all[i]
            q_out[i] = q
        else:
            i = (me + 1 + step) % count
            q = q_ref[tile_rows(i), :]
        masked = [head_lanes(head, q) for head in range(heads)]
        total[...] = jnp.zeros_like(total)
        peak[...] = jnp.full_like(peak, NEG)

        def score(j, target):
            k = k_ref[tile_rows(j), :]
            for head in range(heads):
                target[head] = nt(k, masked[head])

        def soft(j, source, shown=None):
            for head in range(heads):
                scores = source[head]
                if shown is not None:
                    scores = jnp.where(shown, scores, NEG)
                soften(
                    scores, total.at[head], peak.at[head], value_t[head, :, tile_rows(j)]
                )

        if cross:
            both = (score_a, score_b)
            score(0, score_a)
            for j in range(key_tiles):
                if j + 1 < key_tiles:
                    score(j + 1, both[(j + 1) % 2])
                soft(j, both[j % 2])
        elif conts == 1:
            score(i, score_a)
            diagonal = visible(0, 0, TILE, TILE, 0, None)

            @pl.when(i > 0)
            def _():
                score(i - 1, score_b)
                soft(i, score_a, diagonal)

            @pl.when(i == 0)
            def _():
                soft(i, score_a, diagonal)

            def two(t, carry):
                j = i - 1 - 2 * t
                score(jnp.maximum(j - 1, 0), score_a)
                soft(j, score_b)
                score(jnp.maximum(j - 2, 0), score_b)
                soft(j - 1, score_a)
                return carry

            lax.fori_loop(0, i // 2, two, 0)

            @pl.when(i % 2 == 1)
            def _():
                soft(0, score_b)
        else:
            cont = jnp.maximum(i * TILE - prompt, 0) // CONT
            inside = i * TILE < prompt
            own = jnp.where(inside, 0, prompt + cont * CONT)
            limit = offs_ref[0, cont]

            def one(j, carry):
                score(j, score_a)
                soft(j, score_a, visible(j * TILE, i * TILE, TILE, TILE, own, limit))
                return carry

            lax.fori_loop(jnp.where(inside, 0, own // TILE), i + 1, one, 0)
            lax.fori_loop(0, jnp.where(inside, 0, prompt_tiles), one, 0)

        for head in range(heads):
            part = total[head]
            att_ref[64 * head : 64 * head + 64, tile_rows(i)] = part[:64] / part[64:65]
            lse_ref[head : head + 1, tile_rows(i)] = peak[head][:1] + jnp.log(part[64:65])
        stage[i] = att_ref[:, tile_rows(i)].T.astype(BF)
        send(i)
        if cross:

            @pl.when(step == tiles - 2)
            def _():
                keep_rows.wait()
                for copy in spread:
                    copy.wait_recv()
                pair_copy.start()

        else:

            @pl.when(step == tiles - 3)
            def _():
                for index in range(min(2, count // 2 - 1)):
                    enc_land(index)

        return carry

    if heads < 2:
        att_ref[...] = jnp.zeros_like(att_ref)
    lax.fori_loop(0, tiles, query_tile, 0)
    for step in range(count):
        arrived((me + step) % count)
    sent()
    pair_copy.wait()
    if cross:
        put_done()
        for copy in spread:
            copy.wait_send()
    else:
        for index in range(2, count // 2 - 1):
            enc_land(index)
        for index in range(count // 2):
            enc_rest(index)
        for copy in first:
            copy.wait_send()
            copy.wait_recv()
        for copy in local:
            copy.wait()
        enc_done()


def chain_spread(source, target, send, recv):
    zone, groups = lax.axis_index("fsdp"), lax.axis_size("fsdp")

    def copy(way, stage):
        step = 1 - 2 * way
        block = jnp.clip(zone - step * stage, 0, groups - 1)
        at = way * groups + stage
        return remote(
            source if stage == 0 else target.at[block], target.at[block],
            send.at[at], recv.at[at], {"fsdp": jnp.clip(zone + step, 0, groups - 1)},
        )

    def arrival(way, stage):
        step = 1 - 2 * way
        block = jnp.clip(zone - step * (stage + 1), 0, groups - 1)
        at = way * groups + stage
        return remote(
            target.at[block], target.at[block], send.at[at], recv.at[at],
            {"fsdp": jnp.clip(zone + step, 0, groups - 1)},
        )

    def sends(way, stage):
        return (zone + 1 < groups) & (zone >= stage) if way == 0 else (
            (zone > 0) & (zone + stage < groups)
        )

    def comes(way, stage):
        return zone >= stage + 1 if way == 0 else zone + stage + 1 < groups

    def send_all(stage):
        for way in range(2):

            @pl.when(sends(way, stage))
            def _():
                copy(way, stage).start()

    def wait_all(stage):
        for way in range(2):

            @pl.when(comes(way, stage))
            def _():
                arrival(way, stage).wait_recv()

    def start():
        send_all(0)

    def advance(stage):
        wait_all(stage - 1)
        send_all(stage)

    def finish():
        wait_all(groups - 2)
        for stage in range(groups - 1):
            for way in range(2):

                @pl.when(sends(way, stage))
                def _():
                    copy(way, stage).wait_send()

    return start, advance, finish


def core_swap(source, target, sems):
    there = {"ctx": flipped_bits(lax.axis_index("ctx"), 1)}
    return remote(source, target, sems.at[0], sems.at[1], there)


def group_spread(source, target, send_sem, recv_sem, sem):
    zone, groups = lax.axis_index("fsdp"), lax.axis_size("fsdp")
    return [
        remote(
            source, target.at[zone], send_sem.at[sem + shift - 1], recv_sem.at[sem + shift - 1],
            {"fsdp": (zone + shift) % groups},
        )
        for shift in range(1, groups)
    ]


def attend_forward(cross, heads, offsets, q, k, v, extra=()):
    count = lax.axis_size("ctx")
    rows = count * TILE
    vmem = pl.BlockSpec(memory_space=pltpu.VMEM)
    hbm = pl.BlockSpec(memory_space=pl.ANY)
    dma = pltpu.SemaphoreType.DMA
    tiles = jax.ShapeDtypeStruct((count, TILE, 128), BF)
    outs = [
        tiles,
        jax.ShapeDtypeStruct((128, rows), F32),
        jax.ShapeDtypeStruct((8, rows), F32),
    ]
    scratch = [
        pltpu.VMEM((heads, 80, TILE), F32),
        pltpu.VMEM((heads, 8, TILE), F32),
        pltpu.VMEM((heads, 80, k.shape[0]), BF),
        pltpu.VMEM((heads, TILE, TILE), F32),
        pltpu.VMEM((heads, TILE, TILE), F32),
        pltpu.VMEM((count, TILE, 128), BF),
        dma((count,)), dma((count,)), dma, dma((3,)),
    ]
    groups = lax.axis_size("fsdp")
    if cross:
        spread = jax.ShapeDtypeStruct((groups,) + extra[0].shape, BF)
        outs += [tiles, spread, spread]
        scratch += [pltpu.VMEM((count, TILE, 128), BF), dma((count,)), dma((count,)), dma]
        scratch += [dma((groups - 1,)), dma((groups - 1,))]
        places = [vmem, hbm, hbm]
    else:
        near, enc, kv = extra
        outs.append(jax.ShapeDtypeStruct(near.shape, BF))
        outs.append(jax.ShapeDtypeStruct((count,) + enc.shape, BF))
        outs.append(jax.ShapeDtypeStruct((groups,) + kv.shape, BF))
        scratch += [dma((count + 1,)), dma((count + 1,)), dma((2,))]
        scratch += [dma((groups - 1,)), dma((groups - 1,))]
        places = [hbm] * 3
    return pl.pallas_call(
        functools.partial(attend_forward_kernel, cross, heads, offsets.shape[1]),
        out_shape=outs,
        in_specs=[pl.BlockSpec(memory_space=pltpu.SMEM), vmem, vmem, vmem] + [hbm] * len(extra),
        out_specs=[hbm, vmem, vmem] + places,
        scratch_shapes=scratch,
        compiler_params=pltpu.CompilerParams(
            vmem_limit_bytes=VMEM_BYTES, collective_id=2 if cross else 1,
            has_side_effects=True,
        ),
        cost_estimate=pl.CostEstimate(
            flops=40 * 10**9, bytes_accessed=2**23, transcendentals=2**24
        ),
    )(offsets, q, k, v, *extra)


def rest_copies(sources, targets, send_sem, recv_sem):
    me = lax.axis_index("ctx")
    chips = lax.axis_size("ctx") // 2
    half = chips // 2
    out = []
    for other in range(1, half):
        for part in range(2):
            mine = me // 4 if part == 0 else (me // 2) % half
            sem = len(out)
            out.append(
                remote(
                    sources[part].at[:, :, flipped_bits(mine, other)],
                    targets[part].at[other - 1],
                    send_sem.at[sem], recv_sem.at[sem],
                    {"ctx": flipped_bits(me, (4 if part == 0 else 2) * other)},
                )
            )
    return out + chip_copies(sources[2], targets[2], send_sem, recv_sem, len(out))


def chip_copies(source, target, send_sem, recv_sem, sem):
    me = lax.axis_index("ctx")
    return [
        remote(
            source.at[flipped_bits(me // 2, other)], target.at[other - 1],
            send_sem.at[sem + other - 1], recv_sem.at[sem + other - 1],
            {"ctx": flipped_bits(me, 2 * other)},
        )
        for other in range(1, lax.axis_size("ctx") // 2)
    ]


def group_copies(source, target, send_sem, recv_sem, sem):
    zone, groups = lax.axis_index("fsdp"), lax.axis_size("fsdp")
    return [
        remote(
            source.at[(zone + shift) % groups], target.at[shift - 1],
            send_sem.at[sem + shift - 1], recv_sem.at[sem + shift - 1],
            {"fsdp": (zone + shift) % groups},
        )
        for shift in range(1, groups)
    ]


def last_copies(sources, targets, send_sem, recv_sem):
    out = chip_copies(sources[0], targets[0], send_sem, recv_sem, 0)
    for source, target in zip(sources[1:4], targets[1:4]):
        out = out + group_copies(source, target, send_sem, recv_sem, len(out))
    return out


def attend_backward_kernel(
    cross, heads, conts, scale, carried, number, offs_ref, q_ref, k_ref, v_ref, do_ref, att_ref,
    lse_ref, *refs,
):
    sources, refs = refs[:number], refs[number:]
    if not cross:
        normed_ref, *refs = refs
    if cross:
        moved_ref, dk_ref, dv_ref, *refs = refs
    else:
        moved_ref, stage, product_ref, column_ref, *refs = refs
    targets, refs = refs[:number], refs[number:]
    if cross:
        stage, *refs = refs
    (
        do_all, key_t, delta, dq_sum, dk_sum, dv_sum, score_a, score_b, grad_a, grad_b,
        send_sem, recv_sem, own_sem, do_send, do_recv, do_own, carry_send, carry_recv, *refs,
    ) = refs
    if cross:
        keep_sem, chain_send, chain_recv = refs
        chain_start, chain_advance, chain_finish = chain_spread(
            sources[3], targets[3], chain_send, chain_recv
        )
        keep_own = pltpu.make_async_copy(
            sources[3], targets[3].at[lax.axis_index("fsdp")], keep_sem
        )
    else:
        normed, normed_sem, *pair_sems = refs
        pair_copies = [
            core_swap(sources[4 + index], targets[4 + index], pair_sems[index])
            for index in range(2)
        ]
        product_ref[...] = jnp.zeros_like(product_ref)
        column_ref[...] = jnp.zeros_like(column_ref)
    me, count = lax.axis_index("ctx"), lax.axis_size("ctx")
    tiles = count
    key_tiles = k_ref.shape[0] // TILE
    prompt = tiles * TILE - conts * CONT
    greet(others("ctx") + others("fsdp"))
    put, got, put_done = exchange(do_ref, do_all, do_send, do_recv, do_own)
    for step in range(count):
        put((me + step) % count)
    carry_copies = carried(sources, targets, carry_send, carry_recv)
    for copy in carry_copies:
        copy.start()
    if cross:
        chain_start()
        keep_own.start()
    else:
        for copy in pair_copies:
            copy.start()
    send, arrived, sent = exchange(stage, moved_ref, send_sem, recv_sem, own_sem)
    dq_sum[...] = jnp.zeros_like(dq_sum)
    dk_sum[...] = jnp.zeros_like(dk_sum)
    dv_sum[...] = jnp.zeros_like(dv_sum)
    for tile in range(key_tiles):
        at = pl.ds(tile * TILE, TILE)
        key_t[:, at] = transposed(k_ref[at, :])

    def ready(i):
        got(i)
        both = do_all[i].astype(F32).T * att_ref[:, tile_rows(i)]
        for head in range(heads):
            delta[head : head + 1, tile_rows(i)] = jnp.sum(
                both[64 * head : 64 * head + 64], axis=0, keepdims=True
            )

    def score(i, j, kept):
        row, at = tile_rows(i), tile_rows(j)
        q, do, k, v = q_ref[row, :], do_all[i], k_ref[at, :], v_ref[at, :]
        for head in range(heads):
            kept[0][head] = nt(k, head_lanes(head, q))
            kept[1][head] = nt(v, head_lanes(head, do))

    def settle(i, j, kept, shown=None):
        row, at = tile_rows(i), tile_rows(j)
        q, do = q_ref[row, :], do_all[i]
        for head in range(heads):
            weights = jnp.exp(kept[0][head] - lse_ref[head : head + 1, row])
            if shown is not None:
                weights = jnp.where(shown, weights, 0.0)
            score_grad = weights * (kept[1][head] - delta[head : head + 1, row])
            score_grad = score_grad.astype(BF)
            dv_sum[at, :] += nn(weights.astype(BF), head_lanes(head, do))
            dk_sum[at, :] += nn(score_grad, head_lanes(head, q))
            own = slice(64 * head, 64 * head + 64)
            dq_sum[own, row] += nn(key_t[own, at], score_grad)

    even, odd = (score_a, grad_a), (score_b, grad_b)

    def shown_of(i, j):
        if conts == 1:
            return None
        cont = jnp.maximum(i * TILE - prompt, 0) // CONT
        own = jnp.where(i * TILE < prompt, 0, prompt + cont * CONT)
        return visible(j * TILE, i * TILE, TILE, TILE, own, offs_ref[0, cont])

    def queries_back(i):
        return (dq_sum[:, tile_rows(i)].T.astype(BF).astype(F32) * scale).astype(BF)

    def cross_tile(step, carry):
        i = (me + step) % count
        ready(i)

        for hop in range(1, min(3, lax.axis_size("fsdp") - 1)):

            @pl.when(step == 2 * hop + 1)
            def _():
                chain_advance(hop)

        both = (even, odd)
        score(i, 0, even)
        for j in range(key_tiles):
            if j + 1 < key_tiles:
                score(i, j + 1, both[(j + 1) % 2])
            settle(i, j, both[j % 2])
        stage[i] = queries_back(i)
        send(i)
        return carry

    def self_tile(step, carry):
        i = (me + 1 + step) % count
        fetch = pltpu.make_async_copy(normed_ref.at[i], normed, normed_sem)
        fetch.start()

        def tiles_of(turn):
            p = (i + turn) % count
            return jnp.maximum(i, p), jnp.minimum(i, p)

        def score_turn(turn, kept):
            high, low = tiles_of(turn)
            score(high, low, kept)

        def settle_turn(turn, kept):
            high, low = tiles_of(turn)
            settle(high, low, kept, shown_of(high, low))

        diagonal = visible(0, 0, TILE, TILE, 0, None) if conts == 1 else shown_of(i, i)
        left = count - 1 - step

        @pl.when(step == 0)
        def _():
            ready(i)
            score(i, i, even)
            settle(i, i, even, diagonal)

            def fresh(turn, carry):
                ready((i + turn) % count)
                score_turn(turn, even)
                settle_turn(turn, even)
                return carry

            lax.fori_loop(1, count, fresh, 0)

        @pl.when(step > 0)
        def _():
            score(i, i, even)

            @pl.when(left > 0)
            def _():
                score_turn(1, odd)
                settle(i, i, even, diagonal)

            @pl.when(left == 0)
            def _():
                settle(i, i, even, diagonal)

            def two(turn, carry):
                at = 1 + 2 * turn
                score_turn(at + 1, even)
                settle_turn(at, odd)
                score_turn(at + 2, odd)
                settle_turn(at + 1, even)
                return carry

            lax.fori_loop(0, jnp.maximum(left - 1, 0) // 2, two, 0)

            @pl.when(left % 2 == 1)
            def _():
                settle_turn(left, odd)

            @pl.when((left > 0) & (left % 2 == 0))
            def _():
                score_turn(left, even)
                settle_turn(left - 1, odd)
                settle_turn(left, even)

        stage[i, :, :128] = queries_back(i)
        stage[i, :, 128:256] = dk_sum[tile_rows(i), :].astype(BF)
        stage[i, :, 256:] = dv_sum[tile_rows(i), :].astype(BF)
        send(i)
        fetch.wait()
        grads = stage[i]
        product_ref[...] += tn(normed[...], grads)
        column_ref[...] += jnp.broadcast_to(
            jnp.sum(grads.astype(F32), axis=0, keepdims=True), column_ref.shape
        )
        return carry

    lax.fori_loop(0, tiles, cross_tile if cross else self_tile, 0)
    if cross:
        dk_ref[...] = dk_sum[...].astype(BF)
        dv_ref[...] = dv_sum[...].astype(BF)
    for step in range(count):
        arrived((me + step) % count)
    sent()
    put_done()
    if cross:
        keep_own.wait()
        for hop in range(3, lax.axis_size("fsdp") - 1):
            chain_advance(hop)
        chain_finish()
    else:
        for copy in pair_copies:
            copy.wait()
    for copy in carry_copies:
        copy.wait_send()
        copy.wait_recv()


def attend_backward(
    cross, heads, scale, offsets, q, k, v, do, att, lse, sources, target_shapes, normed=()
):
    count = lax.axis_size("ctx")
    vmem = pl.BlockSpec(memory_space=pltpu.VMEM)
    hbm = pl.BlockSpec(memory_space=pl.ANY)
    dma = pltpu.SemaphoreType.DMA
    keys = k.shape[0]
    wide = 128 if cross else 384
    moved = jax.ShapeDtypeStruct((count, TILE, wide), BF)
    if cross:
        local = [jax.ShapeDtypeStruct((keys, 128), BF)] * 2
        carries = 2 * (count // 4 - 1) + count // 2 - 1
    else:
        local = [
            jax.ShapeDtypeStruct((count, TILE, wide), BF),
            jax.ShapeDtypeStruct((normed[0].shape[2], wide), F32),
            jax.ShapeDtypeStruct((8, wide), F32),
        ]
        carries = count // 2 - 1 + (lax.axis_size("fsdp") - 1) * 3
    targets = [jax.ShapeDtypeStruct(shape, BF) for shape in target_shapes]
    return pl.pallas_call(
        functools.partial(
            attend_backward_kernel, cross, heads, offsets.shape[1], scale,
            rest_copies if cross else last_copies, len(sources),
        ),
        out_shape=[moved] + local + targets,
        in_specs=[pl.BlockSpec(memory_space=pltpu.SMEM)] + [vmem] * 6
        + [hbm] * (len(sources) + len(normed)),
        out_specs=[hbm] + [vmem] * len(local) + [hbm] * len(sources),
        scratch_shapes=([pltpu.VMEM((count, TILE, wide), BF)] if cross else [])
        + [
            pltpu.VMEM((count, TILE, 128), BF),
            pltpu.VMEM((128, keys), BF),
            pltpu.VMEM((8, count * TILE), F32),
            pltpu.VMEM((128, count * TILE), F32),
            pltpu.VMEM((keys, 128), F32),
            pltpu.VMEM((keys, 128), F32),
        ]
        + [pltpu.VMEM((heads, TILE, TILE), F32)] * 4
        + [
            dma((count,)), dma((count,)), dma,
            dma((count,)), dma((count,)), dma,
            dma((carries,)), dma((carries,)),
        ]
        + ([dma] + [dma((2 * lax.axis_size("fsdp"),))] * 2 if cross else [pltpu.VMEM(normed[0].shape[1:], BF), dma, dma((2,)), dma((2,))]),
        compiler_params=pltpu.CompilerParams(
            vmem_limit_bytes=VMEM_BYTES, collective_id=3 if cross else 4,
            has_side_effects=True,
        ),
        cost_estimate=pl.CostEstimate(
            flops=60 * 10**9, bytes_accessed=2**23, transcendentals=2**24
        ),
    )(offsets, q, k, v, do, att, lse, *sources, *normed)


def project_kernel(
    own, scale, tokens_ref, small_ref, head_ref, rows_ref, normed_ref, q_ref, k_ref, v_ref,
    small_all, head_all, rows_all, all_tokens, staged, token_send, token_recv, part_send, part_recv,
    own_sem, stage_sem, rows_send, rows_recv,
):
    me, zone = lax.axis_index("ctx"), lax.axis_index("fsdp")
    count, groups = lax.axis_size("ctx"), lax.axis_size("fsdp")
    chips = count // 2
    chain_start, chain_advance, chain_finish = chain_spread(
        rows_ref, rows_all, rows_send, rows_recv
    )
    keep_rows = pltpu.make_async_copy(rows_ref, rows_all.at[zone], own_sem.at[3])
    shard = small_ref.shape[1]
    sibling = {"ctx": flipped_bits(me, 1)}
    near = [flipped_bits(me, 2 * other) for other in range(1, chips)]
    greet([sibling] + [{"ctx": there} for there in near] + others("fsdp"))

    parts = []
    for shift in range(1, groups):
        there = {"fsdp": (zone + shift) % groups}
        for index, (source, target) in enumerate(((small_ref, small_all), (head_ref, head_all))):
            parts.append(
                remote(source, target.at[zone], part_send.at[index, shift - 1],
                       part_recv.at[index, shift - 1], there)
            )
    local = [
        pltpu.make_async_copy(small_ref, small_all.at[zone], own_sem.at[0]),
        pltpu.make_async_copy(head_ref, head_all.at[zone], own_sem.at[1]),
        pltpu.make_async_copy(tokens_ref, all_tokens.at[me], own_sem.at[2]),
    ]
    for copy in local:
        copy.start()
    for copy in parts:
        copy.start()

    start, land, rest, done = plane_gather(tokens_ref, all_tokens, token_send, token_recv)
    start()
    chain_start()
    keep_rows.start()
    for copy in local:
        copy.wait()
    for copy in parts:
        copy.wait_recv()

    def row(index):
        pieces = [small_all[z].astype(F32)[index : index + 1] for z in range(groups)]
        return jnp.concatenate(pieces, axis=1)

    gain, shift = row(0), row(3)
    mine = small_all[me // (shard // own)].astype(F32)
    q_shift = jnp.where(me % 2 == 0, mine[6:7, :own], mine[6:7, own : 2 * own])
    v_shift = jnp.where(me % 2 == 0, mine[7:8, :own], mine[7:8, own : 2 * own])
    if own < 128:
        for ref in (q_ref, k_ref, v_ref):
            ref[...] = jnp.zeros_like(ref)

    def save(block, place):
        return pltpu.make_async_copy(staged.at[place], normed_ref.at[block], stage_sem.at[place])

    order, ready = [], []
    for step in range(count):
        place = step % 2
        if step in (4, 6) and step // 2 <= groups - 1:
            chain_advance(step // 2 - 1)
        if step == 0:
            ready.append(me)
        elif step == 1:
            ready.append(rest(0))
        elif step == 2:
            for index in range(min(2, chips - 1)):
                ready.append(land(index))
        elif len(ready) == step:
            index = step - chips - 1
            if step == 4 and chips == 4:
                ready += [rest(1), rest(2)]
            elif step == 6 and chips == 4:
                ready.append(land(2))
            elif chips == 4:
                ready.append(rest(3))
            else:
                ready.append(land(step - 2) if step <= chips else rest(index + 1))
        block = ready[step]
        order.append(block)
        if step >= 2:
            save(order[step - 2], place).wait()
        unit, _ = normalize(all_tokens[block].astype(F32))
        staged[place] = (unit * gain + shift).astype(BF)
        save(block, place).start()
        total = jnp.zeros((staged.shape[1], 3 * own), F32)
        for z in range(groups):
            total = total + nn(staged[place, :, z * shard : z * shard + shard], head_all[z])
        q_ref[block, :, :own] = (scale * (total[:, :own] + q_shift)).astype(BF)
        k_ref[block, :, :own] = total[:, own : 2 * own].astype(BF)
        v_ref[block, :, :own] = (total[:, 2 * own :] + v_shift).astype(BF)
    for step in (count - 2, count - 1):
        save(order[step], step % 2).wait()
    for copy in parts:
        copy.wait_send()
    keep_rows.wait()
    for stage in range(3, groups - 1):
        chain_advance(stage)
    chain_finish()
    done()


def project(own, scale, tokens, small, head_in, rows_part):
    count, groups = lax.axis_size("ctx"), lax.axis_size("fsdp")
    rows, width = tokens.shape
    vmem = pl.BlockSpec(memory_space=pltpu.VMEM)
    hbm = pl.BlockSpec(memory_space=pl.ANY)
    dma = pltpu.SemaphoreType.DMA
    lanes = jax.ShapeDtypeStruct((count, rows, 128), BF)
    return pl.pallas_call(
        functools.partial(project_kernel, own, scale),
        out_shape=(
            jax.ShapeDtypeStruct((count, rows, width), BF),
            lanes, lanes, lanes,
            jax.ShapeDtypeStruct((groups,) + small.shape, BF),
            jax.ShapeDtypeStruct((groups,) + head_in.shape, BF),
            jax.ShapeDtypeStruct((groups,) + rows_part.shape, BF),
        ),
        in_specs=[hbm, hbm, hbm, hbm],
        out_specs=(hbm,) + (vmem,) * 5 + (hbm,),
        scratch_shapes=[
            pltpu.VMEM((count, rows, width), BF),
            pltpu.VMEM((2, rows, width), BF),
            dma((count + 1,)), dma((count + 1,)),
            dma((2, groups - 1)), dma((2, groups - 1)),
            dma((4,)), dma((2,)), dma((2 * groups,)), dma((2 * groups,)),
        ],
        compiler_params=pltpu.CompilerParams(
            vmem_limit_bytes=VMEM_BYTES, collective_id=5, has_side_effects=True
        ),
        cost_estimate=pl.CostEstimate(
            flops=50 * 10**9, bytes_accessed=2**25, transcendentals=0
        ),
    )(tokens, small, head_in, rows_part)


def ffn_kernel(
    steps, groups, n_ref, dy_ref, base_ref, bias_ref, win_ref, wout_ref, rows_ref,
    out_ref, gn_ref, gb_ref, in_ref, sum_ref, rows_all,
    n_t, own_in, own_out, post_in, post_out, got_in, got_out,
    keep_in, keep_out, flow_in, flow_out, near_in, near_out,
    send_sem, recv_sem, flow_send, flow_recv, save_sem, rows_send, rows_recv, rows_own,
):
    f = pl.program_id(0)
    spread = group_spread(rows_ref, rows_all, rows_send, rows_recv, 0)
    keep_rows = pltpu.make_async_copy(
        rows_ref, rows_all.at[lax.axis_index("fsdp")], rows_own
    )
    me = lax.axis_index("ctx")
    count = lax.axis_size("ctx")
    chips = count // 2
    core = me % 2
    low_bit = (me // 2) % 2
    high_bit = me // chips
    cols = keep_in.shape[2]
    slot = f % 2
    sibling = {"ctx": flipped_bits(me, 1)}
    low = {"ctx": flipped_bits(me, 2)}
    high = {"ctx": flipped_bits(me, chips)}

    def copies(step, place):
        return (
            remote(post_in.at[place], got_in.at[step], send_sem.at[0, place],
                   recv_sem.at[0, step], sibling),
            remote(post_out.at[place], got_out.at[step], send_sem.at[1, place],
                   recv_sem.at[1, step], sibling),
        )

    def flows(step, place):
        return (
            remote(flow_in.at[place], near_in.at[step], flow_send.at[0, place],
                   flow_recv.at[0, step], low),
            remote(flow_out.at[place], near_out.at[step], flow_send.at[1, place],
                   flow_recv.at[1, step], high),
        )

    @pl.when(f == 0)
    def _():
        greet([sibling, low, high] + others("fsdp"))
        for copy in spread:
            copy.start()
        keep_rows.start()
        n_t[...] = transposed(n_ref[...])
        gn_ref[...] = jnp.zeros_like(gn_ref)
        out_ref[...] = base_ref[...]

    @pl.when(f < steps)
    def _():
        @pl.when(f >= 2)
        def _():
            for copy in copies(jnp.maximum(f - 2, 0), slot):
                copy.wait_send()

        pre = nn(n_ref[...], win_ref[...]) + bias_ref[0, :1]
        below = 0.5 * (1.0 + lax.erf(pre * (1.0 / math.sqrt(2.0))))
        hidden = (pre * below).astype(BF)
        out_ref[...] += nn(hidden, wout_ref[...])
        slope = below + pre * (jnp.exp(-0.5 * pre * pre) * (1.0 / math.sqrt(2.0 * math.pi)))
        dy = dy_ref[...]
        grad_pre = (nt(dy, wout_ref[...]) * slope).astype(BF)
        gb_ref[0] = jnp.broadcast_to(
            jnp.sum(grad_pre.astype(F32), axis=0, keepdims=True), gb_ref.shape[1:]
        )
        gn_ref[...] += nt(grad_pre, win_ref[...])

        def split(part, keep, post, half):
            left, right = part[:, :half], part[:, half:]
            keep[slot] = jnp.where(core == 0, left, right)
            post[slot] = jnp.where(core == 0, right, left).astype(BF)

        first, second = copies(jnp.minimum(f, steps - 1), slot)
        split(nn(n_t[...], grad_pre), own_in, post_in, cols)
        first.start()
        split(tn(hidden, dy), own_out, post_out, 2 * cols)
        second.start()

    @pl.when(f > 0)
    def _():
        past = jnp.maximum(f - 1, 0)
        place = (f + 1) % 2
        for copy in copies(past, place):
            copy.wait_recv()

        @pl.when(f >= 3)
        def _():
            for copy in flows(jnp.maximum(f - 3, 0), place):
                copy.wait_send()

        unit = keep_in.shape[1] // (groups * (chips // 2))
        for slab in range(groups * (chips // 2)):
            for kept in (True, False):
                take = low_bit if kept else 1 - low_bit
                rows = pl.ds(pl.multiple_of((2 * slab + take) * unit, unit), unit)
                both = own_in[place, rows, :] + got_in[past, rows, :].astype(F32)
                at = slice(unit * slab, unit * slab + unit)
                if kept:
                    keep_in[past, at, :] = both.astype(BF)
                else:
                    flow_in[place, at, :] = both.astype(BF)
        unit = n_t.shape[0] // groups // 2
        for slab in range(own_out.shape[1] // (2 * unit)):
            for kept in (True, False):
                take = high_bit if kept else 1 - high_bit
                rows = pl.ds(pl.multiple_of((2 * slab + take) * unit, unit), unit)
                both = own_out[place, rows, :] + got_out[past, rows, :].astype(F32)
                at = slice(unit * slab, unit * slab + unit)
                for half in range(2):
                    value = both[:, half * cols : half * cols + cols].astype(BF)
                    if kept:
                        keep_out[past, half, at, :] = value
                    else:
                        flow_out[place, half, at, :] = value
        for copy in flows(past, place):
            copy.start()

    @pl.when(f == steps)
    def _():
        for back in (2, 1):
            for copy in copies(steps - back, (steps - back) % 2):
                copy.wait_send()
            for copy in flows(steps - back, (steps - back) % 2):
                copy.wait_send()
        per = steps // sum_ref.shape[0]
        height = keep_out.shape[2]

        def saves(step):
            rows = pl.ds(pl.multiple_of((step % per) * height, height), height)
            return (
                pltpu.make_async_copy(
                    keep_in.at[step], in_ref.at[step], save_sem.at[0, step]
                ),
                pltpu.make_async_copy(
                    keep_out.at[step], sum_ref.at[step // per, :, rows], save_sem.at[1, step]
                ),
            )

        def join(step, carry):
            for copy in flows(step, step % 2):
                copy.wait_recv()
            keep_in[step] = (
                keep_in[step].astype(F32) + near_in[step].astype(F32)
            ).astype(BF)
            keep_out[step] = (
                keep_out[step].astype(F32) + near_out[step].astype(F32)
            ).astype(BF)
            for copy in saves(step):
                copy.start()
            return carry

        def saved(step, carry):
            for copy in saves(step):
                copy.wait()
            return carry

        lax.fori_loop(0, steps, join, 0)
        lax.fori_loop(0, steps, saved, 0)
        keep_rows.wait()
        for copy in spread:
            copy.wait_send()
            copy.wait_recv()


def ffn(normed, dy, base, bias, weights, rows_part):
    rows, width = normed.shape
    hidden = weights.shape[1] // 2
    groups = lax.axis_size("fsdp")
    step = 512
    cols = step // 2
    steps = hidden // step
    per = width // step
    last = steps - 1

    def now(f):
        return jnp.minimum(f, last)

    whole = lambda f: (0, 0)
    hbm = pl.BlockSpec(memory_space=pl.ANY)
    dma = pltpu.SemaphoreType.DMA
    once = pl.BlockSpec((rows, width), whole, pipeline_mode=pl.Buffered(1))
    return pl.pallas_call(
        functools.partial(ffn_kernel, steps, groups),
        grid=(steps + 1,),
        out_shape=(
            jax.ShapeDtypeStruct((rows, width), F32),
            jax.ShapeDtypeStruct((rows, width), F32),
            jax.ShapeDtypeStruct((steps, 8, step), F32),
            jax.ShapeDtypeStruct((steps, width // 2, cols), BF),
            jax.ShapeDtypeStruct((hidden // width, 2, width // 2, cols), BF),
            jax.ShapeDtypeStruct((groups,) + rows_part.shape, BF),
        ),
        in_specs=[
            once, once, once,
            pl.BlockSpec((1, 8, step), lambda f: (now(f), 0, 0)),
            pl.BlockSpec((width, step), lambda f: (0, now(f))),
            pl.BlockSpec(
                (step, width), lambda f: (now(f) % per, hidden // width + now(f) // per)
            ),
            hbm,
        ],
        out_specs=(
            pl.BlockSpec((rows, width), whole),
            pl.BlockSpec((rows, width), whole),
            pl.BlockSpec((1, 8, step), lambda f: (now(f), 0, 0)),
            hbm, hbm, hbm,
        ),
        scratch_shapes=[
            pltpu.VMEM((width, rows), BF),
            pltpu.VMEM((2, width, cols), F32),
            pltpu.VMEM((2, step, 2 * cols), F32),
            pltpu.VMEM((2, width, cols), BF),
            pltpu.VMEM((2, step, 2 * cols), BF),
            pltpu.VMEM((steps, width, cols), BF),
            pltpu.VMEM((steps, step, 2 * cols), BF),
            pltpu.VMEM((steps, width // 2, cols), BF),
            pltpu.VMEM((steps, 2, step // 2, cols), BF),
            pltpu.VMEM((2, width // 2, cols), BF),
            pltpu.VMEM((2, 2, step // 2, cols), BF),
            pltpu.VMEM((steps, width // 2, cols), BF),
            pltpu.VMEM((steps, 2, step // 2, cols), BF),
            dma((2, 2)), dma((2, steps)), dma((2, 2)), dma((2, steps)), dma((2, steps)),
            dma((groups - 1,)), dma((groups - 1,)), dma,
        ],
        compiler_params=pltpu.CompilerParams(
            vmem_limit_bytes=60 * 2**20, collective_id=0, has_side_effects=True
        ),
        cost_estimate=pl.CostEstimate(
            flops=30 * 10**9, bytes_accessed=2**26, transcendentals=2**22
        ),
    )(normed, dy, base, bias, weights, weights, rows_part)


def branch_kernel(query, *refs):
    if query:
        moved_ref, query_ref, normed_ref, *refs = refs
    else:
        grad_ref, *refs = refs
    (
        values_ref, gain_ref, base_ref, mixed_ref, weight_ref,
        total_ref, do_ref, sums_ref, send_ref, keep_ref,
    ) = refs
    core = lax.axis_index("ctx") % 2

    def rows_of(ref):
        pieces = [ref[index] for index in range(ref.shape[0])]
        return pieces[0] if len(pieces) == 1 else jnp.concatenate(pieces, axis=1)

    def column_sum(row, value):
        sums_ref[row : row + 1, :] = jnp.sum(value, axis=0, keepdims=True)

    sums_ref[...] = jnp.zeros_like(sums_ref)
    products = []
    if query:
        cq = rows_of(moved_ref)
        grad = nt(cq, query_ref[...])
        column_sum(3, cq.astype(F32))
        products.append((normed_ref[...], cq))
    else:
        grad = grad_ref[...]
    unit, scale = normalize(values_ref[...])
    q = gain_ref[...] * grad
    back = scale * (
        q - jnp.mean(q, axis=-1, keepdims=True) - unit * jnp.mean(q * unit, axis=-1, keepdims=True)
    )
    column_sum(0, grad * unit)
    column_sum(1, grad)
    total = base_ref[...].astype(F32) + back
    total_ref[...] = total
    branch = total.astype(BF)
    column_sum(2, branch.astype(F32))
    do = nt(branch, weight_ref[...]).astype(BF)
    own = do_ref.shape[2]
    for index in range(do_ref.shape[0]):
        do_ref[index] = do[:, index * own : index * own + own]
    products.append((rows_of(mixed_ref), branch))
    half = keep_ref.shape[2]
    for index, (left, right) in enumerate(products):
        low, high = tn(left, right[:, :half]), tn(left, right[:, half:])
        keep_ref[index] = jnp.where(core == 0, low, high).astype(BF)
        send_ref[index] = jnp.where(core == 0, high, low).astype(BF)


def branch(grad, values, gain, base, mixed, weight, query=()):
    rows, width = values.shape
    number = 2 if query else 1
    vmem = pl.BlockSpec(memory_space=pltpu.VMEM)
    half = jax.ShapeDtypeStruct((number, width, width // 2), BF)
    operands = (grad, *query, values, gain, base, mixed, weight)
    return pl.pallas_call(
        functools.partial(branch_kernel, bool(query)),
        out_shape=(
            jax.ShapeDtypeStruct((rows, width), F32),
            jax.ShapeDtypeStruct(mixed.shape, BF),
            jax.ShapeDtypeStruct((8, width), F32),
            half, half,
        ),
        in_specs=[vmem] * len(operands),
        out_specs=(vmem,) * 5,
        compiler_params=pltpu.CompilerParams(vmem_limit_bytes=VMEM_BYTES),
        cost_estimate=pl.CostEstimate(
            flops=10**10, bytes_accessed=2**24, transcendentals=0
        ),
    )(*operands)


def finish_kernel(more, late_ref, done_ref, ffn_ref, *refs):
    if more:
        moved_ref, enc_ref, *late, refs = (*refs[:6], refs[6:])
    all_ffn, all_done, all_late, *refs = refs
    if more:
        token_ref, enc_grad_ref, *refs = refs
    late_own, got, send_sem, recv_sem, zone_send, zone_recv, own_sem, *refs = refs
    me, zone = lax.axis_index("ctx"), lax.axis_index("fsdp")
    count, groups = lax.axis_size("ctx"), lax.axis_size("fsdp")
    chips = count // 2
    greet(others("ctx") + others("fsdp"))
    zones = group_copies(late_ref, got, zone_send, zone_recv, 0)
    for copy in zones:
        copy.start()
    if more:
        all_moved, weights, all_enc, enc_send, enc_recv, enc_own, moved_sem, weight_sem = refs
        put, arrived, put_done = exchange(enc_ref, all_enc, enc_send, enc_recv, enc_own)
        for step in range(count):
            put((me + step) % count)
        fetch_moved = pltpu.make_async_copy(moved_ref, all_moved, moved_sem)
        fetch_moved.start()
    gathers = [
        plane_gather(source, store, send_sem.at[kind], recv_sem.at[kind])
        for kind, (source, store) in enumerate(
            ((ffn_ref, all_ffn), (done_ref, all_done), (late_own, all_late))
        )
    ]
    local = [
        pltpu.make_async_copy(source, store.at[me], own_sem.at[kind])
        for kind, (source, store) in enumerate(
            ((ffn_ref, all_ffn), (done_ref, all_done), (late_own, all_late))
        )
    ]
    for kind in range(2):
        gathers[kind][0]()
        local[kind].start()
    if more:
        width = token_ref.shape[1]

        def fetch(step):
            source = (me + step) % count
            out = []
            for k in range(5):
                columns = pl.ds(pl.multiple_of(k * width + source * 128, 128), 128)
                for index, array in enumerate(late):
                    side = me % 2 if index < 2 else 1 - me % 2
                    out.append(
                        pltpu.make_async_copy(
                            array.at[:, :, columns], weights.at[step % 2, k, :, side, index % 2],
                            weight_sem.at[step % 2, k, index],
                        )
                    )
            return out

        for copy in fetch(0):
            copy.start()
        token_ref[...] = jnp.zeros_like(token_ref)
        enc_grad_ref[...] = jnp.zeros_like(enc_grad_ref)
        fetch_moved.wait()

        def one_source(step, carry):
            source = (me + step) % count

            @pl.when(step + 1 < count)
            def _():
                for copy in fetch(step + 1):
                    copy.start()

            for copy in fetch(step):
                copy.wait()
            grads = all_moved[source]

            def part(index):
                return weights[step % 2, index].reshape(width, 128)

            token_ref[...] += (
                nt(grads[:, :128], part(0))
                + nt(grads[:, 128:256], part(1))
                + nt(grads[:, 256:], part(2))
            )
            arrived(source)
            rows = all_enc[source]
            enc_grad_ref[...] += nt(rows[:, :128], part(3)) + nt(rows[:, 128:], part(4))
            return carry

        lax.fori_loop(0, count, one_source, 0)
    total = late_ref[zone].astype(F32)
    for shift in range(groups - 1):
        zones[shift].wait_recv()
        total = total + got[shift].astype(F32)
    late_own[...] = total.astype(BF)
    gathers[2][0]()
    local[2].start()
    for index in range(chips - 1):
        for gather in gathers:
            gather[1](index)
    for index in range(chips):
        for gather in gathers:
            gather[2](index)
    for copy in local:
        copy.wait()
    for gather in gathers:
        gather[3]()
    for copy in zones:
        copy.wait_send()
    if more:
        put_done()


def finish(late, done, ffn_sums, width, more=()):
    count, groups = lax.axis_size("ctx"), lax.axis_size("fsdp")
    vmem = pl.BlockSpec(memory_space=pltpu.VMEM)
    hbm = pl.BlockSpec(memory_space=pl.ANY)
    dma = pltpu.SemaphoreType.DMA
    outs = [
        jax.ShapeDtypeStruct((count,) + shape, BF)
        for shape in (ffn_sums.shape, done.shape, late.shape[1:])
    ]
    places = [hbm] * 3
    scratch = [
        pltpu.VMEM(late.shape[1:], BF),
        pltpu.VMEM((groups - 1,) + late.shape[1:], BF),
        dma((3, count + 1)), dma((3, count + 1)),
        dma((groups - 1,)), dma((groups - 1,)), dma((3,)),
    ]
    if more:
        moved, enc, weights = more[:3]
        outs.append(jax.ShapeDtypeStruct((moved.shape[1], width), F32))
        outs.append(jax.ShapeDtypeStruct((enc.shape[1], width), F32))
        places += [vmem, vmem]
        scratch += [
            pltpu.VMEM(moved.shape, BF),
            pltpu.VMEM((2, 5, groups, 2, 2, weights.shape[1], 128), BF),
            pltpu.VMEM(enc.shape, BF),
            dma((count,)), dma((count,)), dma, dma, dma((2, 5, 4)),
        ]
    return pl.pallas_call(
        functools.partial(finish_kernel, bool(more)),
        out_shape=outs,
        in_specs=[vmem] + [hbm] * (2 + len(more)),
        out_specs=places,
        scratch_shapes=scratch,
        compiler_params=pltpu.CompilerParams(
            vmem_limit_bytes=VMEM_BYTES, collective_id=6, has_side_effects=True
        ),
        cost_estimate=pl.CostEstimate(
            flops=50 * 10**9, bytes_accessed=2**25, transcendentals=0
        ),
    )(late, done, ffn_sums, *more)


def place_kernel(groups, more, ffn_ref, self_refs, kv_refs, mixed_refs, out_refs, extra):
    in_ref, out_ref, self_ref, kv_ref, *weight_refs = out_refs
    cols = ffn_ref.shape[3]
    steps = ffn_ref.shape[1] // 2
    hidden = in_ref.shape[1]
    blocks = out_ref.shape[0]
    width = out_ref.shape[3]
    depth = width // groups
    per = steps // blocks
    span = min(depth, cols)
    for core in range(2):
        for f in range(steps):
            value = ffn_ref[core, f].astype(F32)
            for piece in range(cols // span):
                unit = (f % per) * 2 * cols + core * cols + piece * span
                at = (unit // depth * blocks + f // per) * depth + unit % depth
                in_ref[:, at : at + span] = value[:, piece * span : piece * span + span]
        for slab in range(steps):
            at = (core * 2 + slab % 2) * cols
            out_ref[slab // 2, 0, :, at : at + cols] = ffn_ref[core, steps + slab].astype(F32)
    for refs, target in ((self_refs, self_ref), (kv_refs, kv_ref)):
        for k, ref in enumerate(refs):
            own = ref.shape[2]
            for source in range(ref.shape[0]):
                at = k * width + source * own
                target[:, at : at + own] = ref[source].astype(F32)
    part = in_ref.shape[0]
    for (ref, count), targets in zip(mixed_refs, (weight_refs[:1], weight_refs[1:])):
        own = ref.shape[2]
        for w, target in enumerate(targets):
            for core in range(2):
                for index in range(count):
                    top = (w * count + index) * part
                    at = core * (width // 2) + index * own
                    target[:, at : at + own] = ref[core, top : top + part, :].astype(F32)
    if more:
        total_ref, tokens_ref, gain_ref, base_ref, enc_ref, token_ref, enc_out = extra
        unit, scale = normalize(tokens_ref[...].astype(F32))
        token_ref[...] = (
            base_ref[...] + normalize_back(unit, scale, gain_ref[...], total_ref[...])[0]
        )
        enc_out[...] = enc_ref[...]


def place(ffn_sums, done, late, hidden, width, more=()):
    count, groups = lax.axis_size("ctx"), lax.axis_size("fsdp")
    chips, own = count // 2, late.shape[2]
    depth = width // groups
    part = depth // chips
    blocks = hidden // width
    wide = width // 2 // own

    def lane_blocks(start, k):
        return pl.BlockSpec((count, part, own), lambda c: (0, (start + k * depth) // part + c, 0))

    in_specs = [pl.BlockSpec((2,) + ffn_sums.shape[1:], lambda c: (c, 0, 0, 0))]
    in_specs += [lane_blocks(2 * wide * part, k) for k in range(3)]
    in_specs += [lane_blocks(wide * part, k) for k in range(2)]
    in_specs += [
        pl.BlockSpec((2, wide * part, own), lambda c: (c, 0, 0)),
        pl.BlockSpec((2, 2 * wide * part, own), lambda c: (c, 0, 0)),
    ]
    row = lambda n: pl.BlockSpec((part, n), lambda c: (c, 0))
    out_specs = [
        row(hidden), pl.BlockSpec((blocks, 1, part, width), lambda c: (0, c, 0, 0)),
        row(3 * width), row(2 * width), row(width), row(width), row(width),
    ]
    out_shape = [
        jax.ShapeDtypeStruct((depth, hidden), F32),
        jax.ShapeDtypeStruct((blocks, chips, part, width), F32),
        jax.ShapeDtypeStruct((depth, 3 * width), F32),
        jax.ShapeDtypeStruct((depth, 2 * width), F32),
    ] + [jax.ShapeDtypeStruct((depth, width), F32)] * 3
    if more:
        total, _, _, _, enc = more
        tall, short = total.shape[0] // chips, enc.shape[0] // chips
        tokens_rows = pl.BlockSpec((tall, width), lambda c: (c, 0))
        enc_rows = pl.BlockSpec((short, width), lambda c: (c, 0))
        in_specs += [
            tokens_rows, tokens_rows, pl.BlockSpec((1, width), lambda c: (0, 0)), tokens_rows,
            enc_rows,
        ]
        out_specs += [tokens_rows, enc_rows]
        out_shape += [
            jax.ShapeDtypeStruct(total.shape, F32), jax.ShapeDtypeStruct(enc.shape, F32)
        ]

    def kernel(*refs):
        ffn_ref, refs = refs[0], refs[1:]
        self_refs, kv_refs, mixed, refs = refs[:3], refs[3:5], refs[5:7], refs[7:]
        extra_in, refs = refs[: len(more)], refs[len(more) :]
        place_kernel(
            groups, bool(more), ffn_ref, self_refs, kv_refs,
            ((mixed[0], wide), (mixed[1], wide)), refs[:7], extra_in + refs[7:],
        )

    return pl.pallas_call(
        kernel,
        grid=(chips,),
        out_shape=out_shape,
        in_specs=in_specs,
        out_specs=out_specs,
        compiler_params=pltpu.CompilerParams(vmem_limit_bytes=VMEM_BYTES),
        cost_estimate=pl.CostEstimate(flops=0, bytes_accessed=2**25, transcendentals=0),
    )(ffn_sums, late, late, late, done, done, done, late, *more)


def swap(value, bit):
    count = lax.axis_size("ctx")
    return lax.ppermute(value, "ctx", [(i, i ^ bit) for i in range(count)])


def pair_sum(send, keep):
    return (keep.astype(F32) + swap(send, 1).astype(F32)).astype(BF)


def gather_ffn(ffn_in, ffn_out):
    count = lax.axis_size("ctx")
    groups = lax.axis_size("fsdp")
    me = lax.axis_index("ctx")
    depth, hidden = ffn_in.shape
    width = ffn_out.shape[1]
    blocks = hidden // width
    rows = depth // count
    left = lax.dynamic_slice_in_dim(ffn_in, me * rows, rows, 0)
    left = left.reshape(rows, groups, blocks, depth)
    left = jnp.transpose(left, (0, 2, 1, 3)).reshape(rows, hidden)
    right = lax.dynamic_index_in_dim(
        ffn_out.reshape(blocks, count, rows, width), me, 1, keepdims=False
    )
    right = jnp.moveaxis(right, 0, 1).reshape(rows, hidden)
    joined = jnp.concatenate([left, right], axis=1)
    return lax.all_gather(joined, ("fsdp", "ctx"), axis=0, tiled=True)


def body(
    tokens, encoder_out, prompt_offsets, gains, shifts, self_in, self_out, cross_q, cross_kv,
    cross_out, ffn_in, ffn_bias, ffn_out, out_bias, cotangent,
):
    row_count, width = tokens.shape
    head_dim = width // HEADS
    scale = 1.0 / math.sqrt(head_dim)
    ctx = lax.axis_size("ctx")
    groups = lax.axis_size("fsdp")
    me = lax.axis_index("ctx")
    heads = HEADS // ctx
    own = heads * head_dim

    shard = gains.shape[1]
    small = jnp.concatenate(
        [gains, shifts, out_bias[None], ffn_bias.reshape(-1, shard)], axis=0
    )
    small_rows = small.shape[0]
    small = jnp.pad(small, ((0, 32 - small_rows), (0, 0)))

    head_in = lax.dynamic_index_in_dim(
        self_in.reshape(self_in.shape[0], 3, ctx, own), me, 2, keepdims=False
    ).reshape(-1, 3 * own)
    half_rows = self_in.shape[0] // 2
    core = me % 2

    def half_of(*weights):
        cut = [lax.dynamic_slice_in_dim(w, core * half_rows, half_rows, 0) for w in weights]
        return jnp.concatenate(cut, axis=1)

    all_normed, queries, keys, values, small, head_in, near_rows = project(
        own, scale, tokens, small, head_in, half_of(self_out, cross_q)
    )
    all_normed = all_normed.reshape(-1, width)
    queries, keys, values = [x.reshape(-1, 128) for x in (queries, keys, values)]
    small = small[:, :small_rows].astype(F32)
    vectors = jnp.moveaxis(small[:, :13], 0, 1).reshape(13, width)
    gain, shift, full_out_bias = vectors[:3], vectors[3:12], vectors[12]
    full_ffn_bias = small[:, 13:].reshape(-1)

    def lanes(value):
        gap = [(0, 0)] * (value.ndim - 1) + [(0, 128 - own)]
        return value if own == 128 else jnp.pad(value, gap)

    head_kv = lax.dynamic_index_in_dim(
        cross_kv.reshape(-1, 2, ctx, own), me, 2, keepdims=False
    ).reshape(-1, 2 * own)
    (queries, ffn_in, ffn_out) = lax.optimization_barrier((queries, ffn_in, ffn_out))
    ffn_weights = gather_ffn(ffn_in, ffn_out)
    mixed_heads, att_self, lse_self, near_other, all_encoder, head_kv = attend_forward(
        False, heads, prompt_offsets, queries, keys, values, (near_rows, encoder_out, head_kv),
    )

    def both_cores(mine, other):
        shape = (mine.shape[0], 2) + mine.shape[1:]
        full = lax.dynamic_update_index_in_dim(jnp.zeros(shape, BF), mine, core, 1)
        full = lax.dynamic_update_index_in_dim(full, other, 1 - core, 1)
        return full.reshape(width, -1)

    full_self_out = both_cores(near_rows[:, :, :width], near_other[:, :, :width])
    full_cross_q = both_cores(near_rows[:, :, width:], near_other[:, :, width:])
    all_encoder = all_encoder.reshape(-1, width)
    head_kv = head_kv.reshape(width, 2 * own)

    def to_rows(value):
        return jnp.moveaxis(value[:, :, :own], 0, 1).reshape(row_count, width)

    def to_heads(value):
        return lanes(jnp.moveaxis(value.reshape(row_count, ctx, own), 1, 0))

    mixed = to_rows(mixed_heads)
    token_values = tokens.astype(F32)
    first = token_values + nn(mixed, full_self_out) + shift[5]
    normed_two = (normalize(first)[0] * gain[1] + shift[1]).astype(BF)
    cross_queries = (scale * (nn(normed_two, full_cross_q) + shift[6])).astype(BF)
    enc_shift = lax.dynamic_slice_in_dim(shift[7], me * own, own, 0)
    enc_projected = nn(all_encoder, head_kv)
    enc_keys = lanes(enc_projected[:, :own].astype(BF))
    enc_values = lanes((enc_projected[:, own:] + enc_shift).astype(BF))
    cross_heads, att_cross, lse_cross, all_cross_q, far_rows, far_other = attend_forward(
        True, heads, prompt_offsets, to_heads(cross_queries), enc_keys, enc_values,
        (half_of(cross_out),),
    )
    full_cross_out = both_cores(far_rows, far_other)
    cross_mixed = to_rows(cross_heads)
    second = first + nn(cross_mixed, full_cross_out) + shift[8]
    normed_three = (normalize(second)[0] * gain[2] + shift[2]).astype(BF)
    depth = ffn_in.shape[0]
    blocks = ffn_in.shape[1] // width
    order = full_ffn_bias.reshape(groups, blocks, depth)
    order = jnp.moveaxis(order, 0, 1).reshape(-1, 1, 512)
    late_rows = half_of(self_in, cross_kv)
    quarter = half_rows // 2
    layer_sum, grad_three, bias_parts, in_sum, out_sum, late_first = ffn(
        normed_three, cotangent, second + full_out_bias,
        jnp.broadcast_to(order, (order.shape[0], 8, 512)), ffn_weights, late_rows[:quarter],
    )
    layer_out = layer_sum.astype(BF)
    chips = ctx // 2
    part = depth // chips
    in_sum = in_sum.reshape(-1, groups, chips // 2, part, 256)
    out_sum = out_sum.reshape(-1, groups, chips // 2, part, 256)

    dy = cotangent.astype(F32)
    chip_first = lambda value: jnp.moveaxis(value.reshape(groups, chips, part, -1), 1, 0)

    def stacked(value):
        return value if own == 128 else to_rows(value)[None]

    def tiles_of(value):
        return value if own == 128 else to_heads(value[0])

    grad_second, cross_do, sums_two, send, keep = branch(
        grad_three, second, gain[2:3], cotangent, stacked(cross_heads), full_cross_out
    )
    cross_part = chip_first(pair_sum(send, keep)[0])
    got_shape = (max(chips // 2 - 1, 1),) + in_sum.shape[:2] + in_sum.shape[3:]
    cross_moved, cross_dk, cross_dv, in_got, out_got, cross_got, late_second = attend_backward(
        True, heads, scale, prompt_offsets, all_cross_q.reshape(-1, 128), enc_keys, enc_values,
        tiles_of(cross_do), att_cross, lse_cross,
        (in_sum, out_sum, cross_part, late_rows[quarter:]),
        (got_shape, got_shape, (chips - 1,) + cross_part.shape[1:], late_first.shape),
    )

    def joined(value, mine, dim, got):
        kept = lax.dynamic_index_in_dim(value, mine, dim, keepdims=False).astype(F32)
        return kept + jnp.sum(got.astype(F32), axis=0)

    grad_first, self_do, sums_one, send, keep = branch(
        stacked(cross_moved), first, gain[1:2], grad_second, stacked(mixed_heads), full_self_out,
        (full_cross_q, normed_two),
    )
    middle = pair_sum(send, keep)
    middle = jnp.moveaxis(middle.reshape(2, groups, chips, part, -1), 2, 0)
    cross_part = joined(cross_part, me // 2, 0, cross_got).astype(BF)
    enc_heads = jnp.concatenate([cross_dk[:, :own], cross_dv[:, :own]], axis=1)
    kv_part = tn(all_encoder, enc_heads).astype(BF).reshape(groups, depth, 2 * own)
    ffn_sums = jnp.concatenate(
        [
            joined(in_sum, me // 4, 2, in_got),
            joined(out_sum, (me // 2) % (chips // 2), 2, out_got),
        ],
        axis=0,
    )
    ffn_sums = jnp.moveaxis(ffn_sums.astype(BF), 1, 0)
    carried = (middle, ffn_sums, cross_part, kv_part, late_first, late_second)
    moved, _, grad_head_in, column, *got = attend_backward(
        False, heads, scale, prompt_offsets, queries, keys, values, tiles_of(self_do),
        att_self, lse_self, carried,
        [(value.shape[0] - 1,) + value.shape[1:] for value in carried[:4]]
        + [value.shape for value in carried[4:]],
        (all_normed.reshape(ctx, row_count, width),),
    )
    grad_head_in = grad_head_in.reshape(width, 3, 128)[:, :, :own].reshape(width, 3 * own)
    column = column[0].reshape(3, 128)[:, :own].reshape(-1)
    zone = lax.axis_index("fsdp")
    middle = joined(middle, me // 2, 0, got[0]).astype(BF)
    ffn_sums, cross_part, kv_part = [
        joined(value, zone, 0, part_got).astype(BF)
        for value, part_got in zip(carried[1:4], got[1:4])
    ]
    other_first, other_second = got[4:]
    weight = head_in.reshape(width, 3 * own).astype(F32)
    grad_shift_one = jnp.sum(weight * column, axis=1)
    grad_gain_one = jnp.sum(weight * (grad_head_in - shift[0][:, None] * column), axis=1) / gain[0]

    def spread(value):
        return lax.dynamic_update_slice_in_dim(jnp.zeros((width,), F32), value, me * own, 0)

    totals = jnp.stack(
        [
            grad_gain_one, sums_one[0], sums_two[0],
            grad_shift_one, sums_one[1], sums_two[1],
            spread(column[:own]), spread(column[2 * own :]),
            sums_one[2],
            sums_one[3],
            spread(jnp.sum(enc_heads[:, own:].astype(F32), axis=0)),
            sums_two[2],
            jnp.sum(dy, axis=0),
        ]
    )
    totals = jnp.moveaxis(totals.reshape(13, groups, shard), 1, 0).reshape(groups, -1)
    bias = jnp.moveaxis(bias_parts[:, 0].reshape(blocks, groups, depth), 0, 1)
    totals = jnp.concatenate([totals, bias.reshape(groups, -1)], axis=1)
    count = totals.shape[1]
    totals = jnp.pad(totals, ((0, 0), (0, 48 * own - count))).reshape(groups, 48, own)

    def by_lanes(value, rows):
        lead = value.shape[:-2]
        value = jnp.moveaxis(value.reshape(lead + (rows, -1, own)), -2, -3)
        return value.reshape(lead + (-1, own))

    middle = jnp.moveaxis(by_lanes(middle, part), 1, 0).reshape(groups, -1, own)
    late = by_lanes(grad_head_in.reshape(groups, depth, 3 * own), depth)
    late = jnp.concatenate([middle, late.astype(BF), totals.astype(BF)], axis=1)
    done = jnp.concatenate([by_lanes(cross_part, part), by_lanes(kv_part, depth)], axis=0)
    enc_sum = enc_heads.reshape(ctx, -1, 2 * own)
    more = ()
    if own == 128:
        more = (moved, enc_sum, late_first, late_second, other_first, other_second)
    all_ffn, all_done, all_late, *more_sums = finish(late, done, ffn_sums, width, more)
    if more:
        more = (more_sums[0], tokens, gain[:1], grad_first, more_sums[1])
    (
        grad_ffn_in, grad_ffn_out, grad_self_in, grad_cross_kv, grad_cross_out, grad_cross_q,
        grad_self_out, *more_grads,
    ) = place(all_ffn, all_done, all_late, ffn_in.shape[1], width, more)
    grad_ffn_out = grad_ffn_out.reshape(-1, width)
    sums = jnp.sum(all_late[:, -48:].astype(F32), axis=0).reshape(-1)[:count]
    mine, grad_ffn_bias = sums[: 13 * shard].reshape(13, shard), sums[13 * shard :]
    if more:
        input_grad, grad_encoder = more_grads
    else:

        late_mine = jnp.concatenate([late_first, late_second], axis=1)
        late_other = jnp.concatenate([other_first, other_second], axis=1)
        late_weights = both_cores(late_mine, late_other)
        cut = moved.reshape(ctx, row_count, 3, 128)[:, :, :, :own]
        grads = jnp.transpose(cut, (1, 2, 0, 3)).reshape(row_count, 3 * width)
        unit_one, scale_one = normalize(token_values)
        grad_normed = nt(grads, late_weights[:, : 3 * width])
        input_grad = grad_first + normalize_back(unit_one, scale_one, gain[0], grad_normed)[0]
        enc_sum = lax.all_to_all(enc_sum, "ctx", split_axis=0, concat_axis=0, tiled=True)
        enc_sum = jnp.transpose(enc_sum.reshape(ctx, -1, 2, own), (1, 2, 0, 3))
        grad_encoder = nt(enc_sum.reshape(-1, 2 * width), late_weights[:, 3 * width :])
    return (
        layer_out, input_grad, grad_encoder, mine[:3], mine[3:12], grad_self_in, grad_self_out,
        grad_cross_q, grad_cross_kv, grad_cross_out, grad_ffn_in, grad_ffn_bias, grad_ffn_out, mine[12],
    )


def solution(mesh):
    rows = P(("fsdp", "ctx"), None)
    shard = P("fsdp", None)
    thin = P(None, "fsdp")
    flat = P("fsdp")
    return jax.shard_map(
        body,
        mesh=mesh,
        in_specs=(
            rows, rows, shard, thin, thin, shard, shard, shard, shard, shard, shard, flat, shard,
            flat, rows,
        ),
        out_specs=(
            rows, rows, rows, thin, thin, shard, shard, shard, shard, shard, shard, flat, shard,
            flat,
        ),
        check_vma=False,
    )
```
